32 devices in a mesh: expert: 8 (over z, x), shard: 4 (over y, core).
Axes of the slice: x: 2, y: 2, z: 4, core: 2. Of those that a mesh axis runs over, the one named last changes fastest.
Arguments:
- layer_input: bfloat16 [4096, 2048], P('expert'), may hold values from -6 to 6
- doc_ids: int32 [4096], P('expert'), may hold values from 0 to 3, as said below
- routes: int32 [4096, 8], P('expert'), may hold values from 0 to 15, all different within a row; in each aligned block of 512 rows (0 to 511, 512 to 1023, ...) at most 384 rows name the same one
- norm1_gain: float32 [2048], replicated, may hold values from 0.5 to 1.5
- query_weight: bfloat16 [2048, 4096], P(None, 'shard'), may hold values from -0.125 to 0.125
- key_matrix: bfloat16 [2048, 512], P(None, 'shard'), may hold values from -0.125 to 0.125
- value_matrix: bfloat16 [2048, 512], P(None, 'shard'), may hold values from -0.125 to 0.125
- query_norm_gain: float32 [128], replicated, may hold values from 0.5 to 1.5
- key_norm_gain: float32 [128], replicated, may hold values from 0.5 to 1.5
- out_weight: bfloat16 [4096, 2048], P('shard'), may hold values from -0.375 to 0.375
- norm2_gain: float32 [2048], replicated, may hold values from 0.5 to 1.5
- router_weight: bfloat16 [2048, 16], replicated, may hold values from -0.0625 to 0.0625
- gate_weight: bfloat16 [16, 2048, 768], P('expert', None, 'shard'), may hold values from -0.125 to 0.125
- up_weight: bfloat16 [16, 2048, 768], P('expert', None, 'shard'), may hold values from -0.125 to 0.125
- down_weight: bfloat16 [16, 768, 2048], P('expert', 'shard'), may hold values from -0.875 to 0.875
- cotangent: bfloat16 [4096, 2048], P('expert'), may hold values from -6 to 6
Outputs:
- layer_out: bfloat16 [4096, 2048], P('expert')
- input_grad: bfloat16 [4096, 2048], P('expert')
- norm1_gain_grad: float32 [2048], replicated
- query_weight_grad: float32 [2048, 4096], P(None, 'shard')
- key_weight_grad: float32 [2048, 512], P(None, 'shard')
- value_weight_grad: float32 [2048, 512], P(None, 'shard')
- query_gain_grad: float32 [128], replicated
- key_gain_grad: float32 [128], replicated
- out_weight_grad: float32 [4096, 2048], P('shard')
- norm2_gain_grad: float32 [2048], replicated
- router_weight_grad: float32 [2048, 16], replicated
- gate_weight_grad: float32 [16, 2048, 768], P('expert', None, 'shard')
- up_weight_grad: float32 [16, 2048, 768], P('expert', None, 'shard')
- down_weight_grad: float32 [16, 768, 2048], P('expert', 'shard')
The draws below stay inside these ranges and needn't reach their ends.
Inputs may be any that keep to these rules, and one draw needn't show every extreme that they name: `doc_ids`: along each device's 512 rows the numbers start at 0 and never fall; in every draw some device holds a single document of all 512 rows. `routes`: each row names 8 different experts. In each device's 512 rows no expert is named more than 384 times, a bound that some block reaches.
All inputs are finite; a program needn't handle non-finite values.
Results may differ from the reference program's by a relative error of at most 0.03.
Values may be sent and summed in bfloat16 or wider, within the bound.
A program may use at most 384 MiB of HBM per device.

```python
import math
import jax
import jax.numpy as jnp
import numpy as np
from jax import lax

MODEL_DIM = 2048
QUERY_HEADS = 32
KEY_VALUE_HEADS = 4
HEAD_DIM = 128
EFF = 768
TOPK = 8
TOKENS_PER_SHARD = 512
EXPERTS = 16
CAP = 384
TOKEN_TOTAL = 4096
N_EXPERT = 8


def draw_doc_ids(key, part):
    key = jax.random.fold_in(key, 11)
    cut_key, whole_key = jax.random.split(key)
    cuts = jnp.sort(jax.random.randint(cut_key, (N_EXPERT, 3), 1, TOKENS_PER_SHARD), axis=1)
    single = jax.random.randint(whole_key, (), 0, N_EXPERT)
    cuts = jnp.where((jnp.arange(N_EXPERT) == single)[:, None], TOKENS_PER_SHARD, cuts)
    row_index = jnp.arange(TOKENS_PER_SHARD)
    numbers = jnp.sum((row_index[None, :, None] >= cuts[:, None, :]).astype(jnp.int32), axis=2)
    return numbers.reshape(-1).astype(jnp.int32)


def levels(own_key, shape, pieces, low, top_value):
    gain = 1.0
    for dim, shards_of in pieces:
        steps = jax.random.uniform(jax.random.fold_in(jax.random.fold_in(own_key, 6), dim), (shards_of,), jnp.float32, low / len(pieces), top_value / len(pieces))
        gain = gain * jnp.repeat(jnp.exp(steps), shape[dim] // shards_of).reshape((-1,) + (1,) * (len(shape) - 1 - dim))
    return gain


def deal_out(rng, own, number, rows, number_of, top, bound, slope):
    ranking = jax.random.permutation(rng, number_of)
    packed, ordinary = portions_of(number_of, rows * top, bound, slope, True), portions_of(number_of, rows * top, bound, slope, False)
    places = jnp.arange(number_of)

    def named(sizes, offset_by):
        used = int((sizes > 0).sum())
        fixed = max(1, used // 4)
        shifted = fixed + (places - fixed + offset_by * (used - fixed)) % max(1, number_of - fixed)
        return jnp.zeros((number_of,), jnp.int32).at[ranking[jnp.where(places < fixed, places, shifted)]].set(jnp.asarray(sizes, jnp.int32))

    sizes = jnp.where(number % 4 == 0, named(packed, number // 4), named(ordinary, number - number // 4 - 1))
    mixed = jax.random.permutation(jax.random.fold_in(own, 3), number_of)
    donor, receiver = mixed[0:number_of // 2 * 2:2], mixed[1:number_of // 2 * 2:2]
    slack = jnp.minimum(sizes[donor] - 1, bound - sizes[receiver]) // 2
    slack = jnp.where((donor == ranking[0]) | (receiver == ranking[0]) | (sizes[receiver] == 0), 0, jnp.maximum(slack, 0))
    shifted = jax.random.randint(jax.random.fold_in(own, 4), (number_of // 2,), 0, 1 << 20) % (slack + 1)
    sizes = sizes.at[donor].add(-shifted).at[receiver].add(shifted)
    members = jnp.searchsorted(jnp.cumsum(sizes), jnp.arange(rows * top), side="right").astype(jnp.int32)
    grid = members.reshape(top, rows).T
    grid = grid[jax.random.permutation(jax.random.fold_in(own, 1), rows)]
    offset_by = jax.random.randint(jax.random.fold_in(own, 2), (rows, 1), 0, top)
    return jnp.take_along_axis(grid, (jnp.arange(top)[None, :] + offset_by) % top, axis=1)


def portions_of(number_of, total, most, lean, full):
    portions = [(1 << 20) // math.isqrt(grade ** lean) + 1 for grade in range(1, number_of + 1)]
    largest = most if full else min(most, max(-(-total // number_of), total * portions[0] // sum(portions)))
    least = 1 if total - largest >= number_of - 1 else 0
    holding, spare = [largest] + [least] * (number_of - 1), total - largest - least * (number_of - 1)
    while spare > 0:
        free = [i for i in range(1, number_of) if holding[i] < largest] or [i for i in range(1, number_of) if holding[i] < most]
        pool, left = sum([portions[i] for i in free]), spare
        for i in free:
            addition = min(most - holding[i], max(1, left * portions[i] // pool), spare)
            holding[i] = holding[i] + addition
            spare = spare - addition
    return np.array(holding)


def bell_draw(key, extent, width, limit, cuts=(), held_as=jnp.bfloat16):
    level = levels(key, extent, cuts, -0.22, 0.18) if cuts else 1.0
    entries = jax.random.normal(key, extent, jnp.float32) * width * level
    return jnp.minimum(jnp.maximum(entries, -limit), limit).astype(held_as)


def setup_inputs(seed: int = 0) -> dict:
    arg_keys = jax.random.split(jax.random.key(seed), 17)
    layer_input = bell_draw(arg_keys[0], (TOKEN_TOTAL, MODEL_DIM), 1.0, 6.0, ((0, 8),))
    doc_ids = draw_doc_ids(jax.random.fold_in(arg_keys[16], 71), 0)
    routes_keys = jax.random.split(jax.random.fold_in(arg_keys[2], 1), TOKEN_TOTAL // TOKENS_PER_SHARD)
    routes_turns = jax.random.permutation(jax.random.fold_in(arg_keys[2], 3), TOKEN_TOTAL // TOKENS_PER_SHARD)
    routes = jax.vmap(lambda own, number: deal_out(jax.random.fold_in(arg_keys[2], 2), own, number, TOKENS_PER_SHARD, EXPERTS, TOPK, CAP, 1))(routes_keys, routes_turns).reshape((TOKEN_TOTAL, TOPK))
    norm1_gain = jnp.clip(1.0 + 0.1 * jax.random.normal(arg_keys[3], (MODEL_DIM,), jnp.float32), 0.5, 1.5)
    query_weight = bell_draw(arg_keys[4], (MODEL_DIM, QUERY_HEADS * HEAD_DIM), MODEL_DIM ** -0.5, 0.125, ((1, 4),))
    key_matrix = bell_draw(arg_keys[5], (MODEL_DIM, KEY_VALUE_HEADS * HEAD_DIM), MODEL_DIM ** -0.5, 0.125, ((1, 4),))
    value_matrix = bell_draw(arg_keys[6], (MODEL_DIM, KEY_VALUE_HEADS * HEAD_DIM), MODEL_DIM ** -0.5, 0.125, ((1, 4),))
    query_norm_gain = jnp.clip(1.0 + 0.1 * jax.random.normal(arg_keys[7], (HEAD_DIM,), jnp.float32), 0.5, 1.5)
    key_norm_gain = jnp.clip(1.0 + 0.1 * jax.random.normal(arg_keys[8], (HEAD_DIM,), jnp.float32), 0.5, 1.5)
    out_weight = bell_draw(arg_keys[9], (QUERY_HEADS * HEAD_DIM, MODEL_DIM), (QUERY_HEADS * HEAD_DIM // 16) ** -0.5, 0.375, ((0, 4),))
    norm2_gain = jnp.clip(1.0 + 0.1 * jax.random.normal(arg_keys[10], (MODEL_DIM,), jnp.float32), 0.5, 1.5)
    router_weight = bell_draw(arg_keys[11], (MODEL_DIM, EXPERTS), (4 * MODEL_DIM) ** -0.5, 0.0625)
    gate_weight = bell_draw(arg_keys[12], (EXPERTS, MODEL_DIM, EFF), MODEL_DIM ** -0.5, 0.125, ((0, 8), (2, 4)))
    up_weight = bell_draw(arg_keys[13], (EXPERTS, MODEL_DIM, EFF), MODEL_DIM ** -0.5, 0.125, ((0, 8), (2, 4)))
    down_weight = bell_draw(arg_keys[14], (EXPERTS, EFF, MODEL_DIM), (EFF // 16) ** -0.5, 0.875, ((0, 8), (1, 4)))
    cotangent = bell_draw(arg_keys[15], (TOKEN_TOTAL, MODEL_DIM), 1.0, 6.0, ((0, 8),))
    return dict(layer_input=layer_input, doc_ids=doc_ids, routes=routes, norm1_gain=norm1_gain, query_weight=query_weight, key_matrix=key_matrix, value_matrix=value_matrix, query_norm_gain=query_norm_gain, key_norm_gain=key_norm_gain, out_weight=out_weight, norm2_gain=norm2_gain, router_weight=router_weight, gate_weight=gate_weight, up_weight=up_weight, down_weight=down_weight, cotangent=cotangent)


PRECISION_HIGH = lax.Precision.HIGHEST
EPS = 1e-06
THETA = 1000000.0

@jax.custom_vjp
def to_lower_precision(v):
    return lax.optimization_barrier(v.astype(jnp.bfloat16)).astype(jnp.float32)

@jax.custom_vjp
def lower_precision_back(v):
    return v

def low_keep(v):
    return (to_lower_precision(v), None)

def low_pass(kept, grad):
    return (grad,)

def back_keep(v):
    return (v, None)

def back_low(kept, grad):
    return (to_lower_precision(grad),)
to_lower_precision.defvjp(low_keep, low_pass)
lower_precision_back.defvjp(back_keep, back_low)

def root_mean_norm_forward(vector, scale_gain):
    inverse = lax.rsqrt(lax.optimization_barrier(jnp.mean(vector * vector, axis=-1, keepdims=True)) + EPS)
    return vector * inverse * scale_gain

def rope_tables(positions, head_size):
    half_size = head_size // 2
    frequency = THETA ** (-2.0 * jnp.arange(half_size, dtype=jnp.float32) / head_size)
    angles = positions.astype(jnp.float32)[:, None] * frequency[None, :]
    return (jnp.cos(angles), jnp.sin(angles))

def apply_rotary(vector, cosine_table, sine_values):
    half_size = vector.shape[-1] // 2
    first_half = vector[..., :half_size]
    second_half = vector[..., half_size:]
    cos_rows = cosine_table[:, None, :]
    sin_rows = sine_values[:, None, :]
    return jnp.concatenate([first_half * cos_rows - second_half * sin_rows, second_half * cos_rows + first_half * sin_rows], axis=-1)

def doc_positions(doc_ids):
    row_index = jnp.arange(doc_ids.shape[0], dtype=jnp.int32)
    doc_starts = jnp.concatenate([jnp.ones((1,), jnp.bool_), doc_ids[1:] != doc_ids[:-1]])
    first_row = lax.cummax(jnp.where(doc_starts, row_index, 0), axis=0)
    return (row_index - first_row).astype(jnp.int32)

def expert_places(routes):
    route_hot = (routes[:, :, None] == jnp.arange(EXPERTS, dtype=jnp.int32)[None, None, :]).astype(jnp.int32)
    hit_count = lax.optimization_barrier(jnp.sum(route_hot, axis=1)).reshape(N_EXPERT, TOKENS_PER_SHARD, EXPERTS)
    before = (jnp.cumsum(hit_count, axis=1) - hit_count).reshape(TOKEN_TOTAL, EXPERTS)
    slot_index = lax.optimization_barrier(jnp.sum(route_hot * before[:, None, :], axis=-1))
    source = (jnp.arange(TOKEN_TOTAL, dtype=jnp.int32) // TOKENS_PER_SHARD)[:, None]
    return (routes * (N_EXPERT * CAP) + source * CAP + slot_index).reshape(-1).astype(jnp.int32)

def attend_block(block_in):
    queries, keys, values, docs = block_in
    row_index = jnp.arange(docs.shape[0], dtype=jnp.int32)
    allowed = (docs[:, None] == docs[None, :]) & (row_index[:, None] >= row_index[None, :])
    scores = lower_precision_back(jnp.einsum('tkgd,skd->kgts', queries, keys, precision=PRECISION_HIGH) * HEAD_DIM ** (-0.5))
    scores = jnp.where(allowed, scores, -1e+30)
    attn_probs = to_lower_precision(jax.nn.softmax(scores, axis=-1))
    return jnp.einsum('kgts,skd->tkgd', attn_probs, values, precision=PRECISION_HIGH)

def expert_block(block_in):
    token_rows, gate_mat, up_mat, down_mat = block_in
    gate_pre = lower_precision_back(jnp.dot(token_rows, gate_mat, precision=PRECISION_HIGH))
    up_pre = lower_precision_back(jnp.dot(token_rows, up_mat, precision=PRECISION_HIGH))
    activated = to_lower_precision(jax.nn.silu(gate_pre) * up_pre)
    return jnp.dot(activated, down_mat, precision=PRECISION_HIGH)

def layer(inputs, weights, doc_blocks, cosine_table, sine_values, routes, places):
    norm1_gain, query_weight, key_matrix, value_matrix, query_norm_gain, key_norm_gain, out_weight, norm2_gain, router_weight, gate_weight, up_weight, down_weight = weights
    first_normed_input = to_lower_precision(root_mean_norm_forward(inputs, norm1_gain))
    query_linear = lower_precision_back(jnp.dot(first_normed_input, query_weight, precision=PRECISION_HIGH)).reshape(TOKEN_TOTAL, QUERY_HEADS, HEAD_DIM)
    key_linear = lower_precision_back(jnp.dot(first_normed_input, key_matrix, precision=PRECISION_HIGH)).reshape(TOKEN_TOTAL, KEY_VALUE_HEADS, HEAD_DIM)
    value_token_rows = to_lower_precision(lower_precision_back(jnp.dot(first_normed_input, value_matrix, precision=PRECISION_HIGH))).reshape(N_EXPERT, TOKENS_PER_SHARD, KEY_VALUE_HEADS, HEAD_DIM)
    query_rotated = to_lower_precision(apply_rotary(root_mean_norm_forward(query_linear, query_norm_gain), cosine_table, sine_values)).reshape(N_EXPERT, TOKENS_PER_SHARD, KEY_VALUE_HEADS, QUERY_HEADS // KEY_VALUE_HEADS, HEAD_DIM)
    key_rotated = to_lower_precision(apply_rotary(root_mean_norm_forward(key_linear, key_norm_gain), cosine_table, sine_values)).reshape(N_EXPERT, TOKENS_PER_SHARD, KEY_VALUE_HEADS, HEAD_DIM)
    mixture = lax.map(jax.checkpoint(attend_block), (query_rotated, key_rotated, value_token_rows, doc_blocks))
    mixed = to_lower_precision(lower_precision_back(mixture.reshape(TOKEN_TOTAL, QUERY_HEADS * HEAD_DIM)))
    residual = inputs + lower_precision_back(jnp.dot(mixed, out_weight, precision=PRECISION_HIGH))
    normed_two = to_lower_precision(root_mean_norm_forward(residual, norm2_gain))
    logits = lower_precision_back(jnp.dot(normed_two, router_weight, precision=PRECISION_HIGH))
    gate_probs = jax.nn.softmax(jnp.take_along_axis(logits, routes, axis=1), axis=-1)
    token_rows = jnp.broadcast_to(normed_two[:, None, :], (TOKEN_TOTAL, TOPK, MODEL_DIM)).reshape(TOKEN_TOTAL * TOPK, MODEL_DIM)
    table = jnp.zeros((EXPERTS * N_EXPERT * CAP, MODEL_DIM), jnp.float32).at[places].set(token_rows)
    table = lower_precision_back(table).reshape(EXPERTS, N_EXPERT * CAP, MODEL_DIM)
    expert_rows = lax.map(jax.checkpoint(expert_block), (table, gate_weight, up_weight, down_weight))
    expert_rows = lower_precision_back(to_lower_precision(expert_rows)).reshape(EXPERTS * N_EXPERT * CAP, MODEL_DIM)
    chosen = expert_rows[places].reshape(TOKEN_TOTAL, TOPK, MODEL_DIM)
    return residual + lax.optimization_barrier(jnp.sum(gate_probs[:, :, None] * chosen, axis=1))

def reference(layer_input, doc_ids, routes, norm1_gain, query_weight, key_matrix, value_matrix, query_norm_gain, key_norm_gain, out_weight, norm2_gain, router_weight, gate_weight, up_weight, down_weight, cotangent):
    doc_blocks = doc_ids.reshape(N_EXPERT, TOKENS_PER_SHARD)
    positions = jax.vmap(doc_positions)(doc_blocks).reshape(-1)
    cosine_table, sine_values = rope_tables(positions, HEAD_DIM)
    places = expert_places(routes)
    weights = tuple((w_item.astype(jnp.float32) for w_item in (norm1_gain, query_weight, key_matrix, value_matrix, query_norm_gain, key_norm_gain, out_weight, norm2_gain, router_weight, gate_weight, up_weight, down_weight)))

    def forward(inputs, *params):
        return layer(inputs, params, doc_blocks, cosine_table, sine_values, routes, places)
    result, pullback = jax.vjp(forward, layer_input.astype(jnp.float32), *weights)
    gradients = pullback(cotangent.astype(jnp.float32))
    return (result.astype(jnp.bfloat16), gradients[0].astype(jnp.bfloat16), gradients[1], gradients[2], gradients[3], gradients[4], gradients[5], gradients[6], gradients[7], gradients[8], gradients[9], gradients[10], gradients[11], gradients[12])
```

```python
import jax
import jax.numpy as jnp
from jax import lax
from jax.experimental import pallas as pl
from jax.experimental.pallas import tpu as pltpu
from jax.sharding import PartitionSpec as P

EPS = 1e-06
THETA = 1000000.0
BF = jnp.bfloat16
F32 = jnp.float32
MESH = pl.DeviceIdType.MESH
VMEM_ROWS = 1024


def dot(a, b):
    return jnp.dot(a, b, preferred_element_type=F32)


def dot_nt(a, b):
    return lax.dot_general(a, b, (((1,), (1,)), ((), ())), preferred_element_type=F32)


def dot_tn(a, b):
    return lax.dot_general(a, b, (((0,), (0,)), ((), ())), preferred_element_type=F32)


LINK_BYTES_PER_US = 1e5


def grid_of(axis):
    size = lax.axis_size(axis)
    lines = 4 if axis == "expert" else 2
    return axis, lines, size // lines, size // lines


def line_of(grid):
    return grid[0], grid[1], 1, grid[3]


def cross_of(grid):
    return grid[0], 1, grid[2], grid[3]


def position(grid):
    axis, lines, width, stride = grid
    me = lax.axis_index(axis)
    return me, me // stride if lines > 1 else 0, me % width if width > 1 else 0


def at_each_line(grid, act):
    _, z, _ = position(grid)
    for at in range(grid[1]):

        @pl.when(z == at)
        def _():
            act(at)


def greet(grids):
    barrier = pltpu.get_barrier_semaphore()
    count = 0
    for grid in grids:
        axis, lines, width, stride = grid
        me, z, b = position(grid)

        def signal(peer):
            pl.semaphore_signal(barrier, inc=1, device_id={axis: peer}, device_id_type=MESH)

        @pl.when(z < lines - 1)
        def _():
            signal(me + stride)

        @pl.when(z > 0)
        def _():
            signal(me - stride)

        for o in range(1, width):
            signal(me - b + (b + o) % width)
        count = count + width - 1
        count = count + (z < lines - 1).astype(jnp.int32) + (z > 0).astype(jnp.int32)
    pl.semaphore_wait(barrier, count)


def slice_of(ref, start, rows):
    if not isinstance(start, int):
        start = pl.multiple_of(start, rows)
    return ref.at[pl.ds(start, rows)]


class Gather:
    def __init__(self, grid, source, out, pieces, sems):
        self.axis, self.lines, self.width, self.stride = grid
        self.source, self.out, self.pieces = source, out, pieces
        self.rows_all = source.shape[0]
        self.rows = self.rows_all // pieces
        self.send_r, self.send_l, self.send_x, self.recv = sems
        self.me, _, self.b = position(grid)
        self.bytes = self.rows * source.shape[1] * jnp.dtype(source.dtype).itemsize

    @staticmethod
    def sems(grid, pieces):
        _, lines, width, _ = grid
        dma = pltpu.SemaphoreType.DMA
        return [
            dma((lines, pieces)),
            dma((lines, pieces)),
            dma((max(1, width - 1), lines, pieces)),
            dma((lines * width, pieces)),
        ]

    def copy(self, slot, p, sem, peer, own=False):
        place = slice_of(self.out, slot * self.rows_all + p * self.rows, self.rows)
        source = slice_of(self.source, p * self.rows, self.rows) if own else place
        return pltpu.make_async_remote_copy(
            src_ref=source,
            dst_ref=place,
            send_sem=sem,
            recv_sem=self.recv.at[slot, p],
            device_id={self.axis: peer},
            device_id_type=MESH,
        )

    def sends(self, z, origin, p):
        slot = origin * self.width + self.b
        own = origin == z
        copies = []
        if origin <= z and z < self.lines - 1:
            sem = self.send_r.at[z - origin, p]
            copies.append(self.copy(slot, p, sem, self.me + self.stride, own))
        if origin >= z and z > 0:
            sem = self.send_l.at[origin - z, p]
            copies.append(self.copy(slot, p, sem, self.me - self.stride, own))
        for o in range(1, self.width):
            peer = self.me - self.b + (self.b + o) % self.width
            copies.append(self.copy(slot, p, self.send_x.at[o - 1, origin, p], peer, own))
        return copies

    def start(self, z, p):
        for c in self.sends(z, z, p):
            c.start()

    def arrived(self, slot, p):
        self.copy(slot, p, self.send_r.at[0, p], self.me).wait_recv()

    def forward(self, z, origin, p):
        self.arrived(origin * self.width + self.b, p)
        for c in self.sends(z, origin, p):
            c.start()

    def arrived_across(self, z, p):
        for o in range(1, self.width):
            self.arrived(z * self.width + (self.b + o) % self.width, p)

    def wait_sends(self, z):
        for p in range(self.pieces):
            for origin in range(self.lines):
                for c in self.sends(z, origin, p):
                    c.wait_send()

    def finish(self, z):
        for p in range(self.pieces):
            for line in range(self.lines):
                self.arrived_across(line, p)
        self.wait_sends(z)

    def own_slot(self, z):
        return slice_of(self.out, (z * self.width + self.b) * self.rows_all, self.rows_all)


class Scatter:
    def __init__(self, grid, parts, buffers, pieces, sems):
        self.axis, self.lines, self.width, self.stride = grid
        self.parts, self.pieces = parts, pieces
        self.cross, self.right, self.left = buffers
        self.rows_all = parts.shape[0] // (self.lines * self.width)
        self.rows = self.rows_all // pieces
        self.cross_send, self.cross_recv, self.r_send, self.r_recv, self.l_send, self.l_recv = sems
        self.me, _, self.b = position(grid)
        self.bytes = self.rows * parts.shape[1] * jnp.dtype(parts.dtype).itemsize

    @staticmethod
    def sems(grid, pieces):
        _, lines, width, _ = grid
        dma = pltpu.SemaphoreType.DMA
        across = (max(1, width - 1), lines, pieces)
        return [dma(across), dma(across)] + [dma((lines, pieces)) for _ in range(4)]

    @staticmethod
    def buffers(grid, rows_all, columns, kind):
        _, lines, width, _ = grid
        line = pltpu.VMEM((lines * rows_all if lines > 1 else 16, columns), kind)
        return [pltpu.VMEM((max(1, width - 1) * lines * rows_all, columns), kind), line, line]

    def start_of(self, slot, p):
        return slot * self.rows_all + p * self.rows

    def cross_copy(self, o, k, p):
        peer = (self.b + o) % self.width
        return pltpu.make_async_remote_copy(
            src_ref=slice_of(self.parts, self.start_of(k * self.width + peer, p), self.rows),
            dst_ref=slice_of(self.cross, self.start_of((o - 1) * self.lines + k, p), self.rows),
            send_sem=self.cross_send.at[o - 1, k, p],
            recv_sem=self.cross_recv.at[o - 1, k, p],
            device_id={self.axis: self.me - self.b + peer},
            device_id_type=MESH,
        )

    def line_copy(self, k, p, rightward):
        into = self.right if rightward else self.left
        at = self.start_of(k, p)
        return pltpu.make_async_remote_copy(
            src_ref=slice_of(self.cross, at, self.rows),
            dst_ref=slice_of(into, at, self.rows),
            send_sem=(self.r_send if rightward else self.l_send).at[k, p],
            recv_sem=(self.r_recv if rightward else self.l_recv).at[k, p],
            device_id={self.axis: self.me + self.stride if rightward else self.me - self.stride},
            device_id_type=MESH,
        )

    def start_one(self, k, p):
        for o in range(1, self.width):
            self.cross_copy(o, k, p).start()

    def add(self, k, p, sources, target):
        block = min(16, self.rows)
        own = self.start_of(k * self.width + self.b, p)

        @pl.loop(0, self.rows // block)
        def _(i):
            def rows_at(start):
                return pl.ds(pl.multiple_of(start + i * block, block), block)

            total = self.parts[rows_at(own), :].astype(F32)
            for o in range(self.width - 1):
                at = rows_at(self.start_of(o * self.lines + k, p))
                total = total + self.cross[at, :].astype(F32)
            for source in sources:
                total = total + source[rows_at(self.start_of(k, p)), :].astype(F32)
            target(rows_at(p * self.rows), total)

    def sources(self, z, k, p):
        found = []
        if k >= z and z > 0:
            self.line_copy(k, p, True).wait_recv()
            found.append(self.right)
        if k <= z and z < self.lines - 1:
            self.line_copy(k, p, False).wait_recv()
            found.append(self.left)
        return found

    def reduce_one(self, z, k, p):
        for o in range(1, self.width):
            self.cross_copy(o, k, p).wait_recv()

        def put(at, total):
            offset = pl.multiple_of(at.start + k * self.rows_all, at.size)
            self.cross[pl.ds(offset, at.size), :] = total.astype(self.cross.dtype)

        self.add(k, p, self.sources(z, k, p), put)
        self.line_copy(k, p, k > z).start()

    def total(self, z, p, target):
        for o in range(1, self.width):
            self.cross_copy(o, z, p).wait_recv()
        self.add(z, p, self.sources(z, z, p), target)

    def finish(self, z):
        for p in range(self.pieces):
            for k in range(self.lines):
                for o in range(1, self.width):
                    self.cross_copy(o, k, p).wait_send()
                if k != z:
                    self.line_copy(k, p, k > z).wait_send()


def targets(lines, z):
    others = sorted((k for k in range(lines) if k != z), key=lambda k: (-abs(k - z), -k))
    return others + [z]


class Plan:
    def __init__(self, lines):
        self.lines = lines
        self.steps = [[] for _ in range(lines)]
        self.jobs = 0

    def job(self):
        self.jobs += 1
        return self.jobs

    def add(self, z, waits, act, sends, begin=0.0):
        self.steps[z].append((begin, waits, act, sends))

    def order(self):
        arrived = [dict() for _ in range(self.lines)]
        free = {}
        clock = [0.0] * self.lines
        left = [list(enumerate(steps)) for steps in self.steps]
        result = [[] for _ in range(self.lines)]
        while any(left):
            best = None
            for z in range(self.lines):
                for i, (begin, waits, act, sends) in left[z]:
                    if all(key in arrived[z] for key in waits):
                        ready = max([begin] + [arrived[z][key] for key in waits])
                        if best is None or (max(ready, clock[z]), ready, z, i) < best[0]:
                            best = ((max(ready, clock[z]), ready, z, i), act, sends)
            (now, _, z, i), act, sends = best
            left[z] = [entry for entry in left[z] if entry[0] != i]
            result[z].append((now, act))
            clock[z] = now + 0.7
            for link, time, to, key in sends:
                start = max(now + 1.0, free.get((z, link), 0.0))
                free[z, link] = start + time
                arrived[to][key] = start + time + 1.0
        return result

    def run(self, grid, result, begin, end):
        def act(z):
            for now, step in result[z]:
                if begin <= now < end:
                    step()

        at_each_line(grid, act)


    def run_step(self, grid, result, index, begin, each, steps, early=False):
        _, z, _ = position(grid)
        for at in range(self.lines):
            for now, step in result[at]:
                due = int((now - begin) // each)
                if early:
                    due = max(0, due)
                if 0 <= due < steps:

                    @pl.when(jnp.logical_and(z == at, index == due))
                    def _():
                        step()


def plan_scatter(plan, scatter, p, put, then=None, begin=0.0, start=True):
    n = plan.job()
    lines, width = scatter.lines, scatter.width
    time = 2 * scatter.bytes / LINK_BYTES_PER_US
    for z in range(lines):
        ready = begin if isinstance(begin, (int, float)) else None
        for i, k in enumerate(targets(lines, z)):
            first = ready if ready is not None else begin[i]
            if width > 1:
                plan.add(
                    z,
                    [],
                    (lambda k=k: scatter.start_one(k, p)) if start else (lambda: None),
                    [("x", time * (width - 1), z, (n, "c", k))],
                    first,
                )
            waits = [(n, "c", k)] if width > 1 else []
            if k >= z and z > 0:
                waits.append((n, "r", k))
            if k <= z and z < lines - 1:
                waits.append((n, "l", k))
            if k > z:
                sends = [("r", time, z + 1, (n, "r", k))]
            elif k < z:
                sends = [("l", time, z - 1, (n, "l", k))]
            else:
                follow, sends = then(z) if then else ((lambda: None), [])

                def last(z=z, follow=follow):
                    scatter.total(z, p, put)
                    follow()

                plan.add(z, waits, last, sends, first)
                continue
            plan.add(z, waits, lambda z=z, k=k: scatter.reduce_one(z, k, p), sends, first)


def gather_sends(gather, n, time, z, origin):
    sends = []
    if origin <= z and z < gather.lines - 1:
        sends.append(("r", time, z + 1, (n, "g", origin)))
    if origin >= z and z > 0:
        sends.append(("l", time, z - 1, (n, "g", origin)))
    if gather.width > 1:
        sends.append(("x", time * (gather.width - 1), z, (n, "gx", origin)))
    return sends


def plan_gather(plan, gather, p, begin=None):
    n = plan.job()
    time = 2 * gather.bytes / LINK_BYTES_PER_US
    for z in range(gather.lines):
        for origin in range(gather.lines):
            if origin != z:
                plan.add(
                    z,
                    [(n, "g", origin)],
                    lambda z=z, origin=origin: gather.forward(z, origin, p),
                    gather_sends(gather, n, time, z, origin),
                )

    def then(z):
        return (lambda: gather.start(z, p)), gather_sends(gather, n, time, z, z)

    if begin is not None:
        for z in range(gather.lines):
            act, sends = then(z)
            plan.add(z, [], act, sends, begin)
    return then


class Reduce:
    def __init__(self, grid, parts, out, scratch, pieces, line_first):
        self.grid, self.parts, self.out = grid, parts, out
        self.line_first = line_first
        self.pieces = pieces
        take = Taker(scratch)
        self.sums = take.one()
        if line_first:
            self.pair_sums, self.pair_all = take.take(2)
            self.first = Scatter(line_of(grid), parts, take.take(3), 1, take.take(6))
            self.second = Scatter(cross_of(grid), self.pair_sums, take.take(3), 1, take.take(6))
            self.third = Gather(cross_of(grid), self.sums, self.pair_all, 1, take.take(4))
            self.fourth = Gather(line_of(grid), self.pair_all, out, 1, take.take(4))
        else:
            self.scatter = Scatter(grid, parts, take.take(3), pieces, take.take(6))
            self.gather = Gather(grid, self.sums, out, pieces, take.take(4))
        self.own_sem = take.one()

    @staticmethod
    def scratch(grid, rows, columns, kind, pieces, line_first):
        _, lines, width, _ = grid
        count = rows // (lines * width)
        shapes = [pltpu.VMEM((count, columns), kind)]
        if line_first:
            line, cross = line_of(grid), cross_of(grid)
            shapes += [pltpu.VMEM((width * count, columns), kind)] * 2
            shapes += Scatter.buffers(line, width * count, columns, kind) + Scatter.sems(line, 1)
            shapes += Scatter.buffers(cross, count, columns, kind) + Scatter.sems(cross, 1)
            shapes += Gather.sems(cross, 1) + Gather.sems(line, 1)
        else:
            shapes += Scatter.buffers(grid, count, columns, kind) + Scatter.sems(grid, pieces)
            shapes += Gather.sems(grid, pieces)
        return shapes + [pltpu.SemaphoreType.DMA]

    @staticmethod
    def refs(line_first):
        return 1 + (2 + 9 + 9 + 8 if line_first else 9 + 4) + 1

    def put(self, at, total):
        self.sums[at, :] = total.astype(self.sums.dtype)

    def put_pair(self, at, total):
        self.pair_sums[at, :] = total.astype(self.pair_sums.dtype)

    def own_copy(self, z):
        if self.line_first:
            return pltpu.make_async_copy(self.pair_all, self.fourth.own_slot(z), self.own_sem)
        return pltpu.make_async_copy(self.sums, self.gather.own_slot(z), self.own_sem)

    def start_one(self, k, p):
        if not self.line_first:
            self.scatter.start_one(k, p)

    def plan(self, plan, begin=0.0, start=True):
        if not self.line_first:
            for p in range(self.pieces):
                then = plan_gather(plan, self.gather, p)
                plan_scatter(plan, self.scatter, p, self.put, then, begin, start)
            return
        n = plan.job()
        time = 2 * self.second.bytes / LINK_BYTES_PER_US * (self.grid[2] - 1)
        along = plan_gather(plan, self.fourth, 0)

        def cross(z):
            return (lambda: self.second.start_one(0, 0)), [("x", time, z, (n, "c"))]

        plan_scatter(plan, self.first, 0, self.put_pair, cross, begin)
        for z in range(self.grid[1]):

            def across(z=z):
                self.second.total(0, 0, self.put)
                self.third.start(0, 0)
                at = pl.multiple_of(self.third.b * self.third.rows_all, self.third.rows_all)
                self.pair_all[pl.ds(at, self.third.rows_all), :] = self.sums[...]

            plan.add(z, [(n, "c")], across, [("x", time, z, (n, "x"))])
            follow, sends = along(z)

            def spread(follow=follow):
                self.third.arrived_across(0, 0)
                follow()

            plan.add(z, [(n, "x")], spread, sends)

    def finish(self, z):
        self.own_copy(z).start()
        if self.line_first:
            self.first.finish(z)
            self.second.finish(0)
            self.third.wait_sends(0)
            self.fourth.finish(z)
        else:
            self.scatter.finish(z)
            self.gather.finish(z)
        self.own_copy(z).wait()


def hbm():
    return pl.BlockSpec(memory_space=pl.ANY)


def vmem():
    return pl.BlockSpec(memory_space=pltpu.VMEM)


def params(number, mib=56):
    return pltpu.CompilerParams(
        collective_id=number, has_side_effects=True, vmem_limit_bytes=mib * 1024 * 1024
    )


class Taker:
    def __init__(self, refs):
        self.refs = list(refs)

    def take(self, count):
        taken = self.refs[:count]
        del self.refs[:count]
        return taken

    def one(self):
        return self.take(1)[0]


ALWAYS = (0.0, 1e9)


def gather_rows(arrays, side_arrays, number, pieces):
    grid, side = grid_of("expert"), grid_of("shard")
    values = list(arrays) + list(side_arrays)
    grids = [grid] * len(arrays) + [side] * len(side_arrays)
    n = len(values)

    def kernel(*refs):
        take = Taker(refs)
        ins, outs, own_sems = take.take(n), take.take(n), take.one()
        jobs = [Gather(grids[i], ins[i], outs[i], pieces[i], take.take(4)) for i in range(n)]

        def own(i, z):
            return pltpu.make_async_copy(ins[i], jobs[i].own_slot(z), own_sems.at[i])

        def each(i, act):
            at_each_line(grids[i], act)

        for i in range(n):
            each(i, lambda z, i=i: own(i, z).start())
        greet([grid] + ([side] if side_arrays else []))
        plan = Plan(grid[1])
        for i in range(len(arrays)):
            for p in range(pieces[i]):
                plan_gather(plan, jobs[i], p, 0.0)
        order = plan.order()
        plan.run(grid, order, 0.0, 1.0)
        late = 0.0 if not side_arrays else 1.0
        for i in range(len(arrays), n):
            for p in range(pieces[i]):
                each(i, lambda z, i=i, p=p: jobs[i].start(z, p))
        if side_arrays:
            edge = 2 * jobs[-1].bytes / LINK_BYTES_PER_US + 4.0
            begin = late
            for p in range(pieces[-1]):
                plan.run(grid, order, begin, edge * (p + 1))
                begin = edge * (p + 1)
                for i in range(len(arrays), n):

                    def forward(z, i=i, p=p):
                        for origin in range(grids[i][1]):
                            if origin != z:
                                jobs[i].forward(z, origin, p)

                    each(i, forward)
            plan.run(grid, order, begin, 1e9)
        else:
            plan.run(grid, order, 1.0, 1e9)
        for i in range(n):
            each(i, lambda z, i=i: jobs[i].finish(z))
            each(i, lambda z, i=i: own(i, z).wait())

    scratch = [pltpu.SemaphoreType.DMA((n,))]
    for g, p in zip(grids, pieces):
        scratch += Gather.sems(g, p)
    return pl.pallas_call(
        kernel,
        out_shape=[
            jax.ShapeDtypeStruct((g[1] * g[2] * a.shape[0], a.shape[1]), a.dtype)
            for a, g in zip(values, grids)
        ],
        in_specs=[hbm()] * n,
        out_specs=[hbm()] * n,
        scratch_shapes=scratch,
        compiler_params=params(number),
        name="gather_rows",
    )(*values)


def scatter_rows(parts, axis, number, pieces):
    grid = grid_of(axis)
    columns = parts.shape[1]
    count = parts.shape[0] // (grid[1] * grid[2])

    def kernel(parts_ref, out_ref, cross, right, left, *sems):
        greet([grid])
        job = Scatter(grid, parts_ref, (cross, right, left), pieces, sems)

        def put(at, total):
            out_ref[at, :] = total

        plan = Plan(grid[1])
        for p in range(pieces):
            plan_scatter(plan, job, p, put)
        plan.run(grid, plan.order(), *ALWAYS)
        at_each_line(grid, job.finish)

    return pl.pallas_call(
        kernel,
        out_shape=jax.ShapeDtypeStruct((count, columns), F32),
        in_specs=[vmem()],
        out_specs=vmem(),
        scratch_shapes=Scatter.buffers(grid, count, columns, parts.dtype)
        + Scatter.sems(grid, pieces),
        compiler_params=params(number),
        name="scatter_" + axis,
    )(parts)


def sum_and_gather(across_first, line_first, small, rows, spread, number):
    grid, side = grid_of("expert"), grid_of("shard")
    size = grid[1] * grid[2]
    shards = side[1] * side[2]
    values = [across_first, line_first, small]
    moved = [small] + list(rows)
    m = len(moved)
    kinds = [(2, False), (1, True), (1, False)]

    def kernel(*refs):
        take = Taker(refs)
        first_ref, second_ref, spread_ref = take.take(3)
        side_ins = take.take(m)
        outs, rows_outs, spread_out = take.take(3), take.take(m - 1), take.one()
        small_all, small_parts, own_sems = take.take(3)
        ins = [first_ref, second_ref, small_parts]
        jobs = [
            Reduce(grid, ins[i], outs[i], take.take(Reduce.refs(kinds[i][1])), *kinds[i])
            for i in range(3)
        ]
        spread_job = Scatter(side, spread_ref, take.take(3), 1, take.take(6))
        side_outs = [small_all] + rows_outs
        side_jobs = [Gather(side, side_ins[i], side_outs[i], 1, take.take(4)) for i in range(m)]

        def own(z, i):
            return pltpu.make_async_copy(side_ins[i], side_jobs[i].own_slot(z), own_sems.at[i])

        def begin_side(z):
            for i in range(m):
                own(z, i).start()

        at_each_line(side, begin_side)
        greet([grid, side])
        edges = [0.0, 6.0, 16.0, 28.0, 55.0]
        plan = Plan(grid[1])
        jobs[1].plan(plan)
        jobs[0].plan(plan)
        jobs[2].plan(plan, edges[3])
        order = plan.order()
        plan.run(grid, order, 0.0, edges[1])
        at_each_line(side, lambda z: side_jobs[0].start(z, 0))
        plan.run(grid, order, edges[1], edges[2])

        def forward(z, chosen):
            for origin in range(side[1]):
                if origin != z:
                    for job in chosen:
                        job.forward(z, origin, 0)

        def start(z):
            forward(z, side_jobs[:1])
            for job in side_jobs[1:]:
                job.start(z, 0)
            for k in targets(side[1], z):
                spread_job.start_one(k, 0)

        at_each_line(side, start)
        plan.run(grid, order, edges[2], edges[3])

        def end_small(z):
            side_jobs[0].finish(z)
            own(z, 0).wait()

        at_each_line(side, end_small)
        count = small.shape[0]
        total = small_all[pl.ds(0, count), :]
        for s in range(1, shards):
            total = total + small_all[pl.ds(s * count, count), :]
        small_parts[...] = total
        plan.run(grid, order, edges[3], edges[4])

        def spread_on(z):
            for k in targets(side[1], z)[:-1]:
                spread_job.reduce_one(z, k, 0)
            forward(z, side_jobs[1:])

        at_each_line(side, spread_on)
        plan.run(grid, order, edges[4], 1e9)

        def end(z):
            for job in jobs:
                job.finish(z)

        at_each_line(grid, end)

        def put_spread(at, total):
            spread_out[at, :] = total

        def end_rows(z):
            spread_job.total(z, 0, put_spread)
            spread_job.finish(z)
            for i in range(1, m):
                side_jobs[i].finish(z)
                own(z, i).wait()

        at_each_line(side, end_rows)

    scratch = [
        pltpu.VMEM((shards * small.shape[0], small.shape[1]), small.dtype),
        pltpu.VMEM(small.shape, small.dtype),
        pltpu.SemaphoreType.DMA((m,)),
    ]
    for a, kind in zip(values, kinds):
        scratch += Reduce.scratch(grid, a.shape[0], a.shape[1], a.dtype, *kind)
    spread_rows = spread.shape[0] // shards
    scratch += Scatter.buffers(side, spread_rows, spread.shape[1], BF) + Scatter.sems(side, 1)
    for _ in range(m):
        scratch += Gather.sems(side, 1)
    out = pl.pallas_call(
        kernel,
        out_shape=[jax.ShapeDtypeStruct(a.shape, a.dtype) for a in values]
        + [jax.ShapeDtypeStruct((shards * a.shape[0], a.shape[1]), a.dtype) for a in rows]
        + [jax.ShapeDtypeStruct((spread_rows, spread.shape[1]), F32)],
        in_specs=[vmem()] * 3 + [hbm()] * m,
        out_specs=[hbm()] * (2 + m) + [vmem()],
        scratch_shapes=scratch,
        compiler_params=params(number),
        name="sum_and_gather",
    )(across_first, line_first, spread, small, *rows)
    return out[:3], out[3:-1], out[-1]


CHUNK_US = 4.0
PAIR_US = 1.5
HEAD_US = 5.5
TILE_US = 1.5
EXTRA = 128


def share_of(columns):
    return 4 * columns // 5 // 256 * 256


def expert_rows(normed, cot, gates, weights_rel, own, number):
    grid, side = grid_of("expert"), grid_of("shard")
    _, lines, width, _ = grid
    size = lines * width
    shards = side[1] * side[2]
    experts, hidden, columns = weights_rel[0].shape
    full = shards * hidden
    both = 2 * full
    total_rows = normed.shape[0]
    count = total_rows // size
    pair = width * count
    tile = 256
    half = 512
    wide = 2 * hidden
    extra = EXTRA
    orders = [targets(lines, z) for z in range(lines)]
    out_tiles = columns // tile
    grad_tiles = experts * 3 * full // wide
    out_us, grad_us = 1.3, 2.3

    def kernel(*refs):
        take = Taker(refs)
        normed_hbm, cot_hbm, gates_ref = take.take(3)
        gate_hbm, up_hbm, down_hbm = take.take(shards), take.take(shards), take.take(shards)
        residual_hbm, own_gates, router, norm_gain = take.take(4)
        d_residual, d_logits, norm_gain_grad, d_attn = take.take(4)
        out_hbm = take.one()
        grad_hbm = take.take(3)
        normed_v, cot_v, weights, down = take.take(4)
        grads_low, act_low, parts = take.take(3)
        buffers = take.take(3)
        out_stage, grad_stage, d_gates_ref = take.take(3)
        sum_ref, residual, d_low = take.take(3)
        load_sems, weight_sems, out_sems, grad_sems = take.take(4)
        rows_job = Gather(side, d_low, d_attn, 2, take.take(4))
        job = Scatter(grid, parts, buffers, 1, take.take(6))
        me, z, _ = position(grid)

        def put(at, total):
            sum_ref[at, :] = total

        plan = Plan(lines)
        plan_scatter(
            plan, job, 0, put, None, [(i + 1) * CHUNK_US for i in range(lines)], False
        )
        order = plan.order()
        shard = lax.axis_index("shard")
        near = shard + 1 - 2 * (shard % 2)
        places = [shard, near, (shard + 2) % shards, (near + 2) % shards]

        loads = [
            pltpu.make_async_copy(normed_hbm, normed_v, load_sems.at[0]),
            pltpu.make_async_copy(cot_hbm, cot_v, load_sems.at[1]),
        ]
        residual_load = pltpu.make_async_copy(residual_hbm, residual, load_sems.at[2])
        weight_loads = [[] for _ in range(experts)]
        for j in range(experts):
            for r in range(shards):
                for w, (source, target) in enumerate(
                    (
                        (gate_hbm[r].at[j], weights.at[pl.ds(j * both + r * hidden, hidden)]),
                        (up_hbm[r].at[j], weights.at[pl.ds(j * both + full + r * hidden, hidden)]),
                        (down_hbm[r].at[j], down.at[pl.ds(j * full + r * hidden, hidden)]),
                    )
                ):
                    weight_loads[j].append(
                        pltpu.make_async_copy(source, target, weight_sems.at[j, r, w])
                    )
        for c in loads + weight_loads[0]:
            c.start()
        for j in range(1, experts):
            for c in weight_loads[j]:
                c.start()
        residual_load.start()
        greet([grid, side])
        for c in loads:
            c.wait()

        for j in range(experts):
            for c in weight_loads[j]:
                c.wait()

            @pl.loop(0, total_rows // half)
            def _(m):
                rows = pl.ds(pl.multiple_of(m * half, half), half)

                @pl.loop(0, full // tile)
                def _(t):
                    at = t * tile

                    def lines_of(base):
                        return pl.ds(pl.multiple_of(base + at, tile), tile)

                    x = normed_v[rows, :]
                    gate_pre = dot_nt(x, weights[lines_of(j * both), :])
                    up_pre = dot_nt(x, weights[lines_of(j * both + full), :])
                    back = dot_nt(cot_v[rows, :], down[lines_of(j * full), :])
                    probs = gates_ref[rows, j : j + 1]
                    sig = 0.5 + 0.5 * jnp.tanh(0.5 * gate_pre)
                    silu = gate_pre * sig
                    act = silu * up_pre
                    act_low[rows, lines_of(j * full)] = (act * probs).astype(BF)
                    d_act = back * probs
                    d_gate = d_act * up_pre * (sig * (1.0 + gate_pre * (1.0 - sig)))
                    grads_low[rows, lines_of(j * both)] = d_gate.astype(BF)
                    grads_low[rows, lines_of(j * both + full)] = (d_act * silu).astype(BF)
                    part = jnp.sum(act * back, axis=1, keepdims=True)

                    @pl.when(t == 0)
                    def _():
                        d_gates_ref[rows, j : j + 1] = part

                    @pl.when(t > 0)
                    def _():
                        d_gates_ref[rows, j : j + 1] = d_gates_ref[rows, j : j + 1] + part

        lane = lax.broadcasted_iota(jnp.int32, (count, extra), 1)

        @pl.loop(0, size)
        def _(e):
            rows = pl.ds(pl.multiple_of(e * count, count), count)
            block = jnp.zeros((count, extra), F32)
            for j in range(experts):
                value = d_gates_ref[rows, j : j + 1]
                high = value.astype(BF).astype(F32)
                mine = me * experts + j
                block = jnp.where(lane == mine, high, block)
                block = jnp.where(lane == mine + size * experts, value - high, block)
            parts[rows, columns:] = block.astype(BF)

        @pl.loop(0, lines)
        def _(i):
            k = jnp.int32(0)
            for at in range(lines):
                for step in range(lines):
                    k = jnp.where(jnp.logical_and(z == at, i == step), orders[at][step], k)
            rows = pl.ds(pl.multiple_of(k * pair, pair), pair)

            @pl.loop(0, columns // tile)
            def _(t):
                cols = pl.ds(pl.multiple_of(t * tile, tile), tile)
                value = dot(grads_low[rows, :], weights[:, cols])
                parts[rows, cols] = value.astype(BF)

            job.start_one(k, 0)

        begin = lines * CHUNK_US

        def out_copy(t, slot):
            cols = pl.ds(pl.multiple_of(t * tile, tile), tile)
            return pltpu.make_async_copy(
                out_stage.at[slot], out_hbm.at[:, cols], out_sems.at[slot]
            )

        plan.run(grid, order, -1.0, begin)

        @pl.loop(0, out_tiles)
        def _(t):
            slot = t % 2

            @pl.when(t >= 2)
            def _():
                out_copy(t - 2, slot).wait()

            cols = pl.ds(pl.multiple_of(t * tile, tile), tile)
            out_stage[slot, :, :] = dot(act_low[...], down[:, cols]).astype(BF)
            out_copy(t, slot).start()
            plan.run_step(grid, order, t, begin, out_us, out_tiles)

        begin = begin + out_tiles * out_us

        def grad_copies(kind, j, r, slot):
            copies = []
            for h in range(2):
                place = places[h]
                for step in range(1, shards // 2):
                    place = jnp.where(r == step, places[2 * step + h], place)
                copies.append(
                    pltpu.make_async_copy(
                        grad_stage.at[slot, pl.ds(h * hidden, hidden)],
                        grad_hbm[kind].at[place, j],
                        grad_sems.at[slot, h],
                    )
                )
            return copies

        per = full // wide

        def norm_backward():
            ext = sum_ref[:, columns:]
            d_gates = ext + pltpu.roll(ext, extra - size * experts, 1)
            probs = own_gates[...]
            inner = jnp.sum(probs * d_gates, axis=-1, keepdims=True)
            low = (probs * (d_gates - inner)).astype(BF)
            d_logits[...] = low
            for q in range(columns // half):
                cols = pl.ds(q * half, half)
                sum_ref[:, cols] = sum_ref[:, cols] + dot_nt(low, router[cols, :])
            norm_gain_grad[...] = jnp.zeros_like(norm_gain_grad)
            residual_load.wait()

            @pl.loop(0, count // 16)
            def _(i):
                rows = pl.ds(pl.multiple_of(i * 16, 16), 16)
                grad = sum_ref[rows, :columns]
                value = residual[rows, :]
                inverse = lax.rsqrt(jnp.mean(value * value, axis=-1, keepdims=True) + EPS)
                norm_gain_grad[0:1, :] = norm_gain_grad[0:1, :] + jnp.sum(
                    grad * value * inverse, axis=0, keepdims=True
                )
                back = rms_backward(value, inverse, norm_gain[...], grad)
                back = back + cot_v[pl.ds(pl.multiple_of(me * count + i * 16, 16), 16), :].astype(F32)
                d_residual[rows, :] = back
                d_low[rows, :] = back.astype(BF)

            def start(z):
                for p in range(2):
                    rows_job.start(z, p)

            at_each_line(side, start)

        def rows_forward(z):
            for p in range(2):
                for origin in range(side[1]):
                    if origin != z:
                        rows_job.forward(z, origin, p)

        def rows_end(z):
            own_rows = pltpu.make_async_copy(d_low, rows_job.own_slot(z), load_sems.at[3])
            own_rows.start()
            rows_job.finish(z)
            own_rows.wait()

        for kind in range(3):
            if kind == 2:
                plan.run(grid, order, begin, 1e9)
                norm_backward()

            @pl.loop(0, experts * per)
            def _(i):
                j, r = i // per, i % per
                slot = i % 2
                if kind == 2:
                    low, base, rows_v = act_low, j * full, cot_v
                else:
                    low, base, rows_v = grads_low, j * both + kind * full, normed_v
                lanes = pl.ds(pl.multiple_of(base + r * wide, wide), wide)

                @pl.when(i >= 2)
                def _():
                    for c in grad_copies(kind, (i - 2) // per, (i - 2) % per, slot):
                        c.wait()

                for q in range(2):
                    cols = pl.ds(q * columns // 2, columns // 2)
                    value = dot_tn(low[:, lanes], rows_v[:, cols])
                    grad_stage[slot, :, cols] = value.astype(BF)
                for c in grad_copies(kind, j, r, slot):
                    c.start()
                if kind < 2:
                    plan.run_step(grid, order, i, begin, grad_us, experts * per)

            for i in range(max(0, experts * per - 2), experts * per):
                for c in grad_copies(kind, i // per, i % per, i % 2):
                    c.wait()
            begin = begin + experts * per * grad_us

        at_each_line(side, rows_forward)
        for t in range(max(0, out_tiles - 2), out_tiles):
            out_copy(t, t % 2).wait()
        at_each_line(side, rows_end)
        at_each_line(grid, job.finish)

    dma = pltpu.SemaphoreType.DMA
    weight_shape = jax.ShapeDtypeStruct((shards, experts, hidden, columns), BF)
    return pl.pallas_call(
        kernel,
        out_shape=[
            jax.ShapeDtypeStruct((count, columns), F32),
            jax.ShapeDtypeStruct((count, extra), BF),
            jax.ShapeDtypeStruct((8, columns), F32),
            jax.ShapeDtypeStruct((shards * count, columns), BF),
            jax.ShapeDtypeStruct((total_rows, columns), BF),
            weight_shape,
            weight_shape,
            weight_shape,
        ],
        in_specs=[hbm()] * 2 + [vmem()] + [hbm()] * (3 * shards) + [hbm()] + [vmem()] * 3,
        out_specs=[vmem()] * 3 + [hbm()] * 5,
        scratch_shapes=[
            pltpu.VMEM((total_rows, columns), BF),
            pltpu.VMEM((total_rows, columns), BF),
            pltpu.VMEM((experts * both, columns), BF),
            pltpu.VMEM((experts * full, columns), BF),
            pltpu.VMEM((total_rows, experts * both), BF),
            pltpu.VMEM((total_rows, experts * full), BF),
            pltpu.VMEM((total_rows, columns + extra), BF),
        ]
        + Scatter.buffers(grid, count, columns + extra, BF)
        + [
            pltpu.VMEM((2, total_rows, tile), BF),
            pltpu.VMEM((2, wide, columns), BF),
            pltpu.VMEM((total_rows, experts), F32),
            pltpu.VMEM((count, columns + extra), F32),
            pltpu.VMEM((count, columns), F32),
            pltpu.VMEM((count, columns), BF),
            dma((4,)),
            dma((experts, shards, 3)),
            dma((2,)),
            dma((2, 2)),
        ]
        + Gather.sems(side, 2)
        + Scatter.sems(grid, 1),
        compiler_params=params(number, 63),
        name="expert_rows",
    )(normed, cot, gates, *weights_rel, *own)


def rms_forward(vector, gain):
    inverse = lax.rsqrt(jnp.mean(vector * vector, axis=-1, keepdims=True) + EPS)
    return vector * inverse * gain, inverse


def rms_backward(vector, inverse, gain, grad):
    scaled = grad * gain
    inner = jnp.mean(scaled * vector, axis=-1, keepdims=True)
    return inverse * scaled - vector * (inverse * inverse * inverse * inner)


def attention_backward(arrays, heads, number):
    grid, side = grid_of("expert"), grid_of("shard")
    _, lines, width, _ = grid
    size = lines * width
    shards = side[1] * side[2]
    names = list(arrays)
    tokens, columns = arrays["d_attn"].shape
    own_rows = tokens // shards
    inner = arrays["mixed"].shape[1]
    head = inner // heads
    count = inner // size
    pair = width * count
    tile = 256
    scale = head ** (-0.5)
    block = min(256, tokens)
    orders = [targets(lines, z) for z in range(lines)]
    split = [share_of(columns), columns - share_of(columns)]
    kinds = [(2, False), (1, True)]
    share = share_of(inner + 2 * head)

    def kernel(*refs):
        take = Taker(refs)
        hbm_refs = take.take(len(names))
        grad_refs = take.take(2)
        input_grad_ref, norm_gain_ref, gains_ref = take.take(3)
        sum_refs = take.take(2)
        v = dict(zip(names, take.take(len(names))))
        d_mixed, bias, dk, dv, lines_ref, d_norm_ref = take.take(6)
        parts = take.take(2)
        jobs = [
            Reduce(grid, parts[i], sum_refs[i], take.take(Reduce.refs(kinds[i][1])), *kinds[i])
            for i in range(2)
        ]
        side_parts = take.one()
        side_buffers = take.take(3)
        load_sems = take.one()
        side_job = Scatter(side, side_parts, side_buffers, 2, take.take(6))
        me, z, _ = position(grid)
        plan = Plan(lines)
        for job in jobs:
            job.plan(plan, [(i + 1) * PAIR_US for i in range(lines)], False)
        order = plan.order()

        loads = [
            pltpu.make_async_copy(ref, v[name], load_sems.at[i])
            for i, (name, ref) in enumerate(zip(names, hbm_refs))
        ]
        for c in loads:
            c.start()
        greet([grid, side])

        for c in loads[:2]:
            c.wait()
        d_attn = v["d_attn"]

        @pl.loop(0, lines)
        def _(i):
            k = jnp.int32(0)
            for at in range(lines):
                for step in range(lines):
                    k = jnp.where(jnp.logical_and(z == at, i == step), orders[at][step], k)
            lanes = pl.ds(pl.multiple_of(k * pair, pair), pair)

            rows = pl.ds(pl.multiple_of(k * pair, pair), pair)
            first = 0
            for n in range(2):

                value = dot_tn(v["mixed"][:, lanes], d_attn[:, first : first + split[n]])
                parts[n][rows, :] = value.astype(BF)
                first += split[n]
                for p in range(kinds[n][0]):
                    jobs[n].start_one(k, p)

        for c in loads[2:]:
            c.wait()
        rows_at = lax.broadcasted_iota(jnp.int32, (tokens, tokens), 0)
        cols_at = lax.broadcasted_iota(jnp.int32, (tokens, tokens), 1)
        allowed = jnp.logical_and(v["doc_col"][...] == v["doc_row"][...], rows_at >= cols_at)
        bias[...] = jnp.where(allowed, 0.0, -1e30)
        dk[...] = jnp.zeros_like(dk)
        dv[...] = jnp.zeros_like(dv)
        gains_ref[...] = jnp.zeros_like(gains_ref)

        @pl.loop(0, inner // tile)
        def _(t):
            rows = pl.ds(pl.multiple_of(t * tile, tile), tile)
            d_mixed[:, rows] = dot_nt(d_attn[...], v["out_weight"][rows, :]).astype(BF)

        def unturn(grad):
            turned = pltpu.roll(grad * v["sine"][...], head // 2, 1)
            return grad * v["cosine"][...] + turned

        def unnorm(grad, linear, gain, row):
            inverse = lax.rsqrt(jnp.mean(linear * linear, axis=-1, keepdims=True) + EPS)
            gains_ref[row : row + 1, :] = gains_ref[row : row + 1, :] + jnp.sum(
                grad * linear * inverse, axis=0, keepdims=True
            )
            return rms_backward(linear, inverse, gain, grad)

        begin = lines * PAIR_US + 3.0

        @pl.loop(0, heads)
        def _(h):
            lanes = pl.ds(pl.multiple_of(h * head, head), head)
            grads = []
            for first in range(0, tokens, block):
                rows = pl.ds(first, block)
                keys = pl.ds(0, first + block)
                query = v["query"][rows, lanes]
                scores = dot_nt(query, v["key"][keys, :])
                probs = jnp.exp(scores * scale + bias[rows, keys] - v["log_total"][h, rows, :])
                back = d_mixed[rows, lanes]
                d_probs = dot_nt(back, v["value"][keys, :])
                inner_sum = jnp.sum(probs * d_probs, axis=-1, keepdims=True)
                d_scores = (probs * (d_probs - inner_sum)).astype(BF)
                dv[keys, :] = dv[keys, :] + dot_tn(probs.astype(BF), back)
                dk[keys, :] = dk[keys, :] + dot_tn(d_scores, query)
                grads.append(dot(d_scores, v["key"][keys, :]))
            grad = jnp.concatenate(grads, axis=0) * scale
            grad = unnorm(unturn(grad), v["query_lin"][:, lanes], v["query_gain"][...], 0)
            lines_ref[:, lanes] = grad.astype(BF)
            plan.run_step(grid, order, h, begin, HEAD_US, heads, True)

        grad = unnorm(unturn(dk[...] * scale), v["key_lin"][...], v["key_gain"][...], 1)
        lines_ref[:, inner : inner + head] = grad.astype(BF)
        lines_ref[:, inner + head : inner + 2 * head] = dv[...].astype(BF)

        @pl.loop(0, columns // tile)
        def _(t):
            rows = pl.ds(pl.multiple_of(t * tile, tile), tile)
            value = dot_nt(lines_ref[:, :inner], v["query_weight"][rows, :])
            value = value + dot_nt(lines_ref[:, inner : inner + head], v["key_weight"][rows, :])
            value = value + dot_nt(lines_ref[:, inner + head :], v["value_weight"][rows, :])
            side_parts[:, rows] = value.astype(BF)

        def put_norm(at, total):
            d_norm_ref[at, :] = total

        side_plan = Plan(side[1])
        for p in range(2):
            plan_scatter(side_plan, side_job, p, put_norm)
        side_order = side_plan.order()

        def side_begin(z):
            for _, act in side_order[z][:-2]:
                act()

        def side_end(z):
            for _, act in side_order[z][-2:]:
                act()

        at_each_line(side, side_begin)
        middle = begin + heads * HEAD_US
        tiles = columns // tile

        @pl.loop(0, tiles)
        def _(t):
            rows = pl.ds(pl.multiple_of(t * tile, tile), tile)
            value = dot_tn(v["normed"][:, rows], lines_ref[...])
            grad_refs[0][rows, :] = value[:, :share].astype(BF)
            grad_refs[1][rows, :] = value[:, share:].astype(BF)
            plan.run_step(grid, order, t, middle, TILE_US, tiles)

        at_each_line(side, side_end)
        plan.run(grid, order, middle + tiles * TILE_US, middle + tiles * TILE_US + 6.0)

        norm_gain_ref[...] = jnp.zeros_like(norm_gain_ref)

        @pl.loop(0, own_rows // 16)
        def _(i):
            rows = pl.ds(pl.multiple_of(i * 16, 16), 16)
            value = v["input_own"][rows, :].astype(F32)
            grad = d_norm_ref[rows, :]
            inverse = lax.rsqrt(jnp.mean(value * value, axis=-1, keepdims=True) + EPS)
            norm_gain_ref[0:1, :] = norm_gain_ref[0:1, :] + jnp.sum(
                grad * value * inverse, axis=0, keepdims=True
            )
            back = rms_backward(value, inverse, v["norm_gain"][...], grad)
            input_grad_ref[rows, :] = (v["d_residual"][rows, :] + back).astype(BF)

        plan.run(grid, order, middle + tiles * TILE_US + 6.0, 1e9)

        def end(z):
            for job in jobs:
                job.finish(z)

        at_each_line(grid, end)
        at_each_line(side, side_job.finish)

    dma = pltpu.SemaphoreType.DMA
    values = [arrays[name] for name in names]
    out = pl.pallas_call(
        kernel,
        out_shape=[
            jax.ShapeDtypeStruct((columns, share), BF),
            jax.ShapeDtypeStruct((columns, inner + 2 * head - share), BF),
            jax.ShapeDtypeStruct((own_rows, columns), BF),
            jax.ShapeDtypeStruct((8, columns), F32),
            jax.ShapeDtypeStruct((8, head), F32),
            jax.ShapeDtypeStruct((inner, split[0]), BF),
            jax.ShapeDtypeStruct((inner, split[1]), BF),
        ],
        in_specs=[hbm()] * len(names),
        out_specs=[vmem()] * 5 + [hbm()] * 2,
        scratch_shapes=[pltpu.VMEM(a.shape, a.dtype) for a in values]
        + [
            pltpu.VMEM((tokens, inner), BF),
            pltpu.VMEM((tokens, tokens), F32),
            pltpu.VMEM((tokens, head), F32),
            pltpu.VMEM((tokens, head), F32),
            pltpu.VMEM((tokens, inner + 2 * head), BF),
            pltpu.VMEM((own_rows, columns), F32),
            pltpu.VMEM((inner, split[0]), BF),
            pltpu.VMEM((inner, split[1]), BF),
        ]
        + Reduce.scratch(grid, inner, split[0], BF, *kinds[0])
        + Reduce.scratch(grid, inner, split[1], BF, *kinds[1])
        + [pltpu.VMEM((tokens, columns), BF)]
        + Scatter.buffers(side, own_rows, columns, BF)
        + [dma((len(names),))]
        + Scatter.sems(side, 2),
        compiler_params=params(number),
        name="attention_backward",
    )(*values)
    first, second, input_grad, norm_gain, gains, *out_sums = out
    out_sum = jnp.concatenate(out_sums, axis=1)
    return (first, second), input_grad, norm_gain[0], gains[0], gains[1], out_sum


def rope_tables(positions, head_size):
    half_size = head_size // 2
    frequency = THETA ** (-2.0 * jnp.arange(half_size, dtype=F32) / head_size)
    angles = positions.astype(F32)[:, None] * frequency[None, :]
    return (jnp.cos(angles), jnp.sin(angles))


def apply_rotary(vector, cosine_table, sine_values):
    half_size = vector.shape[-1] // 2
    first_half = vector[..., :half_size]
    second_half = vector[..., half_size:]
    cos_rows = cosine_table[:, None, :]
    sin_rows = sine_values[:, None, :]
    return jnp.concatenate(
        [
            first_half * cos_rows - second_half * sin_rows,
            second_half * cos_rows + first_half * sin_rows,
        ],
        axis=-1,
    )


def root_mean_norm_forward(vector, gain):
    return rms_forward(vector, gain)[0]


def doc_positions(doc_ids):
    row_index = jnp.arange(doc_ids.shape[0], dtype=jnp.int32)
    doc_starts = jnp.concatenate([jnp.ones((1,), jnp.bool_), doc_ids[1:] != doc_ids[:-1]])
    first_row = lax.cummax(jnp.where(doc_starts, row_index, 0), axis=0)
    return row_index - first_row


def from_near(rows, count):
    return lax.ppermute(rows, "shard", [(s, s + 1 - 2 * (s % 2)) for s in range(count)])


def from_far(rows, count):
    return lax.ppermute(rows, "shard", [(s, (s + 2) % count) for s in range(count)])


def local(
    layer_input,
    doc_ids,
    routes,
    norm1_gain,
    query_weight,
    key_matrix,
    value_matrix,
    query_norm_gain,
    key_norm_gain,
    out_weight,
    norm2_gain,
    router_weight,
    gate_weight,
    up_weight,
    down_weight,
    cotangent,
):
    tokens_here, model_width = layer_input.shape
    head_size = query_norm_gain.shape[0]
    heads_here = query_weight.shape[1] // head_size
    kv_here = key_matrix.shape[1] // head_size
    group_size = heads_here // kv_here
    experts_all = router_weight.shape[1]
    local_experts, _, hidden_here = gate_weight.shape
    expert_peers = lax.axis_size("expert")
    shard_count = lax.axis_size("shard")
    rows_here = tokens_here // shard_count
    shard_index = lax.axis_index("shard")
    expert_index = lax.axis_index("expert")
    score_scale = head_size ** (-0.5)
    hidden_all = shard_count * local_experts * hidden_here

    def own(rows):
        return lax.dynamic_slice_in_dim(rows, shard_index * rows_here, rows_here, axis=0)

    def gather_weight(weight):
        return lax.all_gather(weight, "shard", axis=0).reshape(hidden_all, model_width)

    fused = expert_peers * rows_here <= VMEM_ROWS
    cot_own = own(cotangent)
    cot_all = lax.all_gather(cot_own, "expert", axis=0, tiled=True)
    routes_own = own(routes)
    experts = jnp.arange(experts_all, dtype=jnp.int32)
    chosen_own = jnp.any(routes_own[:, :, None] == experts[None, None, :], axis=1)
    gate_weight = jnp.swapaxes(gate_weight, 1, 2)
    up_weight = jnp.swapaxes(up_weight, 1, 2)
    if fused:
        gate_far = from_far(gate_weight, shard_count)
        gate_near = from_near(gate_weight, shard_count)
    else:
        down_all = gather_weight(down_weight)
        gate_all = gather_weight(gate_weight)
        up_all = gather_weight(up_weight)

    inputs = layer_input.astype(F32)
    norm_one, _ = rms_forward(inputs, norm1_gain)
    first_normed_input = norm_one.astype(BF)
    query_linear = dot(first_normed_input, query_weight).reshape(
        tokens_here, heads_here, head_size
    )
    key_linear = dot(first_normed_input, key_matrix).reshape(tokens_here, kv_here, head_size)
    value_token_rows = (
        dot(first_normed_input, value_matrix).astype(BF).reshape(tokens_here, kv_here, head_size)
    )
    positions = doc_positions(doc_ids)
    cosine_table, sine_values = rope_tables(positions, head_size)

    def head_prep(linear, gain):
        return apply_rotary(root_mean_norm_forward(linear, gain), cosine_table, sine_values)

    query_rotated = head_prep(query_linear, query_norm_gain)
    key_rotated = head_prep(key_linear, key_norm_gain)
    query_low = query_rotated.astype(BF).reshape(tokens_here, kv_here, group_size, head_size)
    key_low = key_rotated.astype(BF)
    row_index = jnp.arange(tokens_here)
    allowed = (doc_ids[:, None] == doc_ids[None, :]) & (row_index[:, None] >= row_index[None, :])

    def masked_scores():
        raw_scores = (
            jnp.einsum("tkgd,skd->kgts", query_low, key_low, preferred_element_type=F32)
            * score_scale
        )
        return jnp.where(allowed, raw_scores, -1e30)

    scores = masked_scores()
    row_max = jnp.max(scores, axis=-1, keepdims=True)
    exp_scores = jnp.exp(scores - row_max)
    row_total = jnp.sum(exp_scores, axis=-1, keepdims=True)
    log_total = row_max + jnp.log(row_total)
    probs_low = (exp_scores / row_total).astype(BF)
    mixture = jnp.einsum(
        "kgts,skd->tkgd", probs_low, value_token_rows, preferred_element_type=F32
    )
    mixed = mixture.astype(BF).reshape(tokens_here, heads_here * head_size)
    attn_part = dot(mixed, out_weight)
    attn_part = attn_part.astype(BF)
    if fused:
        gate_far, attn_part = lax.optimization_barrier((gate_far, attn_part))
    attn_own = scatter_rows(attn_part, "shard", 1, 2)

    if fused:
        up_late, down_late, attn_own = lax.optimization_barrier((up_weight, down_weight, attn_own))
        up_far, down_far = from_far(up_late, shard_count), from_far(down_late, shard_count)
        up_near, down_near = from_near(up_late, shard_count), from_near(down_late, shard_count)
    inputs_own = own(layer_input).astype(F32)
    residual = inputs_own + attn_own
    norm_two, inverse_two = rms_forward(residual, norm2_gain)
    normed_two = norm_two.astype(BF)
    normed_all, chosen_all = gather_rows(
        [normed_two, chosen_own.T.astype(F32)], [], 2, (2, 1)
    )
    if fused:
        up_far, down_far, normed_all = lax.optimization_barrier((up_far, down_far, normed_all))
        weights_rel = []
        for own_one, near, far in (
            (gate_weight, gate_near, gate_far),
            (up_weight, up_near, up_far),
            (down_weight, down_near, down_far),
        ):
            weights_rel += [own_one, near, far, from_near(far, shard_count)]
    chosen_all = chosen_all.reshape(expert_peers, experts_all, rows_here).transpose(0, 2, 1)
    chosen_all = chosen_all.reshape(expert_peers * rows_here, experts_all) > 0.5

    def gate_table(rows, chosen):
        logits = jnp.where(chosen, dot(rows, router_weight), -jnp.inf)
        top = jnp.max(logits, axis=-1, keepdims=True)
        powers = jnp.exp(logits - top)
        return powers / jnp.sum(powers, axis=-1, keepdims=True)

    gates_all = gate_table(normed_all, chosen_all)
    gates_here = lax.dynamic_slice_in_dim(
        gates_all, expert_index * local_experts, local_experts, axis=1
    )
    gates_own = gate_table(normed_two, chosen_own)
    inner = heads_here * head_size
    backward = dict(
        mixed=mixed,
        out_weight=out_weight,
        query=query_low.reshape(tokens_here, inner),
        key=key_low.reshape(tokens_here, head_size),
        value=value_token_rows.reshape(tokens_here, head_size),
        query_lin=query_linear.reshape(tokens_here, inner),
        key_lin=key_linear.reshape(tokens_here, head_size),
        log_total=log_total.reshape(heads_here, tokens_here, 1),
        cosine=jnp.concatenate([cosine_table, cosine_table], axis=1),
        sine=jnp.concatenate([-sine_values, sine_values], axis=1),
        query_gain=query_norm_gain[None, :],
        key_gain=key_norm_gain[None, :],
        doc_col=doc_ids[:, None],
        doc_row=doc_ids[None, :],
        query_weight=query_weight,
        key_weight=key_matrix,
        value_weight=value_matrix,
        normed=first_normed_input,
        input_own=own(layer_input),
        norm_gain=norm1_gain[None, :],
    )
    names = list(backward)
    gates_here, gates_own, *values = lax.optimization_barrier(
        (gates_here, gates_own, *backward.values())
    )
    backward = dict(zip(names, values))

    if fused:
        wide = ((0, 0), (0, EXTRA - experts_all))
        own_arrays = (
            residual,
            jnp.pad(gates_own, wide),
            jnp.pad(router_weight, wide),
            norm2_gain[None, :],
        )
        d_residual, d_logits_low, norm2_grad, d_attn, out_part, *grad_parts = expert_rows(
            normed_all, cot_all, gates_here, weights_rel, own_arrays, 3
        )
        d_logits_low, norm2_grad = d_logits_low[:, :experts_all], norm2_grad[0]
        gate_part, up_part, down_part = grad_parts
    else:
        column_expert = (jnp.arange(hidden_all, dtype=jnp.int32) // hidden_here) % local_experts
        gate_columns = jnp.zeros((1, 1), F32)
        for j in range(local_experts):
            gate_columns = jnp.where(column_expert[None, :] == j, gates_here[:, j : j + 1], gate_columns)

        d_act_raw = dot_nt(cot_all, down_all)
        gate_pre = dot_nt(normed_all, gate_all)
        up_pre = dot_nt(normed_all, up_all)
        sig = jax.nn.sigmoid(gate_pre)
        silu = gate_pre * sig
        act = silu * up_pre
        act_gated = (act * gate_columns).astype(BF)
        d_act = d_act_raw * gate_columns
        d_gate_low = (d_act * up_pre * sig * (1.0 + gate_pre * (1.0 - sig))).astype(BF)
        d_up_low = (d_act * silu).astype(BF)
        act_back = act * d_act_raw
        d_gates_here = jnp.stack(
            [
                jnp.sum(jnp.where(column_expert[None, :] == j, act_back, 0.0), axis=1)
                for j in range(local_experts)
            ],
            axis=-1,
        )
        d_rows = dot(d_gate_low, gate_all) + dot(d_up_low, up_all)
        d_rows_own = scatter_rows(d_rows.astype(BF), "expert", 3, 2)
        out_part = dot(act_gated, down_all).astype(BF)

        def split(grad):
            return grad.astype(BF).reshape(shard_count, local_experts, hidden_here, model_width)

        gate_part = split(dot_tn(d_gate_low, normed_all))
        up_part = split(dot_tn(d_up_low, normed_all))
        down_part = split(dot_tn(act_gated, cot_all))

        d_gates_own = lax.all_to_all(
            d_gates_here.reshape(expert_peers, rows_here, local_experts),
            "expert",
            split_axis=0,
            concat_axis=0,
            tiled=True,
        )
        d_gates_own = jnp.swapaxes(d_gates_own, 0, 1).reshape(rows_here, experts_all)

        d_logits = gates_own * (
            d_gates_own - jnp.sum(gates_own * d_gates_own, axis=-1, keepdims=True)
        )
        d_logits_low = d_logits.astype(BF)
        d_normed_two = d_rows_own + dot_nt(d_logits_low, router_weight)
        norm2_grad = jnp.sum(d_normed_two * residual * inverse_two, axis=0)
        d_residual = cot_own.astype(F32) + rms_backward(
            residual, inverse_two, norm2_gain, d_normed_two
        )
        d_attn = gather_rows([], [d_residual.astype(BF)], 7, (2,))[0]
    router_grad = dot_tn(normed_two, d_logits_low)
    backward = dict(mixed=backward.pop("mixed"), d_attn=d_attn, **backward, d_residual=d_residual)
    out_own = lax.psum_scatter(out_part, "expert", scatter_dimension=0, tiled=True)
    def scatter_grad(grad):
        return lax.psum_scatter(grad, "shard", scatter_dimension=0, tiled=False)

    gate_grad = jnp.swapaxes(scatter_grad(gate_part).astype(F32), 1, 2)
    up_grad = jnp.swapaxes(scatter_grad(up_part).astype(F32), 1, 2)

    line_grads, input_grad_own, norm1_grad, d_query_gain, d_key_gain, out_sum = (
        attention_backward(backward, heads_here, 4)
    )
    share = share_of(inner + 2 * head_size)
    out_own, _ = lax.optimization_barrier((out_own, norm1_grad))
    layer_out_own = (residual + out_own).astype(BF)

    flat = jnp.concatenate(
        [router_grad.T.reshape(-1), norm2_grad, norm1_grad, d_query_gain, d_key_gain]
    )
    small_rows = 8 * expert_peers
    small_columns = -(-flat.shape[0] // (128 * small_rows)) * 128
    small = jnp.pad(flat, (0, small_rows * small_columns - flat.shape[0]))
    (line_first, line_second, small), (input_grad, layer_out), down_sum = sum_and_gather(
        *line_grads,
        small.reshape(small_rows, small_columns),
        (input_grad_own, layer_out_own),
        down_part.reshape(hidden_all, model_width),
        5,
    )
    down_grad = down_sum.reshape(local_experts, hidden_here, model_width)
    query_cols = inner - share
    query_sum = jnp.concatenate([line_first, line_second[:, :query_cols]], axis=1)
    key_sum = line_second[:, query_cols : query_cols + head_size]
    value_sum = line_second[:, query_cols + head_size :]
    small = small.reshape(-1)
    bounds = [experts_all * model_width, model_width, model_width, head_size, head_size]
    taken = []
    at = 0
    for bound in bounds:
        taken.append(small[at : at + bound])
        at += bound
    router_sum, norm2_sum, norm1_sum, query_gain_sum, key_gain_sum = taken
    router_sum = router_sum.reshape(experts_all, model_width).T
    return (
        layer_out,
        input_grad,
        norm1_sum,
        query_sum.astype(F32),
        key_sum.astype(F32),
        value_sum.astype(F32),
        query_gain_sum,
        key_gain_sum,
        out_sum.astype(F32),
        norm2_sum,
        router_sum,
        gate_grad,
        up_grad,
        down_grad,
    )


def solution(mesh):
    return jax.shard_map(
        local,
        mesh=mesh,
        in_specs=(
            P("expert", None),
            P("expert"),
            P("expert", None),
            P(),
            P(None, "shard"),
            P(None, "shard"),
            P(None, "shard"),
            P(),
            P(),
            P("shard", None),
            P(),
            P(),
            P("expert", None, "shard"),
            P("expert", None, "shard"),
            P("expert", "shard", None),
            P("expert", None),
        ),
        out_specs=(
            P("expert", None),
            P("expert", None),
            P(),
            P(None, "shard"),
            P(None, "shard"),
            P(None, "shard"),
            P(),
            P(),
            P("shard", None),
            P(),
            P(),
            P("expert", None, "shard"),
            P("expert", None, "shard"),
            P("expert", "shard", None),
        ),
        check_vma=False,
    )
```

```python
import jax
import jax.numpy as jnp
from jax import lax
from jax.experimental import pallas as pl
from jax.experimental.pallas import tpu as pltpu
from jax.sharding import PartitionSpec as P

EPS = 1e-06
THETA = 1000000.0
BF = jnp.bfloat16
F32 = jnp.float32
MESH = pl.DeviceIdType.MESH
VMEM_ROWS = 1024


def dot(a, b):
    return jnp.dot(a, b, preferred_element_type=F32)


def dot_nt(a, b):
    return lax.dot_general(a, b, (((1,), (1,)), ((), ())), preferred_element_type=F32)


def dot_tn(a, b):
    return lax.dot_general(a, b, (((0,), (0,)), ((), ())), preferred_element_type=F32)


LINK_BYTES_PER_US = 1e5


def grid_of(axis):
    size = lax.axis_size(axis)
    lines = 4 if axis == "expert" else 2
    return axis, lines, size // lines, size // lines


def line_of(grid):
    return grid[0], grid[1], 1, grid[3]


def cross_of(grid):
    return grid[0], 1, grid[2], grid[3]


def position(grid):
    axis, lines, width, stride = grid
    me = lax.axis_index(axis)
    return me, me // stride if lines > 1 else 0, me % width if width > 1 else 0


def at_each_line(grid, act):
    _, z, _ = position(grid)
    for at in range(grid[1]):

        @pl.when(z == at)
        def _():
            act(at)


def greet(grids):
    barrier = pltpu.get_barrier_semaphore()
    count = 0
    for grid in grids:
        axis, lines, width, stride = grid
        me, z, b = position(grid)

        def signal(peer):
            pl.semaphore_signal(barrier, inc=1, device_id={axis: peer}, device_id_type=MESH)

        @pl.when(z < lines - 1)
        def _():
            signal(me + stride)

        @pl.when(z > 0)
        def _():
            signal(me - stride)

        for o in range(1, width):
            signal(me - b + (b + o) % width)
        count = count + width - 1
        count = count + (z < lines - 1).astype(jnp.int32) + (z > 0).astype(jnp.int32)
    pl.semaphore_wait(barrier, count)


def slice_of(ref, start, rows):
    if not isinstance(start, int):
        start = pl.multiple_of(start, rows)
    return ref.at[pl.ds(start, rows)]


class Gather:
    def __init__(self, grid, source, out, pieces, sems):
        self.axis, self.lines, self.width, self.stride = grid
        self.source, self.out, self.pieces = source, out, pieces
        self.rows_all = source.shape[0]
        self.rows = self.rows_all // pieces
        self.send_r, self.send_l, self.send_x, self.recv = sems
        self.me, _, self.b = position(grid)
        self.bytes = self.rows * source.shape[1] * jnp.dtype(source.dtype).itemsize

    @staticmethod
    def sems(grid, pieces):
        _, lines, width, _ = grid
        dma = pltpu.SemaphoreType.DMA
        return [
            dma((lines, pieces)),
            dma((lines, pieces)),
            dma((max(1, width - 1), lines, pieces)),
            dma((lines * width, pieces)),
        ]

    def copy(self, slot, p, sem, peer, own=False):
        place = slice_of(self.out, slot * self.rows_all + p * self.rows, self.rows)
        source = slice_of(self.source, p * self.rows, self.rows) if own else place
        return pltpu.make_async_remote_copy(
            src_ref=source,
            dst_ref=place,
            send_sem=sem,
            recv_sem=self.recv.at[slot, p],
            device_id={self.axis: peer},
            device_id_type=MESH,
        )

    def sends(self, z, origin, p):
        slot = origin * self.width + self.b
        own = origin == z
        copies = []
        if origin <= z and z < self.lines - 1:
            sem = self.send_r.at[z - origin, p]
            copies.append(self.copy(slot, p, sem, self.me + self.stride, own))
        if origin >= z and z > 0:
            sem = self.send_l.at[origin - z, p]
            copies.append(self.copy(slot, p, sem, self.me - self.stride, own))
        for o in range(1, self.width):
            peer = self.me - self.b + (self.b + o) % self.width
            copies.append(self.copy(slot, p, self.send_x.at[o - 1, origin, p], peer, own))
        return copies

    def start(self, z, p):
        for c in self.sends(z, z, p):
            c.start()

    def arrived(self, slot, p):
        self.copy(slot, p, self.send_r.at[0, p], self.me).wait_recv()

    def forward(self, z, origin, p):
        self.arrived(origin * self.width + self.b, p)
        for c in self.sends(z, origin, p):
            c.start()

    def arrived_across(self, z, p):
        for o in range(1, self.width):
            self.arrived(z * self.width + (self.b + o) % self.width, p)

    def wait_sends(self, z):
        for p in range(self.pieces):
            for origin in range(self.lines):
                for c in self.sends(z, origin, p):
                    c.wait_send()

    def finish(self, z):
        for p in range(self.pieces):
            for line in range(self.lines):
                self.arrived_across(line, p)
        self.wait_sends(z)

    def own_slot(self, z):
        return slice_of(self.out, (z * self.width + self.b) * self.rows_all, self.rows_all)


class Scatter:
    def __init__(self, grid, parts, buffers, pieces, sems):
        self.axis, self.lines, self.width, self.stride = grid
        self.parts, self.pieces = parts, pieces
        self.cross, self.right, self.left = buffers
        self.rows_all = parts.shape[0] // (self.lines * self.width)
        self.rows = self.rows_all // pieces
        self.cross_send, self.cross_recv, self.r_send, self.r_recv, self.l_send, self.l_recv = sems
        self.me, _, self.b = position(grid)
        self.bytes = self.rows * parts.shape[1] * jnp.dtype(parts.dtype).itemsize

    @staticmethod
    def sems(grid, pieces):
        _, lines, width, _ = grid
        dma = pltpu.SemaphoreType.DMA
        across = (max(1, width - 1), lines, pieces)
        return [dma(across), dma(across)] + [dma((lines, pieces)) for _ in range(4)]

    @staticmethod
    def buffers(grid, rows_all, columns, kind):
        _, lines, width, _ = grid
        line = pltpu.VMEM((lines * rows_all if lines > 1 else 16, columns), kind)
        return [pltpu.VMEM((max(1, width - 1) * lines * rows_all, columns), kind), line, line]

    def start_of(self, slot, p):
        return slot * self.rows_all + p * self.rows

    def cross_copy(self, o, k, p):
        peer = (self.b + o) % self.width
        return pltpu.make_async_remote_copy(
            src_ref=slice_of(self.parts, self.start_of(k * self.width + peer, p), self.rows),
            dst_ref=slice_of(self.cross, self.start_of((o - 1) * self.lines + k, p), self.rows),
            send_sem=self.cross_send.at[o - 1, k, p],
            recv_sem=self.cross_recv.at[o - 1, k, p],
            device_id={self.axis: self.me - self.b + peer},
            device_id_type=MESH,
        )

    def line_copy(self, k, p, rightward):
        into = self.right if rightward else self.left
        at = self.start_of(k, p)
        return pltpu.make_async_remote_copy(
            src_ref=slice_of(self.cross, at, self.rows),
            dst_ref=slice_of(into, at, self.rows),
            send_sem=(self.r_send if rightward else self.l_send).at[k, p],
            recv_sem=(self.r_recv if rightward else self.l_recv).at[k, p],
            device_id={self.axis: self.me + self.stride if rightward else self.me - self.stride},
            device_id_type=MESH,
        )

    def start_one(self, k, p):
        for o in range(1, self.width):
            self.cross_copy(o, k, p).start()

    def add(self, k, p, sources, target):
        block = min(16, self.rows)
        own = self.start_of(k * self.width + self.b, p)

        @pl.loop(0, self.rows // block)
        def _(i):
            def rows_at(start):
                return pl.ds(pl.multiple_of(start + i * block, block), block)

            total = self.parts[rows_at(own), :].astype(F32)
            for o in range(self.width - 1):
                at = rows_at(self.start_of(o * self.lines + k, p))
                total = total + self.cross[at, :].astype(F32)
            for source in sources:
                total = total + source[rows_at(self.start_of(k, p)), :].astype(F32)
            target(rows_at(p * self.rows), total)

    def sources(self, z, k, p):
        found = []
        if k >= z and z > 0:
            self.line_copy(k, p, True).wait_recv()
            found.append(self.right)
        if k <= z and z < self.lines - 1:
            self.line_copy(k, p, False).wait_recv()
            found.append(self.left)
        return found

    def reduce_one(self, z, k, p):
        for o in range(1, self.width):
            self.cross_copy(o, k, p).wait_recv()

        def put(at, total):
            offset = pl.multiple_of(at.start + k * self.rows_all, at.size)
            self.cross[pl.ds(offset, at.size), :] = total.astype(self.cross.dtype)

        self.add(k, p, self.sources(z, k, p), put)
        self.line_copy(k, p, k > z).start()

    def total(self, z, p, target):
        for o in range(1, self.width):
            self.cross_copy(o, z, p).wait_recv()
        self.add(z, p, self.sources(z, z, p), target)

    def finish(self, z):
        for p in range(self.pieces):
            for k in range(self.lines):
                for o in range(1, self.width):
                    self.cross_copy(o, k, p).wait_send()
                if k != z:
                    self.line_copy(k, p, k > z).wait_send()


def targets(lines, z):
    others = sorted((k for k in range(lines) if k != z), key=lambda k: (-abs(k - z), -k))
    return others + [z]


class Plan:
    def __init__(self, lines):
        self.lines = lines
        self.steps = [[] for _ in range(lines)]
        self.jobs = 0

    def job(self):
        self.jobs += 1
        return self.jobs

    def add(self, z, waits, act, sends, begin=0.0):
        self.steps[z].append((begin, waits, act, sends))

    def order(self):
        arrived = [dict() for _ in range(self.lines)]
        free = {}
        clock = [0.0] * self.lines
        left = [list(enumerate(steps)) for steps in self.steps]
        result = [[] for _ in range(self.lines)]
        while any(left):
            best = None
            for z in range(self.lines):
                for i, (begin, waits, act, sends) in left[z]:
                    if all(key in arrived[z] for key in waits):
                        ready = max([begin] + [arrived[z][key] for key in waits])
                        if best is None or (max(ready, clock[z]), ready, z, i) < best[0]:
                            best = ((max(ready, clock[z]), ready, z, i), act, sends)
            (now, _, z, i), act, sends = best
            left[z] = [entry for entry in left[z] if entry[0] != i]
            result[z].append((now, act))
            clock[z] = now + 0.7
            for link, time, to, key in sends:
                start = max(now + 1.0, free.get((z, link), 0.0))
                free[z, link] = start + time
                arrived[to][key] = start + time + 1.0
        return result

    def run(self, grid, result, begin, end):
        def act(z):
            for now, step in result[z]:
                if begin <= now < end:
                    step()

        at_each_line(grid, act)


    def run_step(self, grid, result, index, begin, each, steps, early=False):
        _, z, _ = position(grid)
        for at in range(self.lines):
            for now, step in result[at]:
                due = int((now - begin) // each)
                if early:
                    due = max(0, due)
                if 0 <= due < steps:

                    @pl.when(jnp.logical_and(z == at, index == due))
                    def _():
                        step()


def plan_scatter(plan, scatter, p, put, then=None, begin=0.0, start=True):
    n = plan.job()
    lines, width = scatter.lines, scatter.width
    time = 2 * scatter.bytes / LINK_BYTES_PER_US
    for z in range(lines):
        ready = begin if isinstance(begin, (int, float)) else None
        for i, k in enumerate(targets(lines, z)):
            first = ready if ready is not None else begin[i]
            if width > 1:
                plan.add(
                    z,
                    [],
                    (lambda k=k: scatter.start_one(k, p)) if start else (lambda: None),
                    [("x", time * (width - 1), z, (n, "c", k))],
                    first,
                )
            waits = [(n, "c", k)] if width > 1 else []
            if k >= z and z > 0:
                waits.append((n, "r", k))
            if k <= z and z < lines - 1:
                waits.append((n, "l", k))
            if k > z:
                sends = [("r", time, z + 1, (n, "r", k))]
            elif k < z:
                sends = [("l", time, z - 1, (n, "l", k))]
            else:
                follow, sends = then(z) if then else ((lambda: None), [])

                def last(z=z, follow=follow):
                    scatter.total(z, p, put)
                    follow()

                plan.add(z, waits, last, sends, first)
                continue
            plan.add(z, waits, lambda z=z, k=k: scatter.reduce_one(z, k, p), sends, first)


def gather_sends(gather, n, time, z, origin):
    sends = []
    if origin <= z and z < gather.lines - 1:
        sends.append(("r", time, z + 1, (n, "g", origin)))
    if origin >= z and z > 0:
        sends.append(("l", time, z - 1, (n, "g", origin)))
    if gather.width > 1:
        sends.append(("x", time * (gather.width - 1), z, (n, "gx", origin)))
    return sends


def plan_gather(plan, gather, p, begin=None):
    n = plan.job()
    time = 2 * gather.bytes / LINK_BYTES_PER_US
    for z in range(gather.lines):
        for origin in range(gather.lines):
            if origin != z:
                plan.add(
                    z,
                    [(n, "g", origin)],
                    lambda z=z, origin=origin: gather.forward(z, origin, p),
                    gather_sends(gather, n, time, z, origin),
                )

    def then(z):
        return (lambda: gather.start(z, p)), gather_sends(gather, n, time, z, z)

    if begin is not None:
        for z in range(gather.lines):
            act, sends = then(z)
            plan.add(z, [], act, sends, begin)
    return then


class Reduce:
    def __init__(self, grid, parts, out, scratch, pieces, line_first):
        self.grid, self.parts, self.out = grid, parts, out
        self.line_first = line_first
        self.pieces = pieces
        take = Taker(scratch)
        self.sums = take.one()
        if line_first:
            self.pair_sums, self.pair_all = take.take(2)
            self.first = Scatter(line_of(grid), parts, take.take(3), 1, take.take(6))
            self.second = Scatter(cross_of(grid), self.pair_sums, take.take(3), 1, take.take(6))
            self.third = Gather(cross_of(grid), self.sums, self.pair_all, 1, take.take(4))
            self.fourth = Gather(line_of(grid), self.pair_all, out, 1, take.take(4))
        else:
            self.scatter = Scatter(grid, parts, take.take(3), pieces, take.take(6))
            self.gather = Gather(grid, self.sums, out, pieces, take.take(4))
        self.own_sem = take.one()

    @staticmethod
    def scratch(grid, rows, columns, kind, pieces, line_first):
        _, lines, width, _ = grid
        count = rows // (lines * width)
        shapes = [pltpu.VMEM((count, columns), kind)]
        if line_first:
            line, cross = line_of(grid), cross_of(grid)
            shapes += [pltpu.VMEM((width * count, columns), kind)] * 2
            shapes += Scatter.buffers(line, width * count, columns, kind) + Scatter.sems(line, 1)
            shapes += Scatter.buffers(cross, count, columns, kind) + Scatter.sems(cross, 1)
            shapes += Gather.sems(cross, 1) + Gather.sems(line, 1)
        else:
            shapes += Scatter.buffers(grid, count, columns, kind) + Scatter.sems(grid, pieces)
            shapes += Gather.sems(grid, pieces)
        return shapes + [pltpu.SemaphoreType.DMA]

    @staticmethod
    def refs(line_first):
        return 1 + (2 + 9 + 9 + 8 if line_first else 9 + 4) + 1

    def put(self, at, total):
        self.sums[at, :] = total.astype(self.sums.dtype)

    def put_pair(self, at, total):
        self.pair_sums[at, :] = total.astype(self.pair_sums.dtype)

    def own_copy(self, z):
        if self.line_first:
            return pltpu.make_async_copy(self.pair_all, self.fourth.own_slot(z), self.own_sem)
        return pltpu.make_async_copy(self.sums, self.gather.own_slot(z), self.own_sem)

    def start_one(self, k, p):
        if not self.line_first:
            self.scatter.start_one(k, p)

    def plan(self, plan, begin=0.0, start=True):
        if not self.line_first:
            for p in range(self.pieces):
                then = plan_gather(plan, self.gather, p)
                plan_scatter(plan, self.scatter, p, self.put, then, begin, start)
            return
        n = plan.job()
        time = 2 * self.second.bytes / LINK_BYTES_PER_US * (self.grid[2] - 1)
        along = plan_gather(plan, self.fourth, 0)

        def cross(z):
            return (lambda: self.second.start_one(0, 0)), [("x", time, z, (n, "c"))]

        plan_scatter(plan, self.first, 0, self.put_pair, cross, begin)
        for z in range(self.grid[1]):

            def across(z=z):
                self.second.total(0, 0, self.put)
                self.third.start(0, 0)
                at = pl.multiple_of(self.third.b * self.third.rows_all, self.third.rows_all)
                self.pair_all[pl.ds(at, self.third.rows_all), :] = self.sums[...]

            plan.add(z, [(n, "c")], across, [("x", time, z, (n, "x"))])
            follow, sends = along(z)

            def spread(follow=follow):
                self.third.arrived_across(0, 0)
                follow()

            plan.add(z, [(n, "x")], spread, sends)

    def finish(self, z):
        self.own_copy(z).start()
        if self.line_first:
            self.first.finish(z)
            self.second.finish(0)
            self.third.wait_sends(0)
            self.fourth.finish(z)
        else:
            self.scatter.finish(z)
            self.gather.finish(z)
        self.own_copy(z).wait()


def hbm():
    return pl.BlockSpec(memory_space=pl.ANY)


def vmem():
    return pl.BlockSpec(memory_space=pltpu.VMEM)


def params(number, mib=56):
    return pltpu.CompilerParams(
        collective_id=number, has_side_effects=True, vmem_limit_bytes=mib * 1024 * 1024
    )


class Taker:
    def __init__(self, refs):
        self.refs = list(refs)

    def take(self, count):
        taken = self.refs[:count]
        del self.refs[:count]
        return taken

    def one(self):
        return self.take(1)[0]


ALWAYS = (0.0, 1e9)


def gather_rows(arrays, side_arrays, number, pieces):
    grid, side = grid_of("expert"), grid_of("shard")
    values = list(arrays) + list(side_arrays)
    grids = [grid] * len(arrays) + [side] * len(side_arrays)
    n = len(values)

    def kernel(*refs):
        take = Taker(refs)
        ins, outs, own_sems = take.take(n), take.take(n), take.one()
        jobs = [Gather(grids[i], ins[i], outs[i], pieces[i], take.take(4)) for i in range(n)]

        def own(i, z):
            return pltpu.make_async_copy(ins[i], jobs[i].own_slot(z), own_sems.at[i])

        def each(i, act):
            at_each_line(grids[i], act)

        for i in range(n):
            each(i, lambda z, i=i: own(i, z).start())
        greet([grid] + ([side] if side_arrays else []))
        plan = Plan(grid[1])
        for i in range(len(arrays)):
            for p in range(pieces[i]):
                plan_gather(plan, jobs[i], p, 0.0)
        order = plan.order()
        plan.run(grid, order, 0.0, 1.0)
        late = 0.0 if not side_arrays else 1.0
        for i in range(len(arrays), n):
            for p in range(pieces[i]):
                each(i, lambda z, i=i, p=p: jobs[i].start(z, p))
        if side_arrays:
            edge = 2 * jobs[-1].bytes / LINK_BYTES_PER_US + 4.0
            begin = late
            for p in range(pieces[-1]):
                plan.run(grid, order, begin, edge * (p + 1))
                begin = edge * (p + 1)
                for i in range(len(arrays), n):

                    def forward(z, i=i, p=p):
                        for origin in range(grids[i][1]):
                            if origin != z:
                                jobs[i].forward(z, origin, p)

                    each(i, forward)
            plan.run(grid, order, begin, 1e9)
        else:
            plan.run(grid, order, 1.0, 1e9)
        for i in range(n):
            each(i, lambda z, i=i: jobs[i].finish(z))
            each(i, lambda z, i=i: own(i, z).wait())

    scratch = [pltpu.SemaphoreType.DMA((n,))]
    for g, p in zip(grids, pieces):
        scratch += Gather.sems(g, p)
    return pl.pallas_call(
        kernel,
        out_shape=[
            jax.ShapeDtypeStruct((g[1] * g[2] * a.shape[0], a.shape[1]), a.dtype)
            for a, g in zip(values, grids)
        ],
        in_specs=[hbm()] * n,
        out_specs=[hbm()] * n,
        scratch_shapes=scratch,
        compiler_params=params(number),
        name="gather_rows",
    )(*values)


def scatter_rows(parts, axis, number, pieces):
    grid = grid_of(axis)
    columns = parts.shape[1]
    count = parts.shape[0] // (grid[1] * grid[2])

    def kernel(parts_ref, out_ref, cross, right, left, *sems):
        greet([grid])
        job = Scatter(grid, parts_ref, (cross, right, left), pieces, sems)

        def put(at, total):
            out_ref[at, :] = total

        plan = Plan(grid[1])
        for p in range(pieces):
            plan_scatter(plan, job, p, put)
        plan.run(grid, plan.order(), *ALWAYS)
        at_each_line(grid, job.finish)

    return pl.pallas_call(
        kernel,
        out_shape=jax.ShapeDtypeStruct((count, columns), F32),
        in_specs=[vmem()],
        out_specs=vmem(),
        scratch_shapes=Scatter.buffers(grid, count, columns, parts.dtype)
        + Scatter.sems(grid, pieces),
        compiler_params=params(number),
        name="scatter_" + axis,
    )(parts)


def sum_and_gather(across_first, line_first, small, rows, spread, number):
    grid, side = grid_of("expert"), grid_of("shard")
    size = grid[1] * grid[2]
    shards = side[1] * side[2]
    values = [across_first, line_first, small]
    moved = [small] + list(rows)
    m = len(moved)
    kinds = [(2, False), (1, True), (1, False)]

    def kernel(*refs):
        take = Taker(refs)
        first_ref, second_ref, spread_ref = take.take(3)
        side_ins = take.take(m)
        outs, rows_outs, spread_out = take.take(3), take.take(m - 1), take.one()
        small_all, small_parts, own_sems = take.take(3)
        ins = [first_ref, second_ref, small_parts]
        jobs = [
            Reduce(grid, ins[i], outs[i], take.take(Reduce.refs(kinds[i][1])), *kinds[i])
            for i in range(3)
        ]
        spread_job = Scatter(side, spread_ref, take.take(3), 1, take.take(6))
        side_outs = [small_all] + rows_outs
        side_jobs = [Gather(side, side_ins[i], side_outs[i], 1, take.take(4)) for i in range(m)]

        def own(z, i):
            return pltpu.make_async_copy(side_ins[i], side_jobs[i].own_slot(z), own_sems.at[i])

        def begin_side(z):
            for i in range(m):
                own(z, i).start()

        at_each_line(side, begin_side)
        greet([grid, side])
        edges = [0.0, 6.0, 16.0, 28.0, 55.0]
        plan = Plan(grid[1])
        jobs[1].plan(plan)
        jobs[0].plan(plan)
        jobs[2].plan(plan, edges[3])
        order = plan.order()
        plan.run(grid, order, 0.0, edges[1])
        at_each_line(side, lambda z: side_jobs[0].start(z, 0))
        plan.run(grid, order, edges[1], edges[2])

        def forward(z, chosen):
            for origin in range(side[1]):
                if origin != z:
                    for job in chosen:
                        job.forward(z, origin, 0)

        def start(z):
            forward(z, side_jobs[:1])
            for job in side_jobs[1:]:
                job.start(z, 0)
            for k in targets(side[1], z):
                spread_job.start_one(k, 0)

        at_each_line(side, start)
        plan.run(grid, order, edges[2], edges[3])

        def end_small(z):
            side_jobs[0].finish(z)
            own(z, 0).wait()

        at_each_line(side, end_small)
        count = small.shape[0]
        total = small_all[pl.ds(0, count), :]
        for s in range(1, shards):
            total = total + small_all[pl.ds(s * count, count), :]
        small_parts[...] = total
        plan.run(grid, order, edges[3], edges[4])

        def spread_on(z):
            for k in targets(side[1], z)[:-1]:
                spread_job.reduce_one(z, k, 0)
            forward(z, side_jobs[1:])

        at_each_line(side, spread_on)
        plan.run(grid, order, edges[4], 1e9)

        def end(z):
            for job in jobs:
                job.finish(z)

        at_each_line(grid, end)

        def put_spread(at, total):
            spread_out[at, :] = total

        def end_rows(z):
            spread_job.total(z, 0, put_spread)
            spread_job.finish(z)
            for i in range(1, m):
                side_jobs[i].finish(z)
                own(z, i).wait()

        at_each_line(side, end_rows)

    scratch = [
        pltpu.VMEM((shards * small.shape[0], small.shape[1]), small.dtype),
        pltpu.VMEM(small.shape, small.dtype),
        pltpu.SemaphoreType.DMA((m,)),
    ]
    for a, kind in zip(values, kinds):
        scratch += Reduce.scratch(grid, a.shape[0], a.shape[1], a.dtype, *kind)
    spread_rows = spread.shape[0] // shards
    scratch += Scatter.buffers(side, spread_rows, spread.shape[1], BF) + Scatter.sems(side, 1)
    for _ in range(m):
        scratch += Gather.sems(side, 1)
    out = pl.pallas_call(
        kernel,
        out_shape=[jax.ShapeDtypeStruct(a.shape, a.dtype) for a in values]
        + [jax.ShapeDtypeStruct((shards * a.shape[0], a.shape[1]), a.dtype) for a in rows]
        + [jax.ShapeDtypeStruct((spread_rows, spread.shape[1]), F32)],
        in_specs=[vmem()] * 3 + [hbm()] * m,
        out_specs=[hbm()] * (2 + m) + [vmem()],
        scratch_shapes=scratch,
        compiler_params=params(number),
        name="sum_and_gather",
    )(across_first, line_first, spread, small, *rows)
    return out[:3], out[3:-1], out[-1]


CHUNK_US = 4.0
PAIR_US = 1.5
HEAD_US = 5.5
TILE_US = 1.5
EXTRA = 128


def share_of(columns):
    return 4 * columns // 5 // 256 * 256


def expert_rows(normed, cot, gates, weights_rel, shards, number):
    grid = grid_of("expert")
    _, lines, width, _ = grid
    size = lines * width
    experts, hidden, columns = weights_rel[0].shape
    full = shards * hidden
    both = 2 * full
    total_rows = normed.shape[0]
    count = total_rows // size
    pair = width * count
    tile = 256
    half = 512
    wide = 2 * hidden
    extra = EXTRA
    orders = [targets(lines, z) for z in range(lines)]
    out_tiles = columns // tile
    grad_tiles = experts * 3 * full // wide
    out_us, grad_us = 1.3, 2.3

    def kernel(*refs):
        take = Taker(refs)
        normed_hbm, cot_hbm, gates_ref = take.take(3)
        gate_hbm, up_hbm, down_hbm = take.take(shards), take.take(shards), take.take(shards)
        sum_ref, out_hbm = take.take(2)
        grad_hbm = take.take(3)
        normed_v, cot_v, weights, down = take.take(4)
        grads_low, act_low, parts = take.take(3)
        buffers = take.take(3)
        out_stage, grad_stage, d_gates_ref = take.take(3)
        load_sems, weight_sems, out_sems, grad_sems = take.take(4)
        job = Scatter(grid, parts, buffers, 1, take.take(6))
        me, z, _ = position(grid)

        def put(at, total):
            sum_ref[at, :] = total

        plan = Plan(lines)
        plan_scatter(
            plan, job, 0, put, None, [(i + 1) * CHUNK_US for i in range(lines)], False
        )
        order = plan.order()
        shard = lax.axis_index("shard")
        near = shard + 1 - 2 * (shard % 2)
        places = [shard, near, (shard + 2) % shards, (near + 2) % shards]

        loads = [
            pltpu.make_async_copy(normed_hbm, normed_v, load_sems.at[0]),
            pltpu.make_async_copy(cot_hbm, cot_v, load_sems.at[1]),
        ]
        weight_loads = [[] for _ in range(experts)]
        for j in range(experts):
            for r in range(shards):
                for w, (source, target) in enumerate(
                    (
                        (gate_hbm[r].at[j], weights.at[pl.ds(j * both + r * hidden, hidden)]),
                        (up_hbm[r].at[j], weights.at[pl.ds(j * both + full + r * hidden, hidden)]),
                        (down_hbm[r].at[j], down.at[pl.ds(j * full + r * hidden, hidden)]),
                    )
                ):
                    weight_loads[j].append(
                        pltpu.make_async_copy(source, target, weight_sems.at[j, r, w])
                    )
        for c in loads + weight_loads[0]:
            c.start()
        for j in range(1, experts):
            for c in weight_loads[j]:
                c.start()
        greet([grid])
        for c in loads:
            c.wait()

        for j in range(experts):
            for c in weight_loads[j]:
                c.wait()

            @pl.loop(0, total_rows // half)
            def _(m):
                rows = pl.ds(pl.multiple_of(m * half, half), half)

                @pl.loop(0, full // tile)
                def _(t):
                    at = t * tile

                    def lines_of(base):
                        return pl.ds(pl.multiple_of(base + at, tile), tile)

                    x = normed_v[rows, :]
                    gate_pre = dot_nt(x, weights[lines_of(j * both), :])
                    up_pre = dot_nt(x, weights[lines_of(j * both + full), :])
                    back = dot_nt(cot_v[rows, :], down[lines_of(j * full), :])
                    probs = gates_ref[rows, j : j + 1]
                    sig = 1.0 / (1.0 + jnp.exp(-gate_pre))
                    silu = gate_pre * sig
                    act = silu * up_pre
                    act_low[rows, lines_of(j * full)] = (act * probs).astype(BF)
                    d_act = back * probs
                    d_gate = d_act * up_pre * (sig * (1.0 + gate_pre * (1.0 - sig)))
                    grads_low[rows, lines_of(j * both)] = d_gate.astype(BF)
                    grads_low[rows, lines_of(j * both + full)] = (d_act * silu).astype(BF)
                    part = jnp.sum(act * back, axis=1, keepdims=True)

                    @pl.when(t == 0)
                    def _():
                        d_gates_ref[rows, j : j + 1] = part

                    @pl.when(t > 0)
                    def _():
                        d_gates_ref[rows, j : j + 1] = d_gates_ref[rows, j : j + 1] + part

        lane = lax.broadcasted_iota(jnp.int32, (count, extra), 1)

        @pl.loop(0, size)
        def _(e):
            rows = pl.ds(pl.multiple_of(e * count, count), count)
            block = jnp.zeros((count, extra), F32)
            for j in range(experts):
                value = d_gates_ref[rows, j : j + 1]
                high = value.astype(BF).astype(F32)
                mine = me * experts + j
                block = jnp.where(lane == mine, high, block)
                block = jnp.where(lane == mine + size * experts, value - high, block)
            parts[rows, columns:] = block.astype(BF)

        @pl.loop(0, lines)
        def _(i):
            k = jnp.int32(0)
            for at in range(lines):
                for step in range(lines):
                    k = jnp.where(jnp.logical_and(z == at, i == step), orders[at][step], k)
            rows = pl.ds(pl.multiple_of(k * pair, pair), pair)

            @pl.loop(0, columns // tile)
            def _(t):
                cols = pl.ds(pl.multiple_of(t * tile, tile), tile)
                value = dot(grads_low[rows, :], weights[:, cols])
                parts[rows, cols] = value.astype(BF)

            job.start_one(k, 0)

        begin = lines * CHUNK_US

        def out_copy(t, slot):
            cols = pl.ds(pl.multiple_of(t * tile, tile), tile)
            return pltpu.make_async_copy(
                out_stage.at[slot], out_hbm.at[:, cols], out_sems.at[slot]
            )

        plan.run(grid, order, -1.0, begin)

        @pl.loop(0, out_tiles)
        def _(t):
            slot = t % 2

            @pl.when(t >= 2)
            def _():
                out_copy(t - 2, slot).wait()

            cols = pl.ds(pl.multiple_of(t * tile, tile), tile)
            out_stage[slot, :, :] = dot(act_low[...], down[:, cols]).astype(BF)
            out_copy(t, slot).start()
            plan.run_step(grid, order, t, begin, out_us, out_tiles)

        begin = begin + out_tiles * out_us

        def grad_copies(kind, j, r, slot):
            copies = []
            for h in range(2):
                place = places[h]
                for step in range(1, shards // 2):
                    place = jnp.where(r == step, places[2 * step + h], place)
                copies.append(
                    pltpu.make_async_copy(
                        grad_stage.at[slot, pl.ds(h * hidden, hidden)],
                        grad_hbm[kind].at[place, j],
                        grad_sems.at[slot, h],
                    )
                )
            return copies

        per = full // wide
        for kind in range(3):

            @pl.loop(0, experts * per)
            def _(i):
                j, r = i // per, i % per
                slot = i % 2
                if kind == 2:
                    low, base, rows_v = act_low, j * full, cot_v
                else:
                    low, base, rows_v = grads_low, j * both + kind * full, normed_v
                lanes = pl.ds(pl.multiple_of(base + r * wide, wide), wide)

                @pl.when(i >= 2)
                def _():
                    for c in grad_copies(kind, (i - 2) // per, (i - 2) % per, slot):
                        c.wait()

                for q in range(2):
                    cols = pl.ds(q * columns // 2, columns // 2)
                    value = dot_tn(low[:, lanes], rows_v[:, cols])
                    grad_stage[slot, :, cols] = value.astype(BF)
                for c in grad_copies(kind, j, r, slot):
                    c.start()
                plan.run_step(grid, order, i, begin, grad_us, experts * per)

            for i in range(max(0, experts * per - 2), experts * per):
                for c in grad_copies(kind, i // per, i % per, i % 2):
                    c.wait()
            begin = begin + experts * per * grad_us

        plan.run(grid, order, begin, 1e9)

        for t in range(max(0, out_tiles - 2), out_tiles):
            out_copy(t, t % 2).wait()
        at_each_line(grid, job.finish)

    dma = pltpu.SemaphoreType.DMA
    weight_shape = jax.ShapeDtypeStruct((shards, experts, hidden, columns), BF)
    return pl.pallas_call(
        kernel,
        out_shape=[
            jax.ShapeDtypeStruct((count, columns + extra), F32),
            jax.ShapeDtypeStruct((total_rows, columns), BF),
            weight_shape,
            weight_shape,
            weight_shape,
        ],
        in_specs=[hbm()] * 2 + [vmem()] + [hbm()] * (3 * shards),
        out_specs=[vmem()] + [hbm()] * 4,
        scratch_shapes=[
            pltpu.VMEM((total_rows, columns), BF),
            pltpu.VMEM((total_rows, columns), BF),
            pltpu.VMEM((experts * both, columns), BF),
            pltpu.VMEM((experts * full, columns), BF),
            pltpu.VMEM((total_rows, experts * both), BF),
            pltpu.VMEM((total_rows, experts * full), BF),
            pltpu.VMEM((total_rows, columns + extra), BF),
        ]
        + Scatter.buffers(grid, count, columns + extra, BF)
        + [
            pltpu.VMEM((2, total_rows, tile), BF),
            pltpu.VMEM((2, wide, columns), BF),
            pltpu.VMEM((total_rows, experts), F32),
            dma((2,)),
            dma((experts, shards, 3)),
            dma((2,)),
            dma((2, 2)),
        ]
        + Scatter.sems(grid, 1),
        compiler_params=params(number, 62),
        name="expert_rows",
    )(normed, cot, gates, *weights_rel)


def rms_forward(vector, gain):
    inverse = lax.rsqrt(jnp.mean(vector * vector, axis=-1, keepdims=True) + EPS)
    return vector * inverse * gain, inverse


def rms_backward(vector, inverse, gain, grad):
    scaled = grad * gain
    inner = jnp.mean(scaled * vector, axis=-1, keepdims=True)
    return inverse * scaled - vector * (inverse * inverse * inverse * inner)


def attention_forward(arrays, heads, number):
    side = grid_of("shard")
    shards = side[1] * side[2]
    names = list(arrays)
    tokens, columns = arrays["rows"].shape
    inner = arrays["query_weight"].shape[1]
    head = inner // heads
    own_rows = tokens // shards
    tile = 256
    scale = head ** (-0.5)
    block = min(256, tokens)

    def kernel(*refs):
        take = Taker(refs)
        hbm_refs = take.take(len(names))
        normed, query_lin, key_lin, query, key, value, mixed, log_total = take.take(8)
        residual, normed_two = take.take(2)
        v = dict(zip(names, take.take(len(names))))
        bias, parts, summed = take.take(3)
        buffers = take.take(3)
        load_sems = take.one()
        job = Scatter(side, parts, buffers, 2, take.take(6))
        shard = lax.axis_index("shard")
        loads = [
            pltpu.make_async_copy(ref, v[name], load_sems.at[i])
            for i, (name, ref) in enumerate(zip(names, hbm_refs))
        ]
        for c in loads:
            c.start()
        greet([side])
        for c in loads[:-1]:
            c.wait()

        def norm(value, gain):
            return value * lax.rsqrt(jnp.mean(value * value, axis=-1, keepdims=True) + EPS) * gain

        @pl.loop(0, tokens // 32)
        def _(i):
            rows = pl.ds(pl.multiple_of(i * 32, 32), 32)
            normed[rows, :] = norm(v["rows"][rows, :].astype(F32), v["norm_gain"][...]).astype(BF)

        @pl.loop(0, inner // tile)
        def _(t):
            cols = pl.ds(pl.multiple_of(t * tile, tile), tile)
            query_lin[:, cols] = dot(normed[...], v["query_weight"][:, cols])

        key_lin[...] = dot(normed[...], v["key_weight"][...])
        value[...] = dot(normed[...], v["value_weight"][...]).astype(BF)

        def turn(rows):
            return rows * v["cosine"][...] + pltpu.roll(rows, head // 2, 1) * v["sine"][...]

        key[...] = turn(norm(key_lin[...], v["key_gain"][...])).astype(BF)
        rows_at = lax.broadcasted_iota(jnp.int32, (tokens, tokens), 0)
        cols_at = lax.broadcasted_iota(jnp.int32, (tokens, tokens), 1)
        allowed = jnp.logical_and(v["doc_col"][...] == v["doc_row"][...], rows_at >= cols_at)
        bias[...] = jnp.where(allowed, 0.0, -1e30)

        @pl.loop(0, heads)
        def _(h):
            lanes = pl.ds(pl.multiple_of(h * head, head), head)
            query[:, lanes] = turn(norm(query_lin[:, lanes], v["query_gain"][...])).astype(BF)
            for first in range(0, tokens, block):
                rows = pl.ds(first, block)
                keys = pl.ds(0, first + block)
                scores = dot_nt(query[rows, lanes], key[keys, :]) * scale + bias[rows, keys]
                top = jnp.max(scores, axis=-1, keepdims=True)
                powers = jnp.exp(scores - top)
                total = jnp.sum(powers, axis=-1, keepdims=True)
                log_total[h, rows, :] = top + jnp.log(total)
                probs = (powers * (1.0 / total)).astype(BF)
                mixed[rows, lanes] = dot(probs, value[keys, :]).astype(BF)

        loads[-1].wait()

        @pl.loop(0, columns // tile)
        def _(t):
            cols = pl.ds(pl.multiple_of(t * tile, tile), tile)
            parts[:, cols] = dot(mixed[...], v["out_weight"][:, cols]).astype(BF)

        def put(at, total):
            summed[at, :] = total

        plan = Plan(side[1])
        for p in range(2):
            plan_scatter(plan, job, p, put)
        plan.run(side, plan.order(), *ALWAYS)

        @pl.loop(0, own_rows // 16)
        def _(i):
            rows = pl.ds(pl.multiple_of(i * 16, 16), 16)
            from_rows = pl.ds(pl.multiple_of(shard * own_rows + i * 16, 16), 16)
            total = v["rows"][from_rows, :].astype(F32) + summed[rows, :]
            residual[rows, :] = total
            normed_two[rows, :] = norm(total, v["norm_two_gain"][...]).astype(BF)

        at_each_line(side, job.finish)

    values = [arrays[name] for name in names]
    shape = jax.ShapeDtypeStruct
    return pl.pallas_call(
        kernel,
        out_shape=[
            shape((tokens, columns), BF),
            shape((tokens, inner), F32),
            shape((tokens, head), F32),
            shape((tokens, inner), BF),
            shape((tokens, head), BF),
            shape((tokens, head), BF),
            shape((tokens, inner), BF),
            shape((heads, tokens, 1), F32),
            shape((own_rows, columns), F32),
            shape((own_rows, columns), BF),
        ],
        in_specs=[hbm()] * len(names),
        out_specs=[vmem()] * 10,
        scratch_shapes=[pltpu.VMEM(a.shape, a.dtype) for a in values]
        + [
            pltpu.VMEM((tokens, tokens), F32),
            pltpu.VMEM((tokens, columns), BF),
            pltpu.VMEM((own_rows, columns), F32),
        ]
        + Scatter.buffers(side, own_rows, columns, BF)
        + [pltpu.SemaphoreType.DMA((len(names),))]
        + Scatter.sems(side, 2),
        compiler_params=params(number),
        name="attention_forward",
    )(*values)


def attention_backward(arrays, d_own, heads, number):
    grid, side = grid_of("expert"), grid_of("shard")
    _, lines, width, _ = grid
    size = lines * width
    shards = side[1] * side[2]
    names = list(arrays)
    tokens, columns = shards * d_own.shape[0], d_own.shape[1]
    inner = arrays["mixed"].shape[1]
    head = inner // heads
    count = inner // size
    pair = width * count
    tile = 256
    scale = head ** (-0.5)
    block = min(256, tokens)
    orders = [targets(lines, z) for z in range(lines)]
    split = [share_of(columns), columns - share_of(columns)]
    kinds = [(2, False), (1, True)]
    share = share_of(inner + 2 * head)

    def kernel(*refs):
        take = Taker(refs)
        hbm_refs, d_own_ref = take.take(len(names)), take.one()
        grad_refs = take.take(2)
        input_grad_ref, norm_gain_ref, gains_ref = take.take(3)
        sum_refs = take.take(2)
        v = dict(zip(names, take.take(len(names))))
        d_attn, d_mixed, bias, dk, dv, lines_ref, d_norm_ref = take.take(7)
        parts = take.take(2)
        jobs = [
            Reduce(grid, parts[i], sum_refs[i], take.take(Reduce.refs(kinds[i][1])), *kinds[i])
            for i in range(2)
        ]
        side_parts = take.one()
        side_buffers = take.take(3)
        load_sems, own_sems = take.take(2)
        gather = Gather(side, d_own_ref, d_attn, 2, take.take(4))
        side_job = Scatter(side, side_parts, side_buffers, 2, take.take(6))
        me, z, _ = position(grid)
        plan = Plan(lines)
        for job in jobs:
            job.plan(plan, [(i + 1) * PAIR_US for i in range(lines)], False)
        order = plan.order()

        def own(z):
            return pltpu.make_async_copy(d_own_ref, gather.own_slot(z), own_sems.at[0])

        at_each_line(side, lambda z: own(z).start())
        loads = [
            pltpu.make_async_copy(ref, v[name], load_sems.at[i])
            for i, (name, ref) in enumerate(zip(names, hbm_refs))
        ]
        for c in loads:
            c.start()
        greet([grid, side])

        def gather_start(z):
            for p in range(2):
                gather.start(z, p)
            for p in range(2):
                for origin in range(side[1]):
                    if origin != z:
                        gather.forward(z, origin, p)

        at_each_line(side, gather_start)
        for c in loads:
            c.wait()

        rows_at = lax.broadcasted_iota(jnp.int32, (tokens, tokens), 0)
        cols_at = lax.broadcasted_iota(jnp.int32, (tokens, tokens), 1)
        allowed = jnp.logical_and(v["doc_col"][...] == v["doc_row"][...], rows_at >= cols_at)
        bias[...] = jnp.where(allowed, 0.0, -1e30)
        dk[...] = jnp.zeros_like(dk)
        dv[...] = jnp.zeros_like(dv)
        gains_ref[...] = jnp.zeros_like(gains_ref)

        def gather_end(z):
            gather.finish(z)
            own(z).wait()

        at_each_line(side, gather_end)

        @pl.loop(0, lines)
        def _(i):
            k = jnp.int32(0)
            for at in range(lines):
                for step in range(lines):
                    k = jnp.where(jnp.logical_and(z == at, i == step), orders[at][step], k)
            lanes = pl.ds(pl.multiple_of(k * pair, pair), pair)

            rows = pl.ds(pl.multiple_of(k * pair, pair), pair)
            first = 0
            for n in range(2):

                value = dot_tn(v["mixed"][:, lanes], d_attn[:, first : first + split[n]])
                parts[n][rows, :] = value.astype(BF)
                first += split[n]
                for p in range(kinds[n][0]):
                    jobs[n].start_one(k, p)

        @pl.loop(0, inner // tile)
        def _(t):
            rows = pl.ds(pl.multiple_of(t * tile, tile), tile)
            d_mixed[:, rows] = dot_nt(d_attn[...], v["out_weight"][rows, :]).astype(BF)

        def unturn(grad):
            turned = pltpu.roll(grad * v["sine"][...], head // 2, 1)
            return grad * v["cosine"][...] + turned

        def unnorm(grad, linear, gain, row):
            inverse = lax.rsqrt(jnp.mean(linear * linear, axis=-1, keepdims=True) + EPS)
            gains_ref[row : row + 1, :] = gains_ref[row : row + 1, :] + jnp.sum(
                grad * linear * inverse, axis=0, keepdims=True
            )
            return rms_backward(linear, inverse, gain, grad)

        begin = lines * PAIR_US + 3.0

        @pl.loop(0, heads)
        def _(h):
            lanes = pl.ds(pl.multiple_of(h * head, head), head)
            grads = []
            for first in range(0, tokens, block):
                rows = pl.ds(first, block)
                keys = pl.ds(0, first + block)
                query = v["query"][rows, lanes]
                scores = dot_nt(query, v["key"][keys, :])
                probs = jnp.exp(scores * scale + bias[rows, keys] - v["log_total"][h, rows, :])
                back = d_mixed[rows, lanes]
                d_probs = dot_nt(back, v["value"][keys, :])
                inner_sum = jnp.sum(probs * d_probs, axis=-1, keepdims=True)
                d_scores = (probs * (d_probs - inner_sum)).astype(BF)
                dv[keys, :] = dv[keys, :] + dot_tn(probs.astype(BF), back)
                dk[keys, :] = dk[keys, :] + dot_tn(d_scores, query)
                grads.append(dot(d_scores, v["key"][keys, :]))
            grad = jnp.concatenate(grads, axis=0) * scale
            grad = unnorm(unturn(grad), v["query_lin"][:, lanes], v["query_gain"][...], 0)
            lines_ref[:, lanes] = grad.astype(BF)
            plan.run_step(grid, order, h, begin, HEAD_US, heads, True)

        grad = unnorm(unturn(dk[...] * scale), v["key_lin"][...], v["key_gain"][...], 1)
        lines_ref[:, inner : inner + head] = grad.astype(BF)
        lines_ref[:, inner + head : inner + 2 * head] = dv[...].astype(BF)

        @pl.loop(0, columns // tile)
        def _(t):
            rows = pl.ds(pl.multiple_of(t * tile, tile), tile)
            value = dot_nt(lines_ref[:, :inner], v["query_weight"][rows, :])
            value = value + dot_nt(lines_ref[:, inner : inner + head], v["key_weight"][rows, :])
            value = value + dot_nt(lines_ref[:, inner + head :], v["value_weight"][rows, :])
            side_parts[:, rows] = value.astype(BF)

        def put_norm(at, total):
            d_norm_ref[at, :] = total

        side_plan = Plan(side[1])
        for p in range(2):
            plan_scatter(side_plan, side_job, p, put_norm)
        side_order = side_plan.order()

        def side_begin(z):
            for _, act in side_order[z][:-2]:
                act()

        def side_end(z):
            for _, act in side_order[z][-2:]:
                act()

        at_each_line(side, side_begin)
        middle = begin + heads * HEAD_US
        tiles = columns // tile

        @pl.loop(0, tiles)
        def _(t):
            rows = pl.ds(pl.multiple_of(t * tile, tile), tile)
            value = dot_tn(v["normed"][:, rows], lines_ref[...])
            grad_refs[0][rows, :] = value[:, :share].astype(BF)
            grad_refs[1][rows, :] = value[:, share:].astype(BF)
            plan.run_step(grid, order, t, middle, TILE_US, tiles)

        at_each_line(side, side_end)
        plan.run(grid, order, middle + tiles * TILE_US, middle + tiles * TILE_US + 6.0)

        norm_gain_ref[...] = jnp.zeros_like(norm_gain_ref)

        @pl.loop(0, d_own.shape[0] // 16)
        def _(i):
            rows = pl.ds(pl.multiple_of(i * 16, 16), 16)
            value = v["input_own"][rows, :].astype(F32)
            grad = d_norm_ref[rows, :]
            inverse = lax.rsqrt(jnp.mean(value * value, axis=-1, keepdims=True) + EPS)
            norm_gain_ref[0:1, :] = norm_gain_ref[0:1, :] + jnp.sum(
                grad * value * inverse, axis=0, keepdims=True
            )
            back = rms_backward(value, inverse, v["norm_gain"][...], grad)
            input_grad_ref[rows, :] = (v["d_residual"][rows, :] + back).astype(BF)

        plan.run(grid, order, middle + tiles * TILE_US + 6.0, 1e9)

        def end(z):
            for job in jobs:
                job.finish(z)

        at_each_line(grid, end)
        at_each_line(side, side_job.finish)

    dma = pltpu.SemaphoreType.DMA
    values = [arrays[name] for name in names]
    out = pl.pallas_call(
        kernel,
        out_shape=[
            jax.ShapeDtypeStruct((columns, share), BF),
            jax.ShapeDtypeStruct((columns, inner + 2 * head - share), BF),
            jax.ShapeDtypeStruct(d_own.shape, BF),
            jax.ShapeDtypeStruct((8, columns), F32),
            jax.ShapeDtypeStruct((8, head), F32),
            jax.ShapeDtypeStruct((inner, split[0]), BF),
            jax.ShapeDtypeStruct((inner, split[1]), BF),
        ],
        in_specs=[hbm()] * (len(names) + 1),
        out_specs=[vmem()] * 5 + [hbm()] * 2,
        scratch_shapes=[pltpu.VMEM(a.shape, a.dtype) for a in values]
        + [
            pltpu.VMEM((tokens, columns), BF),
            pltpu.VMEM((tokens, inner), BF),
            pltpu.VMEM((tokens, tokens), F32),
            pltpu.VMEM((tokens, head), F32),
            pltpu.VMEM((tokens, head), F32),
            pltpu.VMEM((tokens, inner + 2 * head), BF),
            pltpu.VMEM(d_own.shape, F32),
            pltpu.VMEM((inner, split[0]), BF),
            pltpu.VMEM((inner, split[1]), BF),
        ]
        + Reduce.scratch(grid, inner, split[0], BF, *kinds[0])
        + Reduce.scratch(grid, inner, split[1], BF, *kinds[1])
        + [pltpu.VMEM((tokens, columns), BF)]
        + Scatter.buffers(side, d_own.shape[0], columns, BF)
        + [dma((len(names),)), dma((1,))]
        + Gather.sems(side, 2)
        + Scatter.sems(side, 2),
        compiler_params=params(number),
        name="attention_backward",
    )(*values, d_own)
    first, second, input_grad, norm_gain, gains, *out_sums = out
    out_sum = jnp.concatenate(out_sums, axis=1)
    return (first, second), input_grad, norm_gain[0], gains[0], gains[1], out_sum


def rope_tables(positions, head_size):
    half_size = head_size // 2
    frequency = THETA ** (-2.0 * jnp.arange(half_size, dtype=F32) / head_size)
    angles = positions.astype(F32)[:, None] * frequency[None, :]
    return (jnp.cos(angles), jnp.sin(angles))


def doc_positions(doc_ids):
    row_index = jnp.arange(doc_ids.shape[0], dtype=jnp.int32)
    doc_starts = jnp.concatenate([jnp.ones((1,), jnp.bool_), doc_ids[1:] != doc_ids[:-1]])
    first_row = lax.cummax(jnp.where(doc_starts, row_index, 0), axis=0)
    return row_index - first_row


def from_near(rows, count):
    return lax.ppermute(rows, "shard", [(s, s + 1 - 2 * (s % 2)) for s in range(count)])


def from_far(rows, count):
    return lax.ppermute(rows, "shard", [(s, (s + 2) % count) for s in range(count)])


def local(
    layer_input,
    doc_ids,
    routes,
    norm1_gain,
    query_weight,
    key_matrix,
    value_matrix,
    query_norm_gain,
    key_norm_gain,
    out_weight,
    norm2_gain,
    router_weight,
    gate_weight,
    up_weight,
    down_weight,
    cotangent,
):
    tokens_here, model_width = layer_input.shape
    head_size = query_norm_gain.shape[0]
    heads_here = query_weight.shape[1] // head_size
    experts_all = router_weight.shape[1]
    local_experts, _, hidden_here = gate_weight.shape
    expert_peers = lax.axis_size("expert")
    shard_count = lax.axis_size("shard")
    rows_here = tokens_here // shard_count
    shard_index = lax.axis_index("shard")
    expert_index = lax.axis_index("expert")
    hidden_all = shard_count * local_experts * hidden_here

    def own(rows):
        return lax.dynamic_slice_in_dim(rows, shard_index * rows_here, rows_here, axis=0)

    def gather_weight(weight):
        return lax.all_gather(weight, "shard", axis=0).reshape(hidden_all, model_width)

    fused = expert_peers * rows_here <= VMEM_ROWS
    cot_own = own(cotangent)
    cot_all = lax.all_gather(cot_own, "expert", axis=0, tiled=True)
    routes_own = own(routes)
    experts = jnp.arange(experts_all, dtype=jnp.int32)
    chosen_own = jnp.any(routes_own[:, :, None] == experts[None, None, :], axis=1)
    gate_weight = jnp.swapaxes(gate_weight, 1, 2)
    up_weight = jnp.swapaxes(up_weight, 1, 2)
    if fused:
        gate_far = from_far(gate_weight, shard_count)
        gate_near = from_near(gate_weight, shard_count)
    else:
        down_all = gather_weight(down_weight)
        gate_all = gather_weight(gate_weight)
        up_all = gather_weight(up_weight)

    positions = doc_positions(doc_ids)
    cosine_table, sine_values = rope_tables(positions, head_size)
    inner = heads_here * head_size
    shared = dict(
        cosine=jnp.concatenate([cosine_table, cosine_table], axis=1),
        sine=jnp.concatenate([-sine_values, sine_values], axis=1),
        query_gain=query_norm_gain[None, :],
        key_gain=key_norm_gain[None, :],
        doc_col=doc_ids[:, None],
        doc_row=doc_ids[None, :],
        query_weight=query_weight,
        key_weight=key_matrix,
        value_weight=value_matrix,
        norm_gain=norm1_gain[None, :],
    )
    forward = dict(
        rows=layer_input, norm_two_gain=norm2_gain[None, :], **shared, out_weight=out_weight
    )
    normed_one, query_lin, key_lin, query, key, value, mixed, log_total, residual, normed_two = (
        attention_forward(forward, heads_here, 1)
    )
    if fused:
        gate_far, residual, normed_two = lax.optimization_barrier(
            (gate_far, residual, normed_two)
        )

    if fused:
        up_late, down_late, normed_two = lax.optimization_barrier(
            (up_weight, down_weight, normed_two)
        )
        up_far, down_far = from_far(up_late, shard_count), from_far(down_late, shard_count)
        up_near, down_near = from_near(up_late, shard_count), from_near(down_late, shard_count)
    _, inverse_two = rms_forward(residual, norm2_gain)
    normed_all, chosen_all = gather_rows(
        [normed_two, chosen_own.T.astype(F32)], [], 2, (2, 1)
    )
    if fused:
        up_far, down_far, normed_all = lax.optimization_barrier((up_far, down_far, normed_all))
        weights_rel = []
        for own_one, near, far in (
            (gate_weight, gate_near, gate_far),
            (up_weight, up_near, up_far),
            (down_weight, down_near, down_far),
        ):
            weights_rel += [own_one, near, far, from_near(far, shard_count)]
    chosen_all = chosen_all.reshape(expert_peers, experts_all, rows_here).transpose(0, 2, 1)
    chosen_all = chosen_all.reshape(expert_peers * rows_here, experts_all) > 0.5

    def gate_table(rows, chosen):
        logits = jnp.where(chosen, dot(rows, router_weight), -jnp.inf)
        top = jnp.max(logits, axis=-1, keepdims=True)
        powers = jnp.exp(logits - top)
        return powers / jnp.sum(powers, axis=-1, keepdims=True)

    gates_all = gate_table(normed_all, chosen_all)
    gates_here = lax.dynamic_slice_in_dim(
        gates_all, expert_index * local_experts, local_experts, axis=1
    )
    if fused:
        summed, out_part, gate_part, up_part, down_part = expert_rows(
            normed_all, cot_all, gates_here, weights_rel, shard_count, 3
        )
        d_rows_own = summed[:, :model_width]
        d_gates_own = (
            summed[:, model_width : model_width + experts_all]
            + summed[:, model_width + experts_all : model_width + 2 * experts_all]
        )
    else:
        column_expert = (jnp.arange(hidden_all, dtype=jnp.int32) // hidden_here) % local_experts
        gate_columns = jnp.zeros((1, 1), F32)
        for j in range(local_experts):
            gate_columns = jnp.where(column_expert[None, :] == j, gates_here[:, j : j + 1], gate_columns)

        d_act_raw = dot_nt(cot_all, down_all)
        gate_pre = dot_nt(normed_all, gate_all)
        up_pre = dot_nt(normed_all, up_all)
        sig = jax.nn.sigmoid(gate_pre)
        silu = gate_pre * sig
        act = silu * up_pre
        act_gated = (act * gate_columns).astype(BF)
        d_act = d_act_raw * gate_columns
        d_gate_low = (d_act * up_pre * sig * (1.0 + gate_pre * (1.0 - sig))).astype(BF)
        d_up_low = (d_act * silu).astype(BF)
        act_back = act * d_act_raw
        d_gates_here = jnp.stack(
            [
                jnp.sum(jnp.where(column_expert[None, :] == j, act_back, 0.0), axis=1)
                for j in range(local_experts)
            ],
            axis=-1,
        )
        d_rows = dot(d_gate_low, gate_all) + dot(d_up_low, up_all)
        d_rows_own = scatter_rows(d_rows.astype(BF), "expert", 3, 2)
        out_part = dot(act_gated, down_all).astype(BF)

        def split(grad):
            return grad.astype(BF).reshape(shard_count, local_experts, hidden_here, model_width)

        gate_part = split(dot_tn(d_gate_low, normed_all))
        up_part = split(dot_tn(d_up_low, normed_all))
        down_part = split(dot_tn(act_gated, cot_all))

        d_gates_own = lax.all_to_all(
            d_gates_here.reshape(expert_peers, rows_here, local_experts),
            "expert",
            split_axis=0,
            concat_axis=0,
            tiled=True,
        )
        d_gates_own = jnp.swapaxes(d_gates_own, 0, 1).reshape(rows_here, experts_all)
    out_own = lax.psum_scatter(out_part, "expert", scatter_dimension=0, tiled=True)
    def scatter_grad(grad):
        return lax.psum_scatter(grad, "shard", scatter_dimension=0, tiled=False)

    gate_grad = jnp.swapaxes(scatter_grad(gate_part).astype(F32), 1, 2)
    up_grad = jnp.swapaxes(scatter_grad(up_part).astype(F32), 1, 2)

    gates_own = gate_table(normed_two, chosen_own)
    d_logits = gates_own * (
        d_gates_own - jnp.sum(gates_own * d_gates_own, axis=-1, keepdims=True)
    )
    d_logits_low = d_logits.astype(BF)
    router_grad = dot_tn(normed_two, d_logits_low)
    d_normed_two = d_rows_own + dot_nt(d_logits_low, router_weight)
    norm2_grad = jnp.sum(d_normed_two * residual * inverse_two, axis=0)
    d_residual = cot_own.astype(F32) + rms_backward(
        residual, inverse_two, norm2_gain, d_normed_two
    )
    backward = dict(
        mixed=mixed,
        query=query,
        key=key,
        value=value,
        query_lin=query_lin,
        key_lin=key_lin,
        log_total=log_total,
        out_weight=out_weight,
        normed=normed_one,
        input_own=own(layer_input),
        d_residual=d_residual,
        **shared,
    )
    line_grads, input_grad_own, norm1_grad, d_query_gain, d_key_gain, out_sum = (
        attention_backward(backward, d_residual.astype(BF), heads_here, 4)
    )
    share = share_of(inner + 2 * head_size)
    out_own, _ = lax.optimization_barrier((out_own, norm1_grad))
    layer_out_own = (residual + out_own).astype(BF)

    flat = jnp.concatenate(
        [router_grad.T.reshape(-1), norm2_grad, norm1_grad, d_query_gain, d_key_gain]
    )
    small_rows = 8 * expert_peers
    small_columns = -(-flat.shape[0] // (128 * small_rows)) * 128
    small = jnp.pad(flat, (0, small_rows * small_columns - flat.shape[0]))
    (line_first, line_second, small), (input_grad, layer_out), down_sum = sum_and_gather(
        *line_grads,
        small.reshape(small_rows, small_columns),
        (input_grad_own, layer_out_own),
        down_part.reshape(hidden_all, model_width),
        5,
    )
    down_grad = down_sum.reshape(local_experts, hidden_here, model_width)
    query_cols = inner - share
    query_sum = jnp.concatenate([line_first, line_second[:, :query_cols]], axis=1)
    key_sum = line_second[:, query_cols : query_cols + head_size]
    value_sum = line_second[:, query_cols + head_size :]
    small = small.reshape(-1)
    bounds = [experts_all * model_width, model_width, model_width, head_size, head_size]
    taken = []
    at = 0
    for bound in bounds:
        taken.append(small[at : at + bound])
        at += bound
    router_sum, norm2_sum, norm1_sum, query_gain_sum, key_gain_sum = taken
    router_sum = router_sum.reshape(experts_all, model_width).T
    return (
        layer_out,
        input_grad,
        norm1_sum,
        query_sum.astype(F32),
        key_sum.astype(F32),
        value_sum.astype(F32),
        query_gain_sum,
        key_gain_sum,
        out_sum.astype(F32),
        norm2_sum,
        router_sum,
        gate_grad,
        up_grad,
        down_grad,
    )


def solution(mesh):
    return jax.shard_map(
        local,
        mesh=mesh,
        in_specs=(
            P("expert", None),
            P("expert"),
            P("expert", None),
            P(),
            P(None, "shard"),
            P(None, "shard"),
            P(None, "shard"),
            P(),
            P(),
            P("shard", None),
            P(),
            P(),
            P("expert", None, "shard"),
            P("expert", None, "shard"),
            P("expert", "shard", None),
            P("expert", None),
        ),
        out_specs=(
            P("expert", None),
            P("expert", None),
            P(),
            P(None, "shard"),
            P(None, "shard"),
            P(None, "shard"),
            P(),
            P(),
            P("shard", None),
            P(),
            P(),
            P("expert", None, "shard"),
            P("expert", None, "shard"),
            P("expert", "shard", None),
        ),
        check_vma=False,
    )
```

```python
import jax
import jax.numpy as jnp
from jax import lax
from jax.experimental import pallas as pl
from jax.experimental.pallas import tpu as pltpu
from jax.sharding import PartitionSpec as P

EPS = 1e-06
THETA = 1000000.0
BF = jnp.bfloat16
F32 = jnp.float32
MESH = pl.DeviceIdType.MESH
VMEM_ROWS = 1024


def dot(a, b):
    return jnp.dot(a, b, preferred_element_type=F32)


def dot_nt(a, b):
    return lax.dot_general(a, b, (((1,), (1,)), ((), ())), preferred_element_type=F32)


def dot_tn(a, b):
    return lax.dot_general(a, b, (((0,), (0,)), ((), ())), preferred_element_type=F32)


LINK_BYTES_PER_US = 1e5


def grid_of(axis):
    size = lax.axis_size(axis)
    lines = 4 if axis == "expert" else 2
    return axis, lines, size // lines, size // lines


def line_of(grid):
    return grid[0], grid[1], 1, grid[3]


def cross_of(grid):
    return grid[0], 1, grid[2], grid[3]


def position(grid):
    axis, lines, width, stride = grid
    me = lax.axis_index(axis)
    return me, me // stride if lines > 1 else 0, me % width if width > 1 else 0


def at_each_line(grid, act):
    _, z, _ = position(grid)
    for at in range(grid[1]):

        @pl.when(z == at)
        def _():
            act(at)


def greet(grids):
    barrier = pltpu.get_barrier_semaphore()
    count = 0
    for grid in grids:
        axis, lines, width, stride = grid
        me, z, b = position(grid)

        def signal(peer):
            pl.semaphore_signal(barrier, inc=1, device_id={axis: peer}, device_id_type=MESH)

        @pl.when(z < lines - 1)
        def _():
            signal(me + stride)

        @pl.when(z > 0)
        def _():
            signal(me - stride)

        for o in range(1, width):
            signal(me - b + (b + o) % width)
        count = count + width - 1
        count = count + (z < lines - 1).astype(jnp.int32) + (z > 0).astype(jnp.int32)
    pl.semaphore_wait(barrier, count)


def slice_of(ref, start, rows):
    if not isinstance(start, int):
        start = pl.multiple_of(start, rows)
    return ref.at[pl.ds(start, rows)]


class Gather:
    def __init__(self, grid, source, out, pieces, sems):
        self.axis, self.lines, self.width, self.stride = grid
        self.source, self.out, self.pieces = source, out, pieces
        self.rows_all = source.shape[0]
        self.rows = self.rows_all // pieces
        self.send_r, self.send_l, self.send_x, self.recv = sems
        self.me, _, self.b = position(grid)
        self.bytes = self.rows * source.shape[1] * jnp.dtype(source.dtype).itemsize

    @staticmethod
    def sems(grid, pieces):
        _, lines, width, _ = grid
        dma = pltpu.SemaphoreType.DMA
        return [
            dma((lines, pieces)),
            dma((lines, pieces)),
            dma((max(1, width - 1), lines, pieces)),
            dma((lines * width, pieces)),
        ]

    def copy(self, slot, p, sem, peer, own=False):
        place = slice_of(self.out, slot * self.rows_all + p * self.rows, self.rows)
        source = slice_of(self.source, p * self.rows, self.rows) if own else place
        return pltpu.make_async_remote_copy(
            src_ref=source,
            dst_ref=place,
            send_sem=sem,
            recv_sem=self.recv.at[slot, p],
            device_id={self.axis: peer},
            device_id_type=MESH,
        )

    def sends(self, z, origin, p):
        slot = origin * self.width + self.b
        own = origin == z
        copies = []
        if origin <= z and z < self.lines - 1:
            sem = self.send_r.at[z - origin, p]
            copies.append(self.copy(slot, p, sem, self.me + self.stride, own))
        if origin >= z and z > 0:
            sem = self.send_l.at[origin - z, p]
            copies.append(self.copy(slot, p, sem, self.me - self.stride, own))
        for o in range(1, self.width):
            peer = self.me - self.b + (self.b + o) % self.width
            copies.append(self.copy(slot, p, self.send_x.at[o - 1, origin, p], peer, own))
        return copies

    def start(self, z, p):
        for c in self.sends(z, z, p):
            c.start()

    def arrived(self, slot, p):
        self.copy(slot, p, self.send_r.at[0, p], self.me).wait_recv()

    def forward(self, z, origin, p):
        self.arrived(origin * self.width + self.b, p)
        for c in self.sends(z, origin, p):
            c.start()

    def arrived_across(self, z, p):
        for o in range(1, self.width):
            self.arrived(z * self.width + (self.b + o) % self.width, p)

    def wait_sends(self, z):
        for p in range(self.pieces):
            for origin in range(self.lines):
                for c in self.sends(z, origin, p):
                    c.wait_send()

    def finish(self, z):
        for p in range(self.pieces):
            for line in range(self.lines):
                self.arrived_across(line, p)
        self.wait_sends(z)

    def own_slot(self, z):
        return slice_of(self.out, (z * self.width + self.b) * self.rows_all, self.rows_all)


class Scatter:
    def __init__(self, grid, parts, buffers, pieces, sems):
        self.axis, self.lines, self.width, self.stride = grid
        self.parts, self.pieces = parts, pieces
        self.cross, self.right, self.left = buffers
        self.rows_all = parts.shape[0] // (self.lines * self.width)
        self.rows = self.rows_all // pieces
        self.cross_send, self.cross_recv, self.r_send, self.r_recv, self.l_send, self.l_recv = sems
        self.me, _, self.b = position(grid)
        self.bytes = self.rows * parts.shape[1] * jnp.dtype(parts.dtype).itemsize

    @staticmethod
    def sems(grid, pieces):
        _, lines, width, _ = grid
        dma = pltpu.SemaphoreType.DMA
        across = (max(1, width - 1), lines, pieces)
        return [dma(across), dma(across)] + [dma((lines, pieces)) for _ in range(4)]

    @staticmethod
    def buffers(grid, rows_all, columns, kind):
        _, lines, width, _ = grid
        line = pltpu.VMEM((lines * rows_all if lines > 1 else 16, columns), kind)
        return [pltpu.VMEM((max(1, width - 1) * lines * rows_all, columns), kind), line, line]

    def start_of(self, slot, p):
        return slot * self.rows_all + p * self.rows

    def cross_copy(self, o, k, p):
        peer = (self.b + o) % self.width
        return pltpu.make_async_remote_copy(
            src_ref=slice_of(self.parts, self.start_of(k * self.width + peer, p), self.rows),
            dst_ref=slice_of(self.cross, self.start_of((o - 1) * self.lines + k, p), self.rows),
            send_sem=self.cross_send.at[o - 1, k, p],
            recv_sem=self.cross_recv.at[o - 1, k, p],
            device_id={self.axis: self.me - self.b + peer},
            device_id_type=MESH,
        )

    def line_copy(self, k, p, rightward):
        into = self.right if rightward else self.left
        at = self.start_of(k, p)
        return pltpu.make_async_remote_copy(
            src_ref=slice_of(self.cross, at, self.rows),
            dst_ref=slice_of(into, at, self.rows),
            send_sem=(self.r_send if rightward else self.l_send).at[k, p],
            recv_sem=(self.r_recv if rightward else self.l_recv).at[k, p],
            device_id={self.axis: self.me + self.stride if rightward else self.me - self.stride},
            device_id_type=MESH,
        )

    def start_one(self, k, p):
        for o in range(1, self.width):
            self.cross_copy(o, k, p).start()

    def add(self, k, p, sources, target):
        block = min(16, self.rows)
        own = self.start_of(k * self.width + self.b, p)

        @pl.loop(0, self.rows // block)
        def _(i):
            def rows_at(start):
                return pl.ds(pl.multiple_of(start + i * block, block), block)

            total = self.parts[rows_at(own), :].astype(F32)
            for o in range(self.width - 1):
                at = rows_at(self.start_of(o * self.lines + k, p))
                total = total + self.cross[at, :].astype(F32)
            for source in sources:
                total = total + source[rows_at(self.start_of(k, p)), :].astype(F32)
            target(rows_at(p * self.rows), total)

    def sources(self, z, k, p):
        found = []
        if k >= z and z > 0:
            self.line_copy(k, p, True).wait_recv()
            found.append(self.right)
        if k <= z and z < self.lines - 1:
            self.line_copy(k, p, False).wait_recv()
            found.append(self.left)
        return found

    def reduce_one(self, z, k, p):
        for o in range(1, self.width):
            self.cross_copy(o, k, p).wait_recv()

        def put(at, total):
            offset = pl.multiple_of(at.start + k * self.rows_all, at.size)
            self.cross[pl.ds(offset, at.size), :] = total.astype(self.cross.dtype)

        self.add(k, p, self.sources(z, k, p), put)
        self.line_copy(k, p, k > z).start()

    def total(self, z, p, target):
        for o in range(1, self.width):
            self.cross_copy(o, z, p).wait_recv()
        self.add(z, p, self.sources(z, z, p), target)

    def finish(self, z):
        for p in range(self.pieces):
            for k in range(self.lines):
                for o in range(1, self.width):
                    self.cross_copy(o, k, p).wait_send()
                if k != z:
                    self.line_copy(k, p, k > z).wait_send()


def targets(lines, z):
    others = sorted((k for k in range(lines) if k != z), key=lambda k: (-abs(k - z), -k))
    return others + [z]


class Plan:
    def __init__(self, lines):
        self.lines = lines
        self.steps = [[] for _ in range(lines)]
        self.jobs = 0

    def job(self):
        self.jobs += 1
        return self.jobs

    def add(self, z, waits, act, sends, begin=0.0):
        self.steps[z].append((begin, waits, act, sends))

    def order(self):
        arrived = [dict() for _ in range(self.lines)]
        free = {}
        clock = [0.0] * self.lines
        left = [list(enumerate(steps)) for steps in self.steps]
        result = [[] for _ in range(self.lines)]
        while any(left):
            best = None
            for z in range(self.lines):
                for i, (begin, waits, act, sends) in left[z]:
                    if all(key in arrived[z] for key in waits):
                        ready = max([begin] + [arrived[z][key] for key in waits])
                        if best is None or (max(ready, clock[z]), ready, z, i) < best[0]:
                            best = ((max(ready, clock[z]), ready, z, i), act, sends)
            (now, _, z, i), act, sends = best
            left[z] = [entry for entry in left[z] if entry[0] != i]
            result[z].append((now, act))
            clock[z] = now + 0.7
            for link, time, to, key in sends:
                start = max(now + 1.0, free.get((z, link), 0.0))
                free[z, link] = start + time
                arrived[to][key] = start + time + 1.0
        return result

    def run(self, grid, result, begin, end):
        def act(z):
            for now, step in result[z]:
                if begin <= now < end:
                    step()

        at_each_line(grid, act)


    def run_step(self, grid, result, index, begin, each, steps, early=False):
        _, z, _ = position(grid)
        for at in range(self.lines):
            for now, step in result[at]:
                due = int((now - begin) // each)
                if early:
                    due = max(0, due)
                if 0 <= due < steps:

                    @pl.when(jnp.logical_and(z == at, index == due))
                    def _():
                        step()


def plan_scatter(plan, scatter, p, put, then=None, begin=0.0, start=True):
    n = plan.job()
    lines, width = scatter.lines, scatter.width
    time = 2 * scatter.bytes / LINK_BYTES_PER_US
    for z in range(lines):
        ready = begin if isinstance(begin, (int, float)) else None
        for i, k in enumerate(targets(lines, z)):
            first = ready if ready is not None else begin[i]
            if width > 1:
                plan.add(
                    z,
                    [],
                    (lambda k=k: scatter.start_one(k, p)) if start else (lambda: None),
                    [("x", time * (width - 1), z, (n, "c", k))],
                    first,
                )
            waits = [(n, "c", k)] if width > 1 else []
            if k >= z and z > 0:
                waits.append((n, "r", k))
            if k <= z and z < lines - 1:
                waits.append((n, "l", k))
            if k > z:
                sends = [("r", time, z + 1, (n, "r", k))]
            elif k < z:
                sends = [("l", time, z - 1, (n, "l", k))]
            else:
                follow, sends = then(z) if then else ((lambda: None), [])

                def last(z=z, follow=follow):
                    scatter.total(z, p, put)
                    follow()

                plan.add(z, waits, last, sends, first)
                continue
            plan.add(z, waits, lambda z=z, k=k: scatter.reduce_one(z, k, p), sends, first)


def gather_sends(gather, n, time, z, origin):
    sends = []
    if origin <= z and z < gather.lines - 1:
        sends.append(("r", time, z + 1, (n, "g", origin)))
    if origin >= z and z > 0:
        sends.append(("l", time, z - 1, (n, "g", origin)))
    if gather.width > 1:
        sends.append(("x", time * (gather.width - 1), z, (n, "gx", origin)))
    return sends


def plan_gather(plan, gather, p, begin=None):
    n = plan.job()
    time = 2 * gather.bytes / LINK_BYTES_PER_US
    for z in range(gather.lines):
        for origin in range(gather.lines):
            if origin != z:
                plan.add(
                    z,
                    [(n, "g", origin)],
                    lambda z=z, origin=origin: gather.forward(z, origin, p),
                    gather_sends(gather, n, time, z, origin),
                )

    def then(z):
        return (lambda: gather.start(z, p)), gather_sends(gather, n, time, z, z)

    if begin is not None:
        for z in range(gather.lines):
            act, sends = then(z)
            plan.add(z, [], act, sends, begin)
    return then


class Reduce:
    def __init__(self, grid, parts, out, scratch, pieces, line_first):
        self.grid, self.parts, self.out = grid, parts, out
        self.line_first = line_first
        self.pieces = pieces
        take = Taker(scratch)
        self.sums = take.one()
        if line_first:
            self.pair_sums, self.pair_all = take.take(2)
            self.first = Scatter(line_of(grid), parts, take.take(3), 1, take.take(6))
            self.second = Scatter(cross_of(grid), self.pair_sums, take.take(3), 1, take.take(6))
            self.third = Gather(cross_of(grid), self.sums, self.pair_all, 1, take.take(4))
            self.fourth = Gather(line_of(grid), self.pair_all, out, 1, take.take(4))
        else:
            self.scatter = Scatter(grid, parts, take.take(3), pieces, take.take(6))
            self.gather = Gather(grid, self.sums, out, pieces, take.take(4))
        self.own_sem = take.one()

    @staticmethod
    def scratch(grid, rows, columns, kind, pieces, line_first):
        _, lines, width, _ = grid
        count = rows // (lines * width)
        shapes = [pltpu.VMEM((count, columns), kind)]
        if line_first:
            line, cross = line_of(grid), cross_of(grid)
            shapes += [pltpu.VMEM((width * count, columns), kind)] * 2
            shapes += Scatter.buffers(line, width * count, columns, kind) + Scatter.sems(line, 1)
            shapes += Scatter.buffers(cross, count, columns, kind) + Scatter.sems(cross, 1)
            shapes += Gather.sems(cross, 1) + Gather.sems(line, 1)
        else:
            shapes += Scatter.buffers(grid, count, columns, kind) + Scatter.sems(grid, pieces)
            shapes += Gather.sems(grid, pieces)
        return shapes + [pltpu.SemaphoreType.DMA]

    @staticmethod
    def refs(line_first):
        return 1 + (2 + 9 + 9 + 8 if line_first else 9 + 4) + 1

    def put(self, at, total):
        self.sums[at, :] = total.astype(self.sums.dtype)

    def put_pair(self, at, total):
        self.pair_sums[at, :] = total.astype(self.pair_sums.dtype)

    def own_copy(self, z):
        if self.line_first:
            return pltpu.make_async_copy(self.pair_all, self.fourth.own_slot(z), self.own_sem)
        return pltpu.make_async_copy(self.sums, self.gather.own_slot(z), self.own_sem)

    def start_one(self, k, p):
        if not self.line_first:
            self.scatter.start_one(k, p)

    def plan(self, plan, begin=0.0, start=True):
        if not self.line_first:
            for p in range(self.pieces):
                then = plan_gather(plan, self.gather, p)
                plan_scatter(plan, self.scatter, p, self.put, then, begin, start)
            return
        n = plan.job()
        time = 2 * self.second.bytes / LINK_BYTES_PER_US * (self.grid[2] - 1)
        along = plan_gather(plan, self.fourth, 0)

        def cross(z):
            return (lambda: self.second.start_one(0, 0)), [("x", time, z, (n, "c"))]

        plan_scatter(plan, self.first, 0, self.put_pair, cross, begin)
        for z in range(self.grid[1]):

            def across(z=z):
                self.second.total(0, 0, self.put)
                self.third.start(0, 0)
                at = pl.multiple_of(self.third.b * self.third.rows_all, self.third.rows_all)
                self.pair_all[pl.ds(at, self.third.rows_all), :] = self.sums[...]

            plan.add(z, [(n, "c")], across, [("x", time, z, (n, "x"))])
            follow, sends = along(z)

            def spread(follow=follow):
                self.third.arrived_across(0, 0)
                follow()

            plan.add(z, [(n, "x")], spread, sends)

    def finish(self, z):
        self.own_copy(z).start()
        if self.line_first:
            self.first.finish(z)
            self.second.finish(0)
            self.third.wait_sends(0)
            self.fourth.finish(z)
        else:
            self.scatter.finish(z)
            self.gather.finish(z)
        self.own_copy(z).wait()


def hbm():
    return pl.BlockSpec(memory_space=pl.ANY)


def vmem():
    return pl.BlockSpec(memory_space=pltpu.VMEM)


def params(number, mib=56):
    return pltpu.CompilerParams(
        collective_id=number, has_side_effects=True, vmem_limit_bytes=mib * 1024 * 1024
    )


class Taker:
    def __init__(self, refs):
        self.refs = list(refs)

    def take(self, count):
        taken = self.refs[:count]
        del self.refs[:count]
        return taken

    def one(self):
        return self.take(1)[0]


ALWAYS = (0.0, 1e9)


def gather_rows(arrays, side_arrays, number, pieces):
    grid, side = grid_of("expert"), grid_of("shard")
    values = list(arrays) + list(side_arrays)
    grids = [grid] * len(arrays) + [side] * len(side_arrays)
    n = len(values)

    def kernel(*refs):
        take = Taker(refs)
        ins, outs, own_sems = take.take(n), take.take(n), take.one()
        jobs = [Gather(grids[i], ins[i], outs[i], pieces[i], take.take(4)) for i in range(n)]

        def own(i, z):
            return pltpu.make_async_copy(ins[i], jobs[i].own_slot(z), own_sems.at[i])

        def each(i, act):
            at_each_line(grids[i], act)

        for i in range(n):
            each(i, lambda z, i=i: own(i, z).start())
        greet([grid] + ([side] if side_arrays else []))
        plan = Plan(grid[1])
        for i in range(len(arrays)):
            for p in range(pieces[i]):
                plan_gather(plan, jobs[i], p, 0.0)
        order = plan.order()
        plan.run(grid, order, 0.0, 1.0)
        late = 0.0 if not side_arrays else 1.0
        for i in range(len(arrays), n):
            for p in range(pieces[i]):
                each(i, lambda z, i=i, p=p: jobs[i].start(z, p))
        if side_arrays:
            edge = 2 * jobs[-1].bytes / LINK_BYTES_PER_US + 4.0
            begin = late
            for p in range(pieces[-1]):
                plan.run(grid, order, begin, edge * (p + 1))
                begin = edge * (p + 1)
                for i in range(len(arrays), n):

                    def forward(z, i=i, p=p):
                        for origin in range(grids[i][1]):
                            if origin != z:
                                jobs[i].forward(z, origin, p)

                    each(i, forward)
            plan.run(grid, order, begin, 1e9)
        else:
            plan.run(grid, order, 1.0, 1e9)
        for i in range(n):
            each(i, lambda z, i=i: jobs[i].finish(z))
            each(i, lambda z, i=i: own(i, z).wait())

    scratch = [pltpu.SemaphoreType.DMA((n,))]
    for g, p in zip(grids, pieces):
        scratch += Gather.sems(g, p)
    return pl.pallas_call(
        kernel,
        out_shape=[
            jax.ShapeDtypeStruct((g[1] * g[2] * a.shape[0], a.shape[1]), a.dtype)
            for a, g in zip(values, grids)
        ],
        in_specs=[hbm()] * n,
        out_specs=[hbm()] * n,
        scratch_shapes=scratch,
        compiler_params=params(number),
        name="gather_rows",
    )(*values)


def scatter_rows(parts, axis, number, pieces):
    grid = grid_of(axis)
    columns = parts.shape[1]
    count = parts.shape[0] // (grid[1] * grid[2])

    def kernel(parts_ref, out_ref, cross, right, left, *sems):
        greet([grid])
        job = Scatter(grid, parts_ref, (cross, right, left), pieces, sems)

        def put(at, total):
            out_ref[at, :] = total

        plan = Plan(grid[1])
        for p in range(pieces):
            plan_scatter(plan, job, p, put)
        plan.run(grid, plan.order(), *ALWAYS)
        at_each_line(grid, job.finish)

    return pl.pallas_call(
        kernel,
        out_shape=jax.ShapeDtypeStruct((count, columns), F32),
        in_specs=[vmem()],
        out_specs=vmem(),
        scratch_shapes=Scatter.buffers(grid, count, columns, parts.dtype)
        + Scatter.sems(grid, pieces),
        compiler_params=params(number),
        name="scatter_" + axis,
    )(parts)


def sum_and_gather(across_first, line_first, small, rows, spread, number):
    grid, side = grid_of("expert"), grid_of("shard")
    size = grid[1] * grid[2]
    shards = side[1] * side[2]
    values = [across_first, line_first, small]
    moved = [small] + list(rows)
    m = len(moved)
    kinds = [(2, False), (1, True), (1, False)]

    def kernel(*refs):
        take = Taker(refs)
        first_ref, second_ref, spread_ref = take.take(3)
        side_ins = take.take(m)
        outs, rows_outs, spread_out = take.take(3), take.take(m - 1), take.one()
        small_all, small_parts, own_sems = take.take(3)
        ins = [first_ref, second_ref, small_parts]
        jobs = [
            Reduce(grid, ins[i], outs[i], take.take(Reduce.refs(kinds[i][1])), *kinds[i])
            for i in range(3)
        ]
        spread_job = Scatter(side, spread_ref, take.take(3), 1, take.take(6))
        side_outs = [small_all] + rows_outs
        side_jobs = [Gather(side, side_ins[i], side_outs[i], 1, take.take(4)) for i in range(m)]

        def own(z, i):
            return pltpu.make_async_copy(side_ins[i], side_jobs[i].own_slot(z), own_sems.at[i])

        def begin_side(z):
            for i in range(m):
                own(z, i).start()

        at_each_line(side, begin_side)
        greet([grid, side])
        edges = [0.0, 6.0, 16.0, 28.0, 55.0]
        plan = Plan(grid[1])
        jobs[1].plan(plan)
        jobs[0].plan(plan)
        jobs[2].plan(plan, edges[3])
        order = plan.order()
        plan.run(grid, order, 0.0, edges[1])
        at_each_line(side, lambda z: side_jobs[0].start(z, 0))
        plan.run(grid, order, edges[1], edges[2])

        def forward(z, chosen):
            for origin in range(side[1]):
                if origin != z:
                    for job in chosen:
                        job.forward(z, origin, 0)

        def start(z):
            forward(z, side_jobs[:1])
            for job in side_jobs[1:]:
                job.start(z, 0)
            for k in targets(side[1], z):
                spread_job.start_one(k, 0)

        at_each_line(side, start)
        plan.run(grid, order, edges[2], edges[3])

        def end_small(z):
            side_jobs[0].finish(z)
            own(z, 0).wait()

        at_each_line(side, end_small)
        count = small.shape[0]
        total = small_all[pl.ds(0, count), :]
        for s in range(1, shards):
            total = total + small_all[pl.ds(s * count, count), :]
        small_parts[...] = total
        plan.run(grid, order, edges[3], edges[4])

        def spread_on(z):
            for k in targets(side[1], z)[:-1]:
                spread_job.reduce_one(z, k, 0)
            forward(z, side_jobs[1:])

        at_each_line(side, spread_on)
        plan.run(grid, order, edges[4], 1e9)

        def end(z):
            for job in jobs:
                job.finish(z)

        at_each_line(grid, end)

        def put_spread(at, total):
            spread_out[at, :] = total

        def end_rows(z):
            spread_job.total(z, 0, put_spread)
            spread_job.finish(z)
            for i in range(1, m):
                side_jobs[i].finish(z)
                own(z, i).wait()

        at_each_line(side, end_rows)

    scratch = [
        pltpu.VMEM((shards * small.shape[0], small.shape[1]), small.dtype),
        pltpu.VMEM(small.shape, small.dtype),
        pltpu.SemaphoreType.DMA((m,)),
    ]
    for a, kind in zip(values, kinds):
        scratch += Reduce.scratch(grid, a.shape[0], a.shape[1], a.dtype, *kind)
    spread_rows = spread.shape[0] // shards
    scratch += Scatter.buffers(side, spread_rows, spread.shape[1], BF) + Scatter.sems(side, 1)
    for _ in range(m):
        scratch += Gather.sems(side, 1)
    out = pl.pallas_call(
        kernel,
        out_shape=[jax.ShapeDtypeStruct(a.shape, a.dtype) for a in values]
        + [jax.ShapeDtypeStruct((shards * a.shape[0], a.shape[1]), a.dtype) for a in rows]
        + [jax.ShapeDtypeStruct((spread_rows, spread.shape[1]), F32)],
        in_specs=[vmem()] * 3 + [hbm()] * m,
        out_specs=[hbm()] * (2 + m) + [vmem()],
        scratch_shapes=scratch,
        compiler_params=params(number),
        name="sum_and_gather",
    )(across_first, line_first, spread, small, *rows)
    return out[:3], out[3:-1], out[-1]


CHUNK_US = 4.0
PAIR_US = 1.5
HEAD_US = 5.5
TILE_US = 1.5
FORWARD_US = 3.0
EXTRA = 128


def share_of(columns):
    return 4 * columns // 5 // 256 * 256


def expert_rows(normed, cot, chosen, router, gate_rel, up_first, up_rel, down_rel, number):
    grid = grid_of("expert")
    _, lines, width, _ = grid
    size = lines * width
    experts, hidden, columns = gate_rel[0].shape
    shards = len(gate_rel)
    full = shards * hidden
    both = 2 * full
    total_rows = normed.shape[0]
    count = total_rows // size
    pair = width * count
    tile = 256
    half = 512
    wide = 2 * hidden
    extra = EXTRA
    orders = [targets(lines, z) for z in range(lines)]
    out_tiles = columns // tile
    grad_tiles = experts * 3 * full // wide
    out_us, grad_us = 1.3, 2.3

    def kernel(*refs):
        take = Taker(refs)
        normed_hbm, cot_hbm, chosen_hbm, router_ref = take.take(4)
        gate_hbm, up_first_hbm = take.take(shards), take.one()
        up_hbm, down_hbm = take.take(shards), take.take(shards)
        sum_ref, out_hbm = take.take(2)
        grad_hbm = take.take(3)
        normed_v, cot_v, weights, down = take.take(4)
        grads_low, act_low, parts = take.take(3)
        buffers = take.take(3)
        out_stage, grad_stage, d_gates_ref = take.take(3)
        gates_ref, chosen_v = take.take(2)
        load_sems, weight_sems, out_sems, grad_sems = take.take(4)
        job = Scatter(grid, parts, buffers, 1, take.take(6))
        me, z, _ = position(grid)

        def put(at, total):
            sum_ref[at, :] = total

        plan = Plan(lines)
        plan_scatter(
            plan, job, 0, put, None, [(i + 1) * CHUNK_US for i in range(lines)], False
        )
        order = plan.order()
        shard = lax.axis_index("shard")
        near = shard + 1 - 2 * (shard % 2)
        places = [shard, near, (shard + 2) % shards, (near + 2) % shards]

        loads = [
            pltpu.make_async_copy(normed_hbm, normed_v, load_sems.at[0]),
            pltpu.make_async_copy(chosen_hbm, chosen_v, load_sems.at[2]),
            pltpu.make_async_copy(cot_hbm, cot_v, load_sems.at[1]),
        ]
        weight_loads = [[] for _ in range(experts)]
        for j in range(experts):
            for r in range(shards):
                for w, (source, target) in enumerate(
                    (
                        (gate_hbm[r].at[j], weights.at[pl.ds(j * both + r * hidden, hidden)]),
                        (
                            up_hbm[r].at[j - 1]
                            if j
                            else slice_of(up_first_hbm, places[r] * hidden, hidden),
                            weights.at[pl.ds(j * both + full + r * hidden, hidden)],
                        ),
                        (down_hbm[r].at[j], down.at[pl.ds(j * full + r * hidden, hidden)]),
                    )
                ):
                    weight_loads[j].append(
                        pltpu.make_async_copy(source, target, weight_sems.at[j, r, w])
                    )
        for c in loads + weight_loads[0]:
            c.start()
        for j in range(1, experts):
            for c in weight_loads[j]:
                c.start()
        greet([grid])
        for c in loads:
            c.wait()

        lane = lax.broadcasted_iota(jnp.int32, (half, EXTRA), 1)

        @pl.loop(0, total_rows // half)
        def _(m):
            rows = pl.ds(pl.multiple_of(m * half, half), half)
            named = chosen_v[rows, :].astype(F32) > 0.5
            logits = jnp.where(named, dot(normed_v[rows, :], router_ref[...]), -1e30)
            top = jnp.max(logits, axis=-1, keepdims=True)
            powers = jnp.where(named, jnp.exp(logits - top), 0.0)
            probs = powers / jnp.sum(powers, axis=-1, keepdims=True)
            for j in range(experts):
                gates_ref[rows, j : j + 1] = jnp.sum(
                    jnp.where(lane == me * experts + j, probs, 0.0), axis=-1, keepdims=True
                )

        for j in range(experts):
            for c in weight_loads[j]:
                c.wait()

            @pl.loop(0, total_rows // half)
            def _(m):
                rows = pl.ds(pl.multiple_of(m * half, half), half)

                @pl.loop(0, full // tile)
                def _(t):
                    at = t * tile

                    def lines_of(base):
                        return pl.ds(pl.multiple_of(base + at, tile), tile)

                    x = normed_v[rows, :]
                    gate_pre = dot_nt(x, weights[lines_of(j * both), :])
                    up_pre = dot_nt(x, weights[lines_of(j * both + full), :])
                    back = dot_nt(cot_v[rows, :], down[lines_of(j * full), :])
                    probs = gates_ref[rows, j : j + 1]
                    sig = 1.0 / (1.0 + jnp.exp(-gate_pre))
                    silu = gate_pre * sig
                    act = silu * up_pre
                    act_low[rows, lines_of(j * full)] = (act * probs).astype(BF)
                    d_act = back * probs
                    d_gate = d_act * up_pre * (sig * (1.0 + gate_pre * (1.0 - sig)))
                    grads_low[rows, lines_of(j * both)] = d_gate.astype(BF)
                    grads_low[rows, lines_of(j * both + full)] = (d_act * silu).astype(BF)
                    part = jnp.sum(act * back, axis=1, keepdims=True)

                    @pl.when(t == 0)
                    def _():
                        d_gates_ref[rows, j : j + 1] = part

                    @pl.when(t > 0)
                    def _():
                        d_gates_ref[rows, j : j + 1] = d_gates_ref[rows, j : j + 1] + part

        lane = lax.broadcasted_iota(jnp.int32, (count, extra), 1)

        @pl.loop(0, size)
        def _(e):
            rows = pl.ds(pl.multiple_of(e * count, count), count)
            block = jnp.zeros((count, extra), F32)
            for j in range(experts):
                value = d_gates_ref[rows, j : j + 1]
                high = value.astype(BF).astype(F32)
                mine = me * experts + j
                block = jnp.where(lane == mine, high, block)
                block = jnp.where(lane == mine + size * experts, value - high, block)
            parts[rows, columns:] = block.astype(BF)

        @pl.loop(0, lines)
        def _(i):
            k = jnp.int32(0)
            for at in range(lines):
                for step in range(lines):
                    k = jnp.where(jnp.logical_and(z == at, i == step), orders[at][step], k)
            rows = pl.ds(pl.multiple_of(k * pair, pair), pair)

            @pl.loop(0, columns // tile)
            def _(t):
                cols = pl.ds(pl.multiple_of(t * tile, tile), tile)
                value = dot(grads_low[rows, :], weights[:, cols])
                parts[rows, cols] = value.astype(BF)

            job.start_one(k, 0)

        begin = lines * CHUNK_US

        def out_copy(t, slot):
            cols = pl.ds(pl.multiple_of(t * tile, tile), tile)
            return pltpu.make_async_copy(
                out_stage.at[slot], out_hbm.at[:, cols], out_sems.at[slot]
            )

        plan.run(grid, order, -1.0, begin)

        @pl.loop(0, out_tiles)
        def _(t):
            slot = t % 2

            @pl.when(t >= 2)
            def _():
                out_copy(t - 2, slot).wait()

            cols = pl.ds(pl.multiple_of(t * tile, tile), tile)
            out_stage[slot, :, :] = dot(act_low[...], down[:, cols]).astype(BF)
            out_copy(t, slot).start()
            plan.run_step(grid, order, t, begin, out_us, out_tiles)

        begin = begin + out_tiles * out_us

        def grad_copies(kind, j, r, slot):
            copies = []
            for h in range(2):
                place = places[h]
                for step in range(1, shards // 2):
                    place = jnp.where(r == step, places[2 * step + h], place)
                copies.append(
                    pltpu.make_async_copy(
                        grad_stage.at[slot, pl.ds(h * hidden, hidden)],
                        grad_hbm[kind].at[place, j],
                        grad_sems.at[slot, h],
                    )
                )
            return copies

        per = full // wide
        for kind in range(3):

            @pl.loop(0, experts * per)
            def _(i):
                j, r = i // per, i % per
                slot = i % 2
                if kind == 2:
                    low, base, rows_v = act_low, j * full, cot_v
                else:
                    low, base, rows_v = grads_low, j * both + kind * full, normed_v
                lanes = pl.ds(pl.multiple_of(base + r * wide, wide), wide)

                @pl.when(i >= 2)
                def _():
                    for c in grad_copies(kind, (i - 2) // per, (i - 2) % per, slot):
                        c.wait()

                for q in range(2):
                    cols = pl.ds(q * columns // 2, columns // 2)
                    value = dot_tn(low[:, lanes], rows_v[:, cols])
                    grad_stage[slot, :, cols] = value.astype(BF)
                for c in grad_copies(kind, j, r, slot):
                    c.start()
                plan.run_step(grid, order, i, begin, grad_us, experts * per)

            for i in range(max(0, experts * per - 2), experts * per):
                for c in grad_copies(kind, i // per, i % per, i % 2):
                    c.wait()
            begin = begin + experts * per * grad_us

        plan.run(grid, order, begin, 1e9)

        for t in range(max(0, out_tiles - 2), out_tiles):
            out_copy(t, t % 2).wait()
        at_each_line(grid, job.finish)

    dma = pltpu.SemaphoreType.DMA
    weight_shape = jax.ShapeDtypeStruct((shards, experts, hidden, columns), BF)
    return pl.pallas_call(
        kernel,
        out_shape=[
            jax.ShapeDtypeStruct((count, columns + extra), F32),
            jax.ShapeDtypeStruct((total_rows, columns), BF),
            weight_shape,
            weight_shape,
            weight_shape,
        ],
        in_specs=[hbm()] * 3 + [vmem()] + [hbm()] * (3 * shards + 1),
        out_specs=[vmem()] + [hbm()] * 4,
        scratch_shapes=[
            pltpu.VMEM((total_rows, columns), BF),
            pltpu.VMEM((total_rows, columns), BF),
            pltpu.VMEM((experts * both, columns), BF),
            pltpu.VMEM((experts * full, columns), BF),
            pltpu.VMEM((total_rows, experts * both), BF),
            pltpu.VMEM((total_rows, experts * full), BF),
            pltpu.VMEM((total_rows, columns + extra), BF),
        ]
        + Scatter.buffers(grid, count, columns + extra, BF)
        + [
            pltpu.VMEM((2, total_rows, tile), BF),
            pltpu.VMEM((2, wide, columns), BF),
            pltpu.VMEM((total_rows, experts), F32),
            pltpu.VMEM((total_rows, experts), F32),
            pltpu.VMEM((total_rows, EXTRA), BF),
            dma((3,)),
            dma((experts, shards, 3)),
            dma((2,)),
            dma((2, 2)),
        ]
        + Scatter.sems(grid, 1),
        compiler_params=params(number, 63),
        name="expert_rows",
    )(normed, cot, chosen, router, *gate_rel, up_first, *up_rel, *down_rel)


def rms_forward(vector, gain):
    inverse = lax.rsqrt(jnp.mean(vector * vector, axis=-1, keepdims=True) + EPS)
    return vector * inverse * gain, inverse


def rms_backward(vector, inverse, gain, grad):
    scaled = grad * gain
    inner = jnp.mean(scaled * vector, axis=-1, keepdims=True)
    return inverse * scaled - vector * (inverse * inverse * inverse * inner)


def attention_forward(arrays, cot_own, up_own, heads, number):
    grid, side = grid_of("expert"), grid_of("shard")
    size, shards = grid[1] * grid[2], side[1] * side[2]
    names = list(arrays)
    tokens, columns = arrays["rows"].shape
    inner = arrays["query_weight"].shape[1]
    head = inner // heads
    own_rows = tokens // shards
    tile = 256
    scale = head ** (-0.5)
    block = min(256, tokens)

    def kernel(*refs):
        take = Taker(refs)
        hbm_refs = take.take(len(names))
        cot_ref, up_ref = take.take(2)
        normed, query_lin, key_lin, query, key, value, mixed, log_total = take.take(8)
        residual, normed_two = take.take(2)
        cot_all, up_all = take.take(2)
        v = dict(zip(names, take.take(len(names))))
        bias, parts, summed = take.take(3)
        buffers = take.take(3)
        load_sems, own_sems = take.take(2)
        job = Scatter(side, parts, buffers, 2, take.take(6))
        cot_job = Gather(grid, cot_ref, cot_all, 2, take.take(4))
        up_job = Gather(side, up_ref, up_all, 1, take.take(4))
        shard = lax.axis_index("shard")
        cot_plan = Plan(grid[1])
        for p in range(2):
            plan_gather(cot_plan, cot_job, p, 0.0)
        cot_order = cot_plan.order()

        def own_cot(z):
            return pltpu.make_async_copy(cot_ref, cot_job.own_slot(z), own_sems.at[0])

        def own_up(z):
            return pltpu.make_async_copy(up_ref, up_job.own_slot(z), own_sems.at[1])

        loads = [
            pltpu.make_async_copy(ref, v[name], load_sems.at[i])
            for i, (name, ref) in enumerate(zip(names, hbm_refs))
        ]
        for c in loads:
            c.start()
        at_each_line(grid, lambda z: own_cot(z).start())
        at_each_line(side, lambda z: own_up(z).start())
        greet([grid, side])
        cot_plan.run(grid, cot_order, 0.0, 2.0)
        at_each_line(side, lambda z: up_job.start(z, 0))
        for c in loads[:-1]:
            c.wait()

        def norm(value, gain):
            return value * lax.rsqrt(jnp.mean(value * value, axis=-1, keepdims=True) + EPS) * gain

        @pl.loop(0, tokens // 32)
        def _(i):
            rows = pl.ds(pl.multiple_of(i * 32, 32), 32)
            normed[rows, :] = norm(v["rows"][rows, :].astype(F32), v["norm_gain"][...]).astype(BF)

        @pl.loop(0, inner // tile)
        def _(t):
            cols = pl.ds(pl.multiple_of(t * tile, tile), tile)
            query_lin[:, cols] = dot(normed[...], v["query_weight"][:, cols])

        key_lin[...] = dot(normed[...], v["key_weight"][...])
        value[...] = dot(normed[...], v["value_weight"][...]).astype(BF)

        def turn(rows):
            return rows * v["cosine"][...] + pltpu.roll(rows, head // 2, 1) * v["sine"][...]

        key[...] = turn(norm(key_lin[...], v["key_gain"][...])).astype(BF)
        rows_at = lax.broadcasted_iota(jnp.int32, (tokens, tokens), 0)
        cols_at = lax.broadcasted_iota(jnp.int32, (tokens, tokens), 1)
        allowed = jnp.logical_and(v["doc_col"][...] == v["doc_row"][...], rows_at >= cols_at)
        bias[...] = jnp.where(allowed, 0.0, -1e30)

        cot_order_late = [[s for s in steps if s[0] >= 2.0] for steps in cot_order]

        @pl.loop(0, heads)
        def _(h):
            lanes = pl.ds(pl.multiple_of(h * head, head), head)
            query[:, lanes] = turn(norm(query_lin[:, lanes], v["query_gain"][...])).astype(BF)
            for first in range(0, tokens, block):
                rows = pl.ds(first, block)
                keys = pl.ds(0, first + block)
                scores = dot_nt(query[rows, lanes], key[keys, :]) * scale + bias[rows, keys]
                top = jnp.max(scores, axis=-1, keepdims=True)
                powers = jnp.exp(scores - top)
                total = jnp.sum(powers, axis=-1, keepdims=True)
                log_total[h, rows, :] = top + jnp.log(total)
                probs = (powers * (1.0 / total)).astype(BF)
                mixed[rows, lanes] = dot(probs, value[keys, :]).astype(BF)
            cot_plan.run_step(grid, cot_order_late, h, 10.0, FORWARD_US, heads, True)

        loads[-1].wait()

        @pl.loop(0, columns // tile)
        def _(t):
            cols = pl.ds(pl.multiple_of(t * tile, tile), tile)
            parts[:, cols] = dot(mixed[...], v["out_weight"][:, cols]).astype(BF)

        def put(at, total):
            summed[at, :] = total

        plan = Plan(side[1])
        for p in range(2):
            plan_scatter(plan, job, p, put)
        plan.run(side, plan.order(), *ALWAYS)
        cot_plan.run(grid, cot_order, 10.0 + heads * FORWARD_US, 1e9)

        def forward_up(z):
            for origin in range(side[1]):
                if origin != z:
                    up_job.forward(z, origin, 0)

        at_each_line(side, forward_up)

        @pl.loop(0, own_rows // 16)
        def _(i):
            rows = pl.ds(pl.multiple_of(i * 16, 16), 16)
            from_rows = pl.ds(pl.multiple_of(shard * own_rows + i * 16, 16), 16)
            total = v["rows"][from_rows, :].astype(F32) + summed[rows, :]
            residual[rows, :] = total
            normed_two[rows, :] = norm(total, v["norm_two_gain"][...]).astype(BF)

        at_each_line(side, job.finish)

        def end_cot(z):
            cot_job.finish(z)
            own_cot(z).wait()

        def end_up(z):
            up_job.finish(z)
            own_up(z).wait()

        at_each_line(side, end_up)
        at_each_line(grid, end_cot)

    values = [arrays[name] for name in names]
    shape = jax.ShapeDtypeStruct
    return pl.pallas_call(
        kernel,
        out_shape=[
            shape((tokens, columns), BF),
            shape((tokens, inner), F32),
            shape((tokens, head), F32),
            shape((tokens, inner), BF),
            shape((tokens, head), BF),
            shape((tokens, head), BF),
            shape((tokens, inner), BF),
            shape((heads, tokens, 1), F32),
            shape((own_rows, columns), F32),
            shape((own_rows, columns), BF),
            shape((size * own_rows, columns), BF),
            shape((shards * up_own.shape[0], columns), BF),
        ],
        in_specs=[hbm()] * (len(names) + 2),
        out_specs=[vmem()] * 10 + [hbm()] * 2,
        scratch_shapes=[pltpu.VMEM(a.shape, a.dtype) for a in values]
        + [
            pltpu.VMEM((tokens, tokens), F32),
            pltpu.VMEM((tokens, columns), BF),
            pltpu.VMEM((own_rows, columns), F32),
        ]
        + Scatter.buffers(side, own_rows, columns, BF)
        + [pltpu.SemaphoreType.DMA((len(names),)), pltpu.SemaphoreType.DMA((2,))]
        + Scatter.sems(side, 2)
        + Gather.sems(grid, 2)
        + Gather.sems(side, 1),
        compiler_params=params(number),
        name="attention_forward",
    )(*values, cot_own, up_own)


def attention_backward(arrays, d_own, heads, number):
    grid, side = grid_of("expert"), grid_of("shard")
    _, lines, width, _ = grid
    size = lines * width
    shards = side[1] * side[2]
    names = list(arrays)
    tokens, columns = shards * d_own.shape[0], d_own.shape[1]
    inner = arrays["mixed"].shape[1]
    head = inner // heads
    count = inner // size
    pair = width * count
    tile = 256
    scale = head ** (-0.5)
    block = min(256, tokens)
    orders = [targets(lines, z) for z in range(lines)]
    split = [share_of(columns), columns - share_of(columns)]
    kinds = [(2, False), (1, True)]
    share = share_of(inner + 2 * head)

    def kernel(*refs):
        take = Taker(refs)
        hbm_refs, d_own_ref = take.take(len(names)), take.one()
        grad_refs = take.take(2)
        input_grad_ref, norm_gain_ref, gains_ref = take.take(3)
        sum_refs = take.take(2)
        v = dict(zip(names, take.take(len(names))))
        d_attn, d_mixed, bias, dk, dv, lines_ref, d_norm_ref = take.take(7)
        parts = take.take(2)
        jobs = [
            Reduce(grid, parts[i], sum_refs[i], take.take(Reduce.refs(kinds[i][1])), *kinds[i])
            for i in range(2)
        ]
        side_parts = take.one()
        side_buffers = take.take(3)
        load_sems, own_sems = take.take(2)
        gather = Gather(side, d_own_ref, d_attn, 2, take.take(4))
        side_job = Scatter(side, side_parts, side_buffers, 2, take.take(6))
        me, z, _ = position(grid)
        plan = Plan(lines)
        for job in jobs:
            job.plan(plan, [(i + 1) * PAIR_US for i in range(lines)], False)
        order = plan.order()

        def own(z):
            return pltpu.make_async_copy(d_own_ref, gather.own_slot(z), own_sems.at[0])

        at_each_line(side, lambda z: own(z).start())
        loads = [
            pltpu.make_async_copy(ref, v[name], load_sems.at[i])
            for i, (name, ref) in enumerate(zip(names, hbm_refs))
        ]
        for c in loads:
            c.start()
        greet([grid, side])

        def gather_start(z):
            for p in range(2):
                gather.start(z, p)
            for p in range(2):
                for origin in range(side[1]):
                    if origin != z:
                        gather.forward(z, origin, p)

        at_each_line(side, gather_start)
        for c in loads:
            c.wait()

        rows_at = lax.broadcasted_iota(jnp.int32, (tokens, tokens), 0)
        cols_at = lax.broadcasted_iota(jnp.int32, (tokens, tokens), 1)
        allowed = jnp.logical_and(v["doc_col"][...] == v["doc_row"][...], rows_at >= cols_at)
        bias[...] = jnp.where(allowed, 0.0, -1e30)
        dk[...] = jnp.zeros_like(dk)
        dv[...] = jnp.zeros_like(dv)
        gains_ref[...] = jnp.zeros_like(gains_ref)

        def gather_end(z):
            gather.finish(z)
            own(z).wait()

        at_each_line(side, gather_end)

        @pl.loop(0, lines)
        def _(i):
            k = jnp.int32(0)
            for at in range(lines):
                for step in range(lines):
                    k = jnp.where(jnp.logical_and(z == at, i == step), orders[at][step], k)
            lanes = pl.ds(pl.multiple_of(k * pair, pair), pair)

            rows = pl.ds(pl.multiple_of(k * pair, pair), pair)
            first = 0
            for n in range(2):

                value = dot_tn(v["mixed"][:, lanes], d_attn[:, first : first + split[n]])
                parts[n][rows, :] = value.astype(BF)
                first += split[n]
                for p in range(kinds[n][0]):
                    jobs[n].start_one(k, p)

        @pl.loop(0, inner // tile)
        def _(t):
            rows = pl.ds(pl.multiple_of(t * tile, tile), tile)
            d_mixed[:, rows] = dot_nt(d_attn[...], v["out_weight"][rows, :]).astype(BF)

        def unturn(grad):
            turned = pltpu.roll(grad * v["sine"][...], head // 2, 1)
            return grad * v["cosine"][...] + turned

        def unnorm(grad, linear, gain, row):
            inverse = lax.rsqrt(jnp.mean(linear * linear, axis=-1, keepdims=True) + EPS)
            gains_ref[row : row + 1, :] = gains_ref[row : row + 1, :] + jnp.sum(
                grad * linear * inverse, axis=0, keepdims=True
            )
            return rms_backward(linear, inverse, gain, grad)

        begin = lines * PAIR_US + 3.0

        @pl.loop(0, heads)
        def _(h):
            lanes = pl.ds(pl.multiple_of(h * head, head), head)
            grads = []
            for first in range(0, tokens, block):
                rows = pl.ds(first, block)
                keys = pl.ds(0, first + block)
                query = v["query"][rows, lanes]
                scores = dot_nt(query, v["key"][keys, :])
                probs = jnp.exp(scores * scale + bias[rows, keys] - v["log_total"][h, rows, :])
                back = d_mixed[rows, lanes]
                d_probs = dot_nt(back, v["value"][keys, :])
                inner_sum = jnp.sum(probs * d_probs, axis=-1, keepdims=True)
                d_scores = (probs * (d_probs - inner_sum)).astype(BF)
                dv[keys, :] = dv[keys, :] + dot_tn(probs.astype(BF), back)
                dk[keys, :] = dk[keys, :] + dot_tn(d_scores, query)
                grads.append(dot(d_scores, v["key"][keys, :]))
            grad = jnp.concatenate(grads, axis=0) * scale
            grad = unnorm(unturn(grad), v["query_lin"][:, lanes], v["query_gain"][...], 0)
            lines_ref[:, lanes] = grad.astype(BF)
            plan.run_step(grid, order, h, begin, HEAD_US, heads, True)

        grad = unnorm(unturn(dk[...] * scale), v["key_lin"][...], v["key_gain"][...], 1)
        lines_ref[:, inner : inner + head] = grad.astype(BF)
        lines_ref[:, inner + head : inner + 2 * head] = dv[...].astype(BF)

        @pl.loop(0, columns // tile)
        def _(t):
            rows = pl.ds(pl.multiple_of(t * tile, tile), tile)
            value = dot_nt(lines_ref[:, :inner], v["query_weight"][rows, :])
            value = value + dot_nt(lines_ref[:, inner : inner + head], v["key_weight"][rows, :])
            value = value + dot_nt(lines_ref[:, inner + head :], v["value_weight"][rows, :])
            side_parts[:, rows] = value.astype(BF)

        def put_norm(at, total):
            d_norm_ref[at, :] = total

        side_plan = Plan(side[1])
        for p in range(2):
            plan_scatter(side_plan, side_job, p, put_norm)
        side_order = side_plan.order()

        def side_begin(z):
            for _, act in side_order[z][:-2]:
                act()

        def side_end(z):
            for _, act in side_order[z][-2:]:
                act()

        at_each_line(side, side_begin)
        middle = begin + heads * HEAD_US
        tiles = columns // tile

        @pl.loop(0, tiles)
        def _(t):
            rows = pl.ds(pl.multiple_of(t * tile, tile), tile)
            value = dot_tn(v["normed"][:, rows], lines_ref[...])
            grad_refs[0][rows, :] = value[:, :share].astype(BF)
            grad_refs[1][rows, :] = value[:, share:].astype(BF)
            plan.run_step(grid, order, t, middle, TILE_US, tiles)

        at_each_line(side, side_end)
        plan.run(grid, order, middle + tiles * TILE_US, middle + tiles * TILE_US + 6.0)

        norm_gain_ref[...] = jnp.zeros_like(norm_gain_ref)

        @pl.loop(0, d_own.shape[0] // 16)
        def _(i):
            rows = pl.ds(pl.multiple_of(i * 16, 16), 16)
            value = v["input_own"][rows, :].astype(F32)
            grad = d_norm_ref[rows, :]
            inverse = lax.rsqrt(jnp.mean(value * value, axis=-1, keepdims=True) + EPS)
            norm_gain_ref[0:1, :] = norm_gain_ref[0:1, :] + jnp.sum(
                grad * value * inverse, axis=0, keepdims=True
            )
            back = rms_backward(value, inverse, v["norm_gain"][...], grad)
            input_grad_ref[rows, :] = (v["d_residual"][rows, :] + back).astype(BF)

        plan.run(grid, order, middle + tiles * TILE_US + 6.0, 1e9)

        def end(z):
            for job in jobs:
                job.finish(z)

        at_each_line(grid, end)
        at_each_line(side, side_job.finish)

    dma = pltpu.SemaphoreType.DMA
    values = [arrays[name] for name in names]
    out = pl.pallas_call(
        kernel,
        out_shape=[
            jax.ShapeDtypeStruct((columns, share), BF),
            jax.ShapeDtypeStruct((columns, inner + 2 * head - share), BF),
            jax.ShapeDtypeStruct(d_own.shape, BF),
            jax.ShapeDtypeStruct((8, columns), F32),
            jax.ShapeDtypeStruct((8, head), F32),
            jax.ShapeDtypeStruct((inner, split[0]), BF),
            jax.ShapeDtypeStruct((inner, split[1]), BF),
        ],
        in_specs=[hbm()] * (len(names) + 1),
        out_specs=[vmem()] * 5 + [hbm()] * 2,
        scratch_shapes=[pltpu.VMEM(a.shape, a.dtype) for a in values]
        + [
            pltpu.VMEM((tokens, columns), BF),
            pltpu.VMEM((tokens, inner), BF),
            pltpu.VMEM((tokens, tokens), F32),
            pltpu.VMEM((tokens, head), F32),
            pltpu.VMEM((tokens, head), F32),
            pltpu.VMEM((tokens, inner + 2 * head), BF),
            pltpu.VMEM(d_own.shape, F32),
            pltpu.VMEM((inner, split[0]), BF),
            pltpu.VMEM((inner, split[1]), BF),
        ]
        + Reduce.scratch(grid, inner, split[0], BF, *kinds[0])
        + Reduce.scratch(grid, inner, split[1], BF, *kinds[1])
        + [pltpu.VMEM((tokens, columns), BF)]
        + Scatter.buffers(side, d_own.shape[0], columns, BF)
        + [dma((len(names),)), dma((1,))]
        + Gather.sems(side, 2)
        + Scatter.sems(side, 2),
        compiler_params=params(number),
        name="attention_backward",
    )(*values, d_own)
    first, second, input_grad, norm_gain, gains, *out_sums = out
    out_sum = jnp.concatenate(out_sums, axis=1)
    return (first, second), input_grad, norm_gain[0], gains[0], gains[1], out_sum


def rope_tables(positions, head_size):
    half_size = head_size // 2
    frequency = THETA ** (-2.0 * jnp.arange(half_size, dtype=F32) / head_size)
    angles = positions.astype(F32)[:, None] * frequency[None, :]
    return (jnp.cos(angles), jnp.sin(angles))


def doc_positions(doc_ids):
    row_index = jnp.arange(doc_ids.shape[0], dtype=jnp.int32)
    doc_starts = jnp.concatenate([jnp.ones((1,), jnp.bool_), doc_ids[1:] != doc_ids[:-1]])
    first_row = lax.cummax(jnp.where(doc_starts, row_index, 0), axis=0)
    return row_index - first_row


def from_near(rows, count):
    return lax.ppermute(rows, "shard", [(s, s + 1 - 2 * (s % 2)) for s in range(count)])


def from_far(rows, count):
    return lax.ppermute(rows, "shard", [(s, (s + 2) % count) for s in range(count)])


def local(
    layer_input,
    doc_ids,
    routes,
    norm1_gain,
    query_weight,
    key_matrix,
    value_matrix,
    query_norm_gain,
    key_norm_gain,
    out_weight,
    norm2_gain,
    router_weight,
    gate_weight,
    up_weight,
    down_weight,
    cotangent,
):
    tokens_here, model_width = layer_input.shape
    head_size = query_norm_gain.shape[0]
    heads_here = query_weight.shape[1] // head_size
    experts_all = router_weight.shape[1]
    local_experts, _, hidden_here = gate_weight.shape
    expert_peers = lax.axis_size("expert")
    shard_count = lax.axis_size("shard")
    rows_here = tokens_here // shard_count
    shard_index = lax.axis_index("shard")
    expert_index = lax.axis_index("expert")
    hidden_all = shard_count * local_experts * hidden_here

    def own(rows):
        return lax.dynamic_slice_in_dim(rows, shard_index * rows_here, rows_here, axis=0)

    def gather_weight(weight):
        return lax.all_gather(weight, "shard", axis=0).reshape(hidden_all, model_width)

    fused = expert_peers * rows_here <= VMEM_ROWS
    cot_own = own(cotangent)
    routes_own = own(routes)
    experts = jnp.arange(experts_all, dtype=jnp.int32)
    chosen_own = jnp.any(routes_own[:, :, None] == experts[None, None, :], axis=1)
    gate_weight = jnp.swapaxes(gate_weight, 1, 2)
    up_weight = jnp.swapaxes(up_weight, 1, 2)
    if fused:
        gate_far = from_far(gate_weight, shard_count)
        gate_near = from_near(gate_weight, shard_count)
    else:
        down_all = gather_weight(down_weight)
        gate_all = gather_weight(gate_weight)
        up_all = gather_weight(up_weight)

    positions = doc_positions(doc_ids)
    cosine_table, sine_values = rope_tables(positions, head_size)
    inner = heads_here * head_size
    shared = dict(
        cosine=jnp.concatenate([cosine_table, cosine_table], axis=1),
        sine=jnp.concatenate([-sine_values, sine_values], axis=1),
        query_gain=query_norm_gain[None, :],
        key_gain=key_norm_gain[None, :],
        doc_col=doc_ids[:, None],
        doc_row=doc_ids[None, :],
        query_weight=query_weight,
        key_weight=key_matrix,
        value_weight=value_matrix,
        norm_gain=norm1_gain[None, :],
    )
    forward = dict(
        rows=layer_input, norm_two_gain=norm2_gain[None, :], **shared, out_weight=out_weight
    )
    normed_one, query_lin, key_lin, query, key, value, mixed, log_total, *rest = (
        attention_forward(forward, cot_own, up_weight[0], heads_here, 1)
    )
    residual, normed_two, cot_all, up_first = rest
    if fused:
        gate_far, residual, normed_two = lax.optimization_barrier(
            (gate_far, residual, normed_two)
        )

    if fused:
        up_late, down_late, normed_two = lax.optimization_barrier(
            (up_weight[1:], down_weight, normed_two)
        )
        up_far, down_far = from_far(up_late, shard_count), from_far(down_late, shard_count)
        up_near, down_near = from_near(up_late, shard_count), from_near(down_late, shard_count)
    _, inverse_two = rms_forward(residual, norm2_gain)
    chosen_wide = jnp.pad(chosen_own.astype(BF), ((0, 0), (0, EXTRA - experts_all)))
    normed_all, chosen_all = gather_rows([normed_two, chosen_wide], [], 2, (2, 1))
    if fused:
        up_far, down_far, normed_all = lax.optimization_barrier((up_far, down_far, normed_all))
        rel = []
        for own_one, near, far in (
            (gate_weight, gate_near, gate_far),
            (up_late, up_near, up_far),
            (down_late, down_near, down_far),
        ):
            rel.append([own_one, near, far, from_near(far, shard_count)])

    def gate_table(rows, chosen):
        logits = jnp.where(chosen, dot(rows, router_weight), -jnp.inf)
        top = jnp.max(logits, axis=-1, keepdims=True)
        powers = jnp.exp(logits - top)
        return powers / jnp.sum(powers, axis=-1, keepdims=True)

    if fused:
        router_wide = jnp.pad(router_weight, ((0, 0), (0, EXTRA - experts_all)))
        summed, out_part, gate_part, up_part, down_part = expert_rows(
            normed_all, cot_all, chosen_all, router_wide, rel[0], up_first, rel[1], rel[2], 3
        )
        d_rows_own = summed[:, :model_width]
        d_gates_own = (
            summed[:, model_width : model_width + experts_all]
            + summed[:, model_width + experts_all : model_width + 2 * experts_all]
        )
    else:
        gates_here = lax.dynamic_slice_in_dim(
            gate_table(normed_all, chosen_all[:, :experts_all] > 0.5),
            expert_index * local_experts,
            local_experts,
            axis=1,
        )
        column_expert = (jnp.arange(hidden_all, dtype=jnp.int32) // hidden_here) % local_experts
        gate_columns = jnp.zeros((1, 1), F32)
        for j in range(local_experts):
            gate_columns = jnp.where(column_expert[None, :] == j, gates_here[:, j : j + 1], gate_columns)

        d_act_raw = dot_nt(cot_all, down_all)
        gate_pre = dot_nt(normed_all, gate_all)
        up_pre = dot_nt(normed_all, up_all)
        sig = jax.nn.sigmoid(gate_pre)
        silu = gate_pre * sig
        act = silu * up_pre
        act_gated = (act * gate_columns).astype(BF)
        d_act = d_act_raw * gate_columns
        d_gate_low = (d_act * up_pre * sig * (1.0 + gate_pre * (1.0 - sig))).astype(BF)
        d_up_low = (d_act * silu).astype(BF)
        act_back = act * d_act_raw
        d_gates_here = jnp.stack(
            [
                jnp.sum(jnp.where(column_expert[None, :] == j, act_back, 0.0), axis=1)
                for j in range(local_experts)
            ],
            axis=-1,
        )
        d_rows = dot(d_gate_low, gate_all) + dot(d_up_low, up_all)
        d_rows_own = scatter_rows(d_rows.astype(BF), "expert", 3, 2)
        out_part = dot(act_gated, down_all).astype(BF)

        def split(grad):
            return grad.astype(BF).reshape(shard_count, local_experts, hidden_here, model_width)

        gate_part = split(dot_tn(d_gate_low, normed_all))
        up_part = split(dot_tn(d_up_low, normed_all))
        down_part = split(dot_tn(act_gated, cot_all))

        d_gates_own = lax.all_to_all(
            d_gates_here.reshape(expert_peers, rows_here, local_experts),
            "expert",
            split_axis=0,
            concat_axis=0,
            tiled=True,
        )
        d_gates_own = jnp.swapaxes(d_gates_own, 0, 1).reshape(rows_here, experts_all)
    out_own = lax.psum_scatter(out_part, "expert", scatter_dimension=0, tiled=True)
    def scatter_grad(grad):
        return lax.psum_scatter(grad, "shard", scatter_dimension=0, tiled=False)

    gate_grad = jnp.swapaxes(scatter_grad(gate_part).astype(F32), 1, 2)
    up_grad = jnp.swapaxes(scatter_grad(up_part).astype(F32), 1, 2)

    gates_own = gate_table(normed_two, chosen_own)
    d_logits = gates_own * (
        d_gates_own - jnp.sum(gates_own * d_gates_own, axis=-1, keepdims=True)
    )
    d_logits_low = d_logits.astype(BF)
    router_grad = dot_tn(normed_two, d_logits_low)
    d_normed_two = d_rows_own + dot_nt(d_logits_low, router_weight)
    norm2_grad = jnp.sum(d_normed_two * residual * inverse_two, axis=0)
    d_residual = cot_own.astype(F32) + rms_backward(
        residual, inverse_two, norm2_gain, d_normed_two
    )
    backward = dict(
        mixed=mixed,
        query=query,
        key=key,
        value=value,
        query_lin=query_lin,
        key_lin=key_lin,
        log_total=log_total,
        out_weight=out_weight,
        normed=normed_one,
        input_own=own(layer_input),
        d_residual=d_residual,
        **shared,
    )
    line_grads, input_grad_own, norm1_grad, d_query_gain, d_key_gain, out_sum = (
        attention_backward(backward, d_residual.astype(BF), heads_here, 4)
    )
    share = share_of(inner + 2 * head_size)
    out_own, _ = lax.optimization_barrier((out_own, norm1_grad))
    layer_out_own = (residual + out_own).astype(BF)

    flat = jnp.concatenate(
        [router_grad.T.reshape(-1), norm2_grad, norm1_grad, d_query_gain, d_key_gain]
    )
    small_rows = 8 * expert_peers
    small_columns = -(-flat.shape[0] // (128 * small_rows)) * 128
    small = jnp.pad(flat, (0, small_rows * small_columns - flat.shape[0]))
    (line_first, line_second, small), (input_grad, layer_out), down_sum = sum_and_gather(
        *line_grads,
        small.reshape(small_rows, small_columns),
        (input_grad_own, layer_out_own),
        down_part.reshape(hidden_all, model_width),
        5,
    )
    down_grad = down_sum.reshape(local_experts, hidden_here, model_width)
    query_cols = inner - share
    query_sum = jnp.concatenate([line_first, line_second[:, :query_cols]], axis=1)
    key_sum = line_second[:, query_cols : query_cols + head_size]
    value_sum = line_second[:, query_cols + head_size :]
    small = small.reshape(-1)
    bounds = [experts_all * model_width, model_width, model_width, head_size, head_size]
    taken = []
    at = 0
    for bound in bounds:
        taken.append(small[at : at + bound])
        at += bound
    router_sum, norm2_sum, norm1_sum, query_gain_sum, key_gain_sum = taken
    router_sum = router_sum.reshape(experts_all, model_width).T
    return (
        layer_out,
        input_grad,
        norm1_sum,
        query_sum.astype(F32),
        key_sum.astype(F32),
        value_sum.astype(F32),
        query_gain_sum,
        key_gain_sum,
        out_sum.astype(F32),
        norm2_sum,
        router_sum,
        gate_grad,
        up_grad,
        down_grad,
    )


def solution(mesh):
    return jax.shard_map(
        local,
        mesh=mesh,
        in_specs=(
            P("expert", None),
            P("expert"),
            P("expert", None),
            P(),
            P(None, "shard"),
            P(None, "shard"),
            P(None, "shard"),
            P(),
            P(),
            P("shard", None),
            P(),
            P(),
            P("expert", None, "shard"),
            P("expert", None, "shard"),
            P("expert", "shard", None),
            P("expert", None),
        ),
        out_specs=(
            P("expert", None),
            P("expert", None),
            P(),
            P(None, "shard"),
            P(None, "shard"),
            P(None, "shard"),
            P(),
            P(),
            P("shard", None),
            P(),
            P(),
            P("expert", None, "shard"),
            P("expert", None, "shard"),
            P("expert", "shard", None),
        ),
        check_vma=False,
    )
```

```python
import jax
import jax.numpy as jnp
from jax import lax
from jax.experimental import pallas as pl
from jax.experimental.pallas import tpu as pltpu
from jax.sharding import PartitionSpec as P

EPS = 1e-06
THETA = 1000000.0
BF = jnp.bfloat16
F32 = jnp.float32
MESH = pl.DeviceIdType.MESH
VMEM_ROWS = 1024


def dot(a, b):
    return jnp.dot(a, b, preferred_element_type=F32)


def dot_nt(a, b):
    return lax.dot_general(a, b, (((1,), (1,)), ((), ())), preferred_element_type=F32)


def dot_tn(a, b):
    return lax.dot_general(a, b, (((0,), (0,)), ((), ())), preferred_element_type=F32)


LINK_BYTES_PER_US = 1e5


def grid_of(axis):
    size = lax.axis_size(axis)
    lines = 4 if axis == "expert" else 2
    return axis, lines, size // lines, size // lines


def line_of(grid):
    return grid[0], grid[1], 1, grid[3]


def cross_of(grid):
    return grid[0], 1, grid[2], grid[3]


def position(grid):
    axis, lines, width, stride = grid
    me = lax.axis_index(axis)
    return me, me // stride if lines > 1 else 0, me % width if width > 1 else 0


def at_each_line(grid, act):
    _, z, _ = position(grid)
    for at in range(grid[1]):

        @pl.when(z == at)
        def _():
            act(at)


def greet(grids):
    barrier = pltpu.get_barrier_semaphore()
    count = 0
    for grid in grids:
        axis, lines, width, stride = grid
        me, z, b = position(grid)

        def signal(peer):
            pl.semaphore_signal(barrier, inc=1, device_id={axis: peer}, device_id_type=MESH)

        @pl.when(z < lines - 1)
        def _():
            signal(me + stride)

        @pl.when(z > 0)
        def _():
            signal(me - stride)

        for o in range(1, width):
            signal(me - b + (b + o) % width)
        count = count + width - 1
        count = count + (z < lines - 1).astype(jnp.int32) + (z > 0).astype(jnp.int32)
    pl.semaphore_wait(barrier, count)


def slice_of(ref, start, rows):
    if not isinstance(start, int):
        start = pl.multiple_of(start, rows)
    return ref.at[pl.ds(start, rows)]


class Gather:
    def __init__(self, grid, source, out, pieces, sems):
        self.axis, self.lines, self.width, self.stride = grid
        self.source, self.out, self.pieces = source, out, pieces
        self.rows_all = source.shape[0]
        self.rows = self.rows_all // pieces
        self.send_r, self.send_l, self.send_x, self.recv = sems
        self.me, _, self.b = position(grid)
        self.bytes = self.rows * source.shape[1] * jnp.dtype(source.dtype).itemsize

    @staticmethod
    def sems(grid, pieces):
        _, lines, width, _ = grid
        dma = pltpu.SemaphoreType.DMA
        return [
            dma((lines, pieces)),
            dma((lines, pieces)),
            dma((max(1, width - 1), lines, pieces)),
            dma((lines * width, pieces)),
        ]

    def copy(self, slot, p, sem, peer, own=False):
        place = slice_of(self.out, slot * self.rows_all + p * self.rows, self.rows)
        source = slice_of(self.source, p * self.rows, self.rows) if own else place
        return pltpu.make_async_remote_copy(
            src_ref=source,
            dst_ref=place,
            send_sem=sem,
            recv_sem=self.recv.at[slot, p],
            device_id={self.axis: peer},
            device_id_type=MESH,
        )

    def sends(self, z, origin, p):
        slot = origin * self.width + self.b
        own = origin == z
        copies = []
        if origin <= z and z < self.lines - 1:
            sem = self.send_r.at[z - origin, p]
            copies.append(self.copy(slot, p, sem, self.me + self.stride, own))
        if origin >= z and z > 0:
            sem = self.send_l.at[origin - z, p]
            copies.append(self.copy(slot, p, sem, self.me - self.stride, own))
        for o in range(1, self.width):
            peer = self.me - self.b + (self.b + o) % self.width
            copies.append(self.copy(slot, p, self.send_x.at[o - 1, origin, p], peer, own))
        return copies

    def start(self, z, p):
        for c in self.sends(z, z, p):
            c.start()

    def arrived(self, slot, p):
        self.copy(slot, p, self.send_r.at[0, p], self.me).wait_recv()

    def forward(self, z, origin, p):
        self.arrived(origin * self.width + self.b, p)
        for c in self.sends(z, origin, p):
            c.start()

    def arrived_across(self, z, p):
        for o in range(1, self.width):
            self.arrived(z * self.width + (self.b + o) % self.width, p)

    def wait_sends(self, z):
        for p in range(self.pieces):
            for origin in range(self.lines):
                for c in self.sends(z, origin, p):
                    c.wait_send()

    def finish(self, z):
        for p in range(self.pieces):
            for line in range(self.lines):
                self.arrived_across(line, p)
        self.wait_sends(z)

    def own_slot(self, z):
        return slice_of(self.out, (z * self.width + self.b) * self.rows_all, self.rows_all)


class Scatter:
    def __init__(self, grid, parts, buffers, pieces, sems):
        self.axis, self.lines, self.width, self.stride = grid
        self.parts, self.pieces = parts, pieces
        self.cross, self.right, self.left = buffers
        self.rows_all = parts.shape[0] // (self.lines * self.width)
        self.rows = self.rows_all // pieces
        self.cross_send, self.cross_recv, self.r_send, self.r_recv, self.l_send, self.l_recv = sems
        self.me, _, self.b = position(grid)
        self.bytes = self.rows * parts.shape[1] * jnp.dtype(parts.dtype).itemsize

    @staticmethod
    def sems(grid, pieces):
        _, lines, width, _ = grid
        dma = pltpu.SemaphoreType.DMA
        across = (max(1, width - 1), lines, pieces)
        return [dma(across), dma(across)] + [dma((lines, pieces)) for _ in range(4)]

    @staticmethod
    def buffers(grid, rows_all, columns, kind):
        _, lines, width, _ = grid
        line = pltpu.VMEM((lines * rows_all if lines > 1 else 16, columns), kind)
        return [pltpu.VMEM((max(1, width - 1) * lines * rows_all, columns), kind), line, line]

    def start_of(self, slot, p):
        return slot * self.rows_all + p * self.rows

    def cross_copy(self, o, k, p):
        peer = (self.b + o) % self.width
        return pltpu.make_async_remote_copy(
            src_ref=slice_of(self.parts, self.start_of(k * self.width + peer, p), self.rows),
            dst_ref=slice_of(self.cross, self.start_of((o - 1) * self.lines + k, p), self.rows),
            send_sem=self.cross_send.at[o - 1, k, p],
            recv_sem=self.cross_recv.at[o - 1, k, p],
            device_id={self.axis: self.me - self.b + peer},
            device_id_type=MESH,
        )

    def line_copy(self, k, p, rightward):
        into = self.right if rightward else self.left
        at = self.start_of(k, p)
        return pltpu.make_async_remote_copy(
            src_ref=slice_of(self.cross, at, self.rows),
            dst_ref=slice_of(into, at, self.rows),
            send_sem=(self.r_send if rightward else self.l_send).at[k, p],
            recv_sem=(self.r_recv if rightward else self.l_recv).at[k, p],
            device_id={self.axis: self.me + self.stride if rightward else self.me - self.stride},
            device_id_type=MESH,
        )

    def start_one(self, k, p):
        for o in range(1, self.width):
            self.cross_copy(o, k, p).start()

    def add(self, k, p, sources, target):
        block = min(16, self.rows)
        own = self.start_of(k * self.width + self.b, p)

        @pl.loop(0, self.rows // block)
        def _(i):
            def rows_at(start):
                return pl.ds(pl.multiple_of(start + i * block, block), block)

            total = self.parts[rows_at(own), :].astype(F32)
            for o in range(self.width - 1):
                at = rows_at(self.start_of(o * self.lines + k, p))
                total = total + self.cross[at, :].astype(F32)
            for source in sources:
                total = total + source[rows_at(self.start_of(k, p)), :].astype(F32)
            target(rows_at(p * self.rows), total)

    def sources(self, z, k, p):
        found = []
        if k >= z and z > 0:
            self.line_copy(k, p, True).wait_recv()
            found.append(self.right)
        if k <= z and z < self.lines - 1:
            self.line_copy(k, p, False).wait_recv()
            found.append(self.left)
        return found

    def reduce_one(self, z, k, p):
        for o in range(1, self.width):
            self.cross_copy(o, k, p).wait_recv()

        def put(at, total):
            offset = pl.multiple_of(at.start + k * self.rows_all, at.size)
            self.cross[pl.ds(offset, at.size), :] = total.astype(self.cross.dtype)

        self.add(k, p, self.sources(z, k, p), put)
        self.line_copy(k, p, k > z).start()

    def total(self, z, p, target):
        for o in range(1, self.width):
            self.cross_copy(o, z, p).wait_recv()
        self.add(z, p, self.sources(z, z, p), target)

    def finish(self, z):
        for p in range(self.pieces):
            for k in range(self.lines):
                for o in range(1, self.width):
                    self.cross_copy(o, k, p).wait_send()
                if k != z:
                    self.line_copy(k, p, k > z).wait_send()


def targets(lines, z):
    others = sorted((k for k in range(lines) if k != z), key=lambda k: (-abs(k - z), -k))
    return others + [z]


class Plan:
    def __init__(self, lines):
        self.lines = lines
        self.steps = [[] for _ in range(lines)]
        self.jobs = 0

    def job(self):
        self.jobs += 1
        return self.jobs

    def add(self, z, waits, act, sends, begin=0.0):
        self.steps[z].append((begin, waits, act, sends))

    def order(self):
        arrived = [dict() for _ in range(self.lines)]
        free = {}
        clock = [0.0] * self.lines
        left = [list(enumerate(steps)) for steps in self.steps]
        result = [[] for _ in range(self.lines)]
        while any(left):
            best = None
            for z in range(self.lines):
                for i, (begin, waits, act, sends) in left[z]:
                    if all(key in arrived[z] for key in waits):
                        ready = max([begin] + [arrived[z][key] for key in waits])
                        if best is None or (max(ready, clock[z]), ready, z, i) < best[0]:
                            best = ((max(ready, clock[z]), ready, z, i), act, sends)
            (now, _, z, i), act, sends = best
            left[z] = [entry for entry in left[z] if entry[0] != i]
            result[z].append((now, act))
            clock[z] = now + 0.7
            for link, time, to, key in sends:
                start = max(now + 1.0, free.get((z, link), 0.0))
                free[z, link] = start + time
                arrived[to][key] = start + time + 1.0
        return result

    def run(self, grid, result, begin, end):
        def act(z):
            for now, step in result[z]:
                if begin <= now < end:
                    step()

        at_each_line(grid, act)


    def run_step(self, grid, result, index, begin, each, steps, early=False):
        _, z, _ = position(grid)
        for at in range(self.lines):
            for now, step in result[at]:
                due = int((now - begin) // each)
                if early:
                    due = max(0, due)
                if 0 <= due < steps:

                    @pl.when(jnp.logical_and(z == at, index == due))
                    def _():
                        step()


def plan_scatter(plan, scatter, p, put, then=None, begin=0.0, start=True):
    n = plan.job()
    lines, width = scatter.lines, scatter.width
    time = 2 * scatter.bytes / LINK_BYTES_PER_US
    for z in range(lines):
        ready = begin if isinstance(begin, (int, float)) else None
        for i, k in enumerate(targets(lines, z)):
            first = ready if ready is not None else begin[i]
            if width > 1:
                plan.add(
                    z,
                    [],
                    (lambda k=k: scatter.start_one(k, p)) if start else (lambda: None),
                    [("x", time * (width - 1), z, (n, "c", k))],
                    first,
                )
            waits = [(n, "c", k)] if width > 1 else []
            if k >= z and z > 0:
                waits.append((n, "r", k))
            if k <= z and z < lines - 1:
                waits.append((n, "l", k))
            if k > z:
                sends = [("r", time, z + 1, (n, "r", k))]
            elif k < z:
                sends = [("l", time, z - 1, (n, "l", k))]
            else:
                follow, sends = then(z) if then else ((lambda: None), [])

                def last(z=z, follow=follow):
                    scatter.total(z, p, put)
                    follow()

                plan.add(z, waits, last, sends, first)
                continue
            plan.add(z, waits, lambda z=z, k=k: scatter.reduce_one(z, k, p), sends, first)


def gather_sends(gather, n, time, z, origin):
    sends = []
    if origin <= z and z < gather.lines - 1:
        sends.append(("r", time, z + 1, (n, "g", origin)))
    if origin >= z and z > 0:
        sends.append(("l", time, z - 1, (n, "g", origin)))
    if gather.width > 1:
        sends.append(("x", time * (gather.width - 1), z, (n, "gx", origin)))
    return sends


def plan_gather(plan, gather, p, begin=None):
    n = plan.job()
    time = 2 * gather.bytes / LINK_BYTES_PER_US
    for z in range(gather.lines):
        for origin in range(gather.lines):
            if origin != z:
                plan.add(
                    z,
                    [(n, "g", origin)],
                    lambda z=z, origin=origin: gather.forward(z, origin, p),
                    gather_sends(gather, n, time, z, origin),
                )

    def then(z):
        return (lambda: gather.start(z, p)), gather_sends(gather, n, time, z, z)

    if begin is not None:
        for z in range(gather.lines):
            act, sends = then(z)
            plan.add(z, [], act, sends, begin)
    return then


class Reduce:
    def __init__(self, grid, parts, out, scratch, pieces, line_first):
        self.grid, self.parts, self.out = grid, parts, out
        self.line_first = line_first
        self.pieces = pieces
        take = Taker(scratch)
        self.sums = take.one()
        if line_first:
            self.pair_sums, self.pair_all = take.take(2)
            self.first = Scatter(line_of(grid), parts, take.take(3), 1, take.take(6))
            self.second = Scatter(cross_of(grid), self.pair_sums, take.take(3), 1, take.take(6))
            self.third = Gather(cross_of(grid), self.sums, self.pair_all, 1, take.take(4))
            self.fourth = Gather(line_of(grid), self.pair_all, out, 1, take.take(4))
        else:
            self.scatter = Scatter(grid, parts, take.take(3), pieces, take.take(6))
            self.gather = Gather(grid, self.sums, out, pieces, take.take(4))
        self.own_sem = take.one()

    @staticmethod
    def scratch(grid, rows, columns, kind, pieces, line_first):
        _, lines, width, _ = grid
        count = rows // (lines * width)
        shapes = [pltpu.VMEM((count, columns), kind)]
        if line_first:
            line, cross = line_of(grid), cross_of(grid)
            shapes += [pltpu.VMEM((width * count, columns), kind)] * 2
            shapes += Scatter.buffers(line, width * count, columns, kind) + Scatter.sems(line, 1)
            shapes += Scatter.buffers(cross, count, columns, kind) + Scatter.sems(cross, 1)
            shapes += Gather.sems(cross, 1) + Gather.sems(line, 1)
        else:
            shapes += Scatter.buffers(grid, count, columns, kind) + Scatter.sems(grid, pieces)
            shapes += Gather.sems(grid, pieces)
        return shapes + [pltpu.SemaphoreType.DMA]

    @staticmethod
    def refs(line_first):
        return 1 + (2 + 9 + 9 + 8 if line_first else 9 + 4) + 1

    def put(self, at, total):
        self.sums[at, :] = total.astype(self.sums.dtype)

    def put_pair(self, at, total):
        self.pair_sums[at, :] = total.astype(self.pair_sums.dtype)

    def own_copy(self, z):
        if self.line_first:
            return pltpu.make_async_copy(self.pair_all, self.fourth.own_slot(z), self.own_sem)
        return pltpu.make_async_copy(self.sums, self.gather.own_slot(z), self.own_sem)

    def start_one(self, k, p):
        if not self.line_first:
            self.scatter.start_one(k, p)

    def plan(self, plan, begin=0.0, start=True):
        if not self.line_first:
            for p in range(self.pieces):
                then = plan_gather(plan, self.gather, p)
                plan_scatter(plan, self.scatter, p, self.put, then, begin, start)
            return
        n = plan.job()
        time = 2 * self.second.bytes / LINK_BYTES_PER_US * (self.grid[2] - 1)
        along = plan_gather(plan, self.fourth, 0)

        def cross(z):
            return (lambda: self.second.start_one(0, 0)), [("x", time, z, (n, "c"))]

        plan_scatter(plan, self.first, 0, self.put_pair, cross, begin)
        for z in range(self.grid[1]):

            def across(z=z):
                self.second.total(0, 0, self.put)
                self.third.start(0, 0)
                at = pl.multiple_of(self.third.b * self.third.rows_all, self.third.rows_all)
                self.pair_all[pl.ds(at, self.third.rows_all), :] = self.sums[...]

            plan.add(z, [(n, "c")], across, [("x", time, z, (n, "x"))])
            follow, sends = along(z)

            def spread(follow=follow):
                self.third.arrived_across(0, 0)
                follow()

            plan.add(z, [(n, "x")], spread, sends)

    def finish(self, z):
        self.own_copy(z).start()
        if self.line_first:
            self.first.finish(z)
            self.second.finish(0)
            self.third.wait_sends(0)
            self.fourth.finish(z)
        else:
            self.scatter.finish(z)
            self.gather.finish(z)
        self.own_copy(z).wait()


def hbm():
    return pl.BlockSpec(memory_space=pl.ANY)


def vmem():
    return pl.BlockSpec(memory_space=pltpu.VMEM)


def params(number, mib=56):
    return pltpu.CompilerParams(
        collective_id=number, has_side_effects=True, vmem_limit_bytes=mib * 1024 * 1024
    )


class Taker:
    def __init__(self, refs):
        self.refs = list(refs)

    def take(self, count):
        taken = self.refs[:count]
        del self.refs[:count]
        return taken

    def one(self):
        return self.take(1)[0]


ALWAYS = (0.0, 1e9)


def gather_rows(arrays, side_arrays, number, pieces):
    grid, side = grid_of("expert"), grid_of("shard")
    values = list(arrays) + list(side_arrays)
    grids = [grid] * len(arrays) + [side] * len(side_arrays)
    n = len(values)

    def kernel(*refs):
        take = Taker(refs)
        ins, outs, own_sems = take.take(n), take.take(n), take.one()
        jobs = [Gather(grids[i], ins[i], outs[i], pieces[i], take.take(4)) for i in range(n)]

        def own(i, z):
            return pltpu.make_async_copy(ins[i], jobs[i].own_slot(z), own_sems.at[i])

        def each(i, act):
            at_each_line(grids[i], act)

        for i in range(n):
            each(i, lambda z, i=i: own(i, z).start())
        greet([grid] + ([side] if side_arrays else []))
        plan = Plan(grid[1])
        for i in range(len(arrays)):
            for p in range(pieces[i]):
                plan_gather(plan, jobs[i], p, 0.0)
        order = plan.order()
        plan.run(grid, order, 0.0, 1.0)
        late = 0.0 if not side_arrays else 1.0
        for i in range(len(arrays), n):
            for p in range(pieces[i]):
                each(i, lambda z, i=i, p=p: jobs[i].start(z, p))
        if side_arrays:
            edge = 2 * jobs[-1].bytes / LINK_BYTES_PER_US + 4.0
            begin = late
            for p in range(pieces[-1]):
                plan.run(grid, order, begin, edge * (p + 1))
                begin = edge * (p + 1)
                for i in range(len(arrays), n):

                    def forward(z, i=i, p=p):
                        for origin in range(grids[i][1]):
                            if origin != z:
                                jobs[i].forward(z, origin, p)

                    each(i, forward)
            plan.run(grid, order, begin, 1e9)
        else:
            plan.run(grid, order, 1.0, 1e9)
        for i in range(n):
            each(i, lambda z, i=i: jobs[i].finish(z))
            each(i, lambda z, i=i: own(i, z).wait())

    scratch = [pltpu.SemaphoreType.DMA((n,))]
    for g, p in zip(grids, pieces):
        scratch += Gather.sems(g, p)
    return pl.pallas_call(
        kernel,
        out_shape=[
            jax.ShapeDtypeStruct((g[1] * g[2] * a.shape[0], a.shape[1]), a.dtype)
            for a, g in zip(values, grids)
        ],
        in_specs=[hbm()] * n,
        out_specs=[hbm()] * n,
        scratch_shapes=scratch,
        compiler_params=params(number),
        name="gather_rows",
    )(*values)


def scatter_rows(parts, axis, number, pieces):
    grid = grid_of(axis)
    columns = parts.shape[1]
    count = parts.shape[0] // (grid[1] * grid[2])

    def kernel(parts_ref, out_ref, cross, right, left, *sems):
        greet([grid])
        job = Scatter(grid, parts_ref, (cross, right, left), pieces, sems)

        def put(at, total):
            out_ref[at, :] = total

        plan = Plan(grid[1])
        for p in range(pieces):
            plan_scatter(plan, job, p, put)
        plan.run(grid, plan.order(), *ALWAYS)
        at_each_line(grid, job.finish)

    return pl.pallas_call(
        kernel,
        out_shape=jax.ShapeDtypeStruct((count, columns), F32),
        in_specs=[vmem()],
        out_specs=vmem(),
        scratch_shapes=Scatter.buffers(grid, count, columns, parts.dtype)
        + Scatter.sems(grid, pieces),
        compiler_params=params(number),
        name="scatter_" + axis,
    )(parts)


def sum_and_gather(across_first, line_first, small, rows, spread, number):
    grid, side = grid_of("expert"), grid_of("shard")
    size = grid[1] * grid[2]
    shards = side[1] * side[2]
    values = [across_first, line_first, small]
    moved = [small] + list(rows)
    m = len(moved)
    kinds = [(2, False), (1, True), (1, False)]

    def kernel(*refs):
        take = Taker(refs)
        first_ref, second_ref, spread_ref = take.take(3)
        side_ins = take.take(m)
        outs, rows_outs, spread_out = take.take(3), take.take(m - 1), take.one()
        small_all, small_parts, own_sems = take.take(3)
        ins = [first_ref, second_ref, small_parts]
        jobs = [
            Reduce(grid, ins[i], outs[i], take.take(Reduce.refs(kinds[i][1])), *kinds[i])
            for i in range(3)
        ]
        spread_job = Scatter(side, spread_ref, take.take(3), 1, take.take(6))
        side_outs = [small_all] + rows_outs
        side_jobs = [Gather(side, side_ins[i], side_outs[i], 1, take.take(4)) for i in range(m)]

        def own(z, i):
            return pltpu.make_async_copy(side_ins[i], side_jobs[i].own_slot(z), own_sems.at[i])

        def begin_side(z):
            for i in range(m):
                own(z, i).start()

        at_each_line(side, begin_side)
        greet([grid, side])
        edges = [0.0, 6.0, 16.0, 28.0, 55.0]
        plan = Plan(grid[1])
        jobs[1].plan(plan)
        jobs[0].plan(plan)
        jobs[2].plan(plan, edges[3])
        order = plan.order()
        plan.run(grid, order, 0.0, edges[1])
        at_each_line(side, lambda z: side_jobs[0].start(z, 0))
        plan.run(grid, order, edges[1], edges[2])

        def forward(z, chosen):
            for origin in range(side[1]):
                if origin != z:
                    for job in chosen:
                        job.forward(z, origin, 0)

        def start(z):
            forward(z, side_jobs[:1])
            for job in side_jobs[1:]:
                job.start(z, 0)
            for k in targets(side[1], z):
                spread_job.start_one(k, 0)

        at_each_line(side, start)
        plan.run(grid, order, edges[2], edges[3])

        def end_small(z):
            side_jobs[0].finish(z)
            own(z, 0).wait()

        at_each_line(side, end_small)
        count = small.shape[0]
        total = small_all[pl.ds(0, count), :]
        for s in range(1, shards):
            total = total + small_all[pl.ds(s * count, count), :]
        small_parts[...] = total
        plan.run(grid, order, edges[3], edges[4])

        def spread_on(z):
            for k in targets(side[1], z)[:-1]:
                spread_job.reduce_one(z, k, 0)
            forward(z, side_jobs[1:])

        at_each_line(side, spread_on)
        plan.run(grid, order, edges[4], 1e9)

        def end(z):
            for job in jobs:
                job.finish(z)

        at_each_line(grid, end)

        def put_spread(at, total):
            spread_out[at, :] = total

        def end_rows(z):
            spread_job.total(z, 0, put_spread)
            spread_job.finish(z)
            for i in range(1, m):
                side_jobs[i].finish(z)
                own(z, i).wait()

        at_each_line(side, end_rows)

    scratch = [
        pltpu.VMEM((shards * small.shape[0], small.shape[1]), small.dtype),
        pltpu.VMEM(small.shape, small.dtype),
        pltpu.SemaphoreType.DMA((m,)),
    ]
    for a, kind in zip(values, kinds):
        scratch += Reduce.scratch(grid, a.shape[0], a.shape[1], a.dtype, *kind)
    spread_rows = spread.shape[0] // shards
    scratch += Scatter.buffers(side, spread_rows, spread.shape[1], BF) + Scatter.sems(side, 1)
    for _ in range(m):
        scratch += Gather.sems(side, 1)
    out = pl.pallas_call(
        kernel,
        out_shape=[jax.ShapeDtypeStruct(a.shape, a.dtype) for a in values]
        + [jax.ShapeDtypeStruct((shards * a.shape[0], a.shape[1]), a.dtype) for a in rows]
        + [jax.ShapeDtypeStruct((spread_rows, spread.shape[1]), F32)],
        in_specs=[vmem()] * 3 + [hbm()] * m,
        out_specs=[hbm()] * (2 + m) + [vmem()],
        scratch_shapes=scratch,
        compiler_params=params(number),
        name="sum_and_gather",
    )(across_first, line_first, spread, small, *rows)
    return out[:3], out[3:-1], out[-1]


CHUNK_US = 4.0
PAIR_US = 1.5
HEAD_US = 5.5
TILE_US = 1.5
FORWARD_US = 3.0
EXTRA = 128


def share_of(columns):
    return 4 * columns // 5 // 256 * 256


def expert_rows(normed, cot, chosen, router, gate_rel, up_first, up_rel, down_rel, number):
    grid = grid_of("expert")
    _, lines, width, _ = grid
    size = lines * width
    experts, hidden, columns = gate_rel[0].shape
    shards = len(gate_rel)
    full = shards * hidden
    both = 2 * full
    total_rows = normed.shape[0]
    count = total_rows // size
    pair = width * count
    tile = 256
    half = 512
    wide = 2 * hidden
    extra = EXTRA
    orders = [targets(lines, z) for z in range(lines)]
    out_tiles = columns // tile
    grad_tiles = experts * 3 * full // wide
    out_us, grad_us = 1.3, 2.3

    def kernel(*refs):
        take = Taker(refs)
        normed_hbm, cot_hbm, chosen_hbm, router_ref = take.take(4)
        gate_hbm, up_first_hbm = take.take(shards), take.take(shards)
        up_hbm, down_hbm = take.take(shards), take.take(shards)
        sum_ref, out_hbm = take.take(2)
        grad_hbm = take.take(3)
        normed_v, cot_v, weights, down = take.take(4)
        grads_low, act_low, parts = take.take(3)
        buffers = take.take(3)
        out_stage, grad_stage, d_gates_ref = take.take(3)
        gates_ref, chosen_v = take.take(2)
        load_sems, weight_sems, out_sems, grad_sems = take.take(4)
        job = Scatter(grid, parts, buffers, 1, take.take(6))
        me, z, _ = position(grid)

        def put(at, total):
            sum_ref[at, :] = total

        plan = Plan(lines)
        plan_scatter(
            plan, job, 0, put, None, [(i + 1) * CHUNK_US for i in range(lines)], False
        )
        order = plan.order()
        shard = lax.axis_index("shard")
        near = shard + 1 - 2 * (shard % 2)
        places = [shard, near, (shard + 2) % shards, (near + 2) % shards]

        loads = [
            pltpu.make_async_copy(normed_hbm, normed_v, load_sems.at[0]),
            pltpu.make_async_copy(chosen_hbm, chosen_v, load_sems.at[2]),
            pltpu.make_async_copy(cot_hbm, cot_v, load_sems.at[1]),
        ]
        weight_loads = [[] for _ in range(experts)]
        for j in range(experts):
            for r in range(shards):
                for w, (source, target) in enumerate(
                    (
                        (gate_hbm[r].at[j], weights.at[pl.ds(j * both + r * hidden, hidden)]),
                        (
                            up_hbm[r].at[j - 1]
                            if j
                            else up_first_hbm[r].at[0],
                            weights.at[pl.ds(j * both + full + r * hidden, hidden)],
                        ),
                        (down_hbm[r].at[j], down.at[pl.ds(j * full + r * hidden, hidden)]),
                    )
                ):
                    weight_loads[j].append(
                        pltpu.make_async_copy(source, target, weight_sems.at[j, r, w])
                    )
        for c in loads + weight_loads[0]:
            c.start()
        for j in range(1, experts):
            for c in weight_loads[j]:
                c.start()
        greet([grid])
        for c in loads:
            c.wait()

        lane = lax.broadcasted_iota(jnp.int32, (half, EXTRA), 1)

        @pl.loop(0, total_rows // half)
        def _(m):
            rows = pl.ds(pl.multiple_of(m * half, half), half)
            named = chosen_v[rows, :].astype(F32) > 0.5
            logits = jnp.where(named, dot(normed_v[rows, :], router_ref[...]), -1e30)
            top = jnp.max(logits, axis=-1, keepdims=True)
            powers = jnp.where(named, jnp.exp(logits - top), 0.0)
            probs = powers / jnp.sum(powers, axis=-1, keepdims=True)
            for j in range(experts):
                gates_ref[rows, j : j + 1] = jnp.sum(
                    jnp.where(lane == me * experts + j, probs, 0.0), axis=-1, keepdims=True
                )

        for j in range(experts):
            for c in weight_loads[j]:
                c.wait()

            @pl.loop(0, total_rows // half)
            def _(m):
                rows = pl.ds(pl.multiple_of(m * half, half), half)

                @pl.loop(0, full // tile)
                def _(t):
                    at = t * tile

                    def lines_of(base):
                        return pl.ds(pl.multiple_of(base + at, tile), tile)

                    x = normed_v[rows, :]
                    gate_pre = dot_nt(x, weights[lines_of(j * both), :])
                    up_pre = dot_nt(x, weights[lines_of(j * both + full), :])
                    back = dot_nt(cot_v[rows, :], down[lines_of(j * full), :])
                    probs = gates_ref[rows, j : j + 1]
                    sig = 1.0 / (1.0 + jnp.exp(-gate_pre))
                    silu = gate_pre * sig
                    act = silu * up_pre
                    act_low[rows, lines_of(j * full)] = (act * probs).astype(BF)
                    d_act = back * probs
                    d_gate = d_act * up_pre * (sig * (1.0 + gate_pre * (1.0 - sig)))
                    grads_low[rows, lines_of(j * both)] = d_gate.astype(BF)
                    grads_low[rows, lines_of(j * both + full)] = (d_act * silu).astype(BF)
                    part = jnp.sum(act * back, axis=1, keepdims=True)

                    @pl.when(t == 0)
                    def _():
                        d_gates_ref[rows, j : j + 1] = part

                    @pl.when(t > 0)
                    def _():
                        d_gates_ref[rows, j : j + 1] = d_gates_ref[rows, j : j + 1] + part

        lane = lax.broadcasted_iota(jnp.int32, (count, extra), 1)

        @pl.loop(0, size)
        def _(e):
            rows = pl.ds(pl.multiple_of(e * count, count), count)
            block = jnp.zeros((count, extra), F32)
            for j in range(experts):
                value = d_gates_ref[rows, j : j + 1]
                high = value.astype(BF).astype(F32)
                mine = me * experts + j
                block = jnp.where(lane == mine, high, block)
                block = jnp.where(lane == mine + size * experts, value - high, block)
            parts[rows, columns:] = block.astype(BF)

        @pl.loop(0, lines)
        def _(i):
            k = jnp.int32(0)
            for at in range(lines):
                for step in range(lines):
                    k = jnp.where(jnp.logical_and(z == at, i == step), orders[at][step], k)
            rows = pl.ds(pl.multiple_of(k * pair, pair), pair)

            @pl.loop(0, columns // tile)
            def _(t):
                cols = pl.ds(pl.multiple_of(t * tile, tile), tile)
                value = dot(grads_low[rows, :], weights[:, cols])
                parts[rows, cols] = value.astype(BF)

            job.start_one(k, 0)

        begin = lines * CHUNK_US

        def out_copy(t, slot):
            cols = pl.ds(pl.multiple_of(t * tile, tile), tile)
            return pltpu.make_async_copy(
                out_stage.at[slot], out_hbm.at[:, cols], out_sems.at[slot]
            )

        plan.run(grid, order, -1.0, begin)

        @pl.loop(0, out_tiles)
        def _(t):
            slot = t % 2

            @pl.when(t >= 2)
            def _():
                out_copy(t - 2, slot).wait()

            cols = pl.ds(pl.multiple_of(t * tile, tile), tile)
            out_stage[slot, :, :] = dot(act_low[...], down[:, cols]).astype(BF)
            out_copy(t, slot).start()
            plan.run_step(grid, order, t, begin, out_us, out_tiles)

        begin = begin + out_tiles * out_us

        def grad_copies(kind, j, r, slot):
            copies = []
            for h in range(2):
                place = places[h]
                for step in range(1, shards // 2):
                    place = jnp.where(r == step, places[2 * step + h], place)
                copies.append(
                    pltpu.make_async_copy(
                        grad_stage.at[slot, pl.ds(h * hidden, hidden)],
                        grad_hbm[kind].at[place, j],
                        grad_sems.at[slot, h],
                    )
                )
            return copies

        per = full // wide
        for kind in range(3):

            @pl.loop(0, experts * per)
            def _(i):
                j, r = i // per, i % per
                slot = i % 2
                if kind == 2:
                    low, base, rows_v = act_low, j * full, cot_v
                else:
                    low, base, rows_v = grads_low, j * both + kind * full, normed_v
                lanes = pl.ds(pl.multiple_of(base + r * wide, wide), wide)

                @pl.when(i >= 2)
                def _():
                    for c in grad_copies(kind, (i - 2) // per, (i - 2) % per, slot):
                        c.wait()

                for q in range(2):
                    cols = pl.ds(q * columns // 2, columns // 2)
                    value = dot_tn(low[:, lanes], rows_v[:, cols])
                    grad_stage[slot, :, cols] = value.astype(BF)
                for c in grad_copies(kind, j, r, slot):
                    c.start()
                plan.run_step(grid, order, i, begin, grad_us, experts * per)

            for i in range(max(0, experts * per - 2), experts * per):
                for c in grad_copies(kind, i // per, i % per, i % 2):
                    c.wait()
            begin = begin + experts * per * grad_us

        plan.run(grid, order, begin, 1e9)

        for t in range(max(0, out_tiles - 2), out_tiles):
            out_copy(t, t % 2).wait()
        at_each_line(grid, job.finish)

    dma = pltpu.SemaphoreType.DMA
    weight_shape = jax.ShapeDtypeStruct((shards, experts, hidden, columns), BF)
    return pl.pallas_call(
        kernel,
        out_shape=[
            jax.ShapeDtypeStruct((count, columns + extra), F32),
            jax.ShapeDtypeStruct((total_rows, columns), BF),
            weight_shape,
            weight_shape,
            weight_shape,
        ],
        in_specs=[hbm()] * 3 + [vmem()] + [hbm()] * (4 * shards),
        out_specs=[vmem()] + [hbm()] * 4,
        scratch_shapes=[
            pltpu.VMEM((total_rows, columns), BF),
            pltpu.VMEM((total_rows, columns), BF),
            pltpu.VMEM((experts * both, columns), BF),
            pltpu.VMEM((experts * full, columns), BF),
            pltpu.VMEM((total_rows, experts * both), BF),
            pltpu.VMEM((total_rows, experts * full), BF),
            pltpu.VMEM((total_rows, columns + extra), BF),
        ]
        + Scatter.buffers(grid, count, columns + extra, BF)
        + [
            pltpu.VMEM((2, total_rows, tile), BF),
            pltpu.VMEM((2, wide, columns), BF),
            pltpu.VMEM((total_rows, experts), F32),
            pltpu.VMEM((total_rows, experts), F32),
            pltpu.VMEM((total_rows, EXTRA), BF),
            dma((3,)),
            dma((experts, shards, 3)),
            dma((2,)),
            dma((2, 2)),
        ]
        + Scatter.sems(grid, 1),
        compiler_params=params(number, 63),
        name="expert_rows",
    )(normed, cot, chosen, router, *gate_rel, *up_first, *up_rel, *down_rel)


def rms_forward(vector, gain):
    inverse = lax.rsqrt(jnp.mean(vector * vector, axis=-1, keepdims=True) + EPS)
    return vector * inverse * gain, inverse


def rms_backward(vector, inverse, gain, grad):
    scaled = grad * gain
    inner = jnp.mean(scaled * vector, axis=-1, keepdims=True)
    return inverse * scaled - vector * (inverse * inverse * inverse * inner)


def attention_forward(arrays, cot_own, heads, number):
    grid, side = grid_of("expert"), grid_of("shard")
    size, shards = grid[1] * grid[2], side[1] * side[2]
    names = list(arrays)
    tokens, columns = arrays["rows"].shape
    inner = arrays["query_weight"].shape[1]
    head = inner // heads
    own_rows = tokens // shards
    tile = 256
    scale = head ** (-0.5)
    block = min(256, tokens)

    def kernel(*refs):
        take = Taker(refs)
        hbm_refs = take.take(len(names))
        cot_ref = take.one()
        normed, query_lin, key_lin, query, key, value, mixed, log_total = take.take(8)
        residual, normed_two = take.take(2)
        cot_all = take.one()
        v = dict(zip(names, take.take(len(names))))
        bias, parts, summed = take.take(3)
        buffers = take.take(3)
        load_sems, own_sems = take.take(2)
        job = Scatter(side, parts, buffers, 2, take.take(6))
        cot_job = Gather(grid, cot_ref, cot_all, 2, take.take(4))
        shard = lax.axis_index("shard")
        cot_plan = Plan(grid[1])
        for p in range(2):
            plan_gather(cot_plan, cot_job, p, 0.0)
        cot_order = cot_plan.order()

        def own_cot(z):
            return pltpu.make_async_copy(cot_ref, cot_job.own_slot(z), own_sems.at[0])

        loads = [
            pltpu.make_async_copy(ref, v[name], load_sems.at[i])
            for i, (name, ref) in enumerate(zip(names, hbm_refs))
        ]
        for c in loads:
            c.start()
        at_each_line(grid, lambda z: own_cot(z).start())
        greet([grid, side])
        cot_plan.run(grid, cot_order, 0.0, 2.0)
        for c in loads[:-1]:
            c.wait()

        def norm(value, gain):
            return value * lax.rsqrt(jnp.mean(value * value, axis=-1, keepdims=True) + EPS) * gain

        @pl.loop(0, tokens // 32)
        def _(i):
            rows = pl.ds(pl.multiple_of(i * 32, 32), 32)
            normed[rows, :] = norm(v["rows"][rows, :].astype(F32), v["norm_gain"][...]).astype(BF)

        @pl.loop(0, inner // tile)
        def _(t):
            cols = pl.ds(pl.multiple_of(t * tile, tile), tile)
            query_lin[:, cols] = dot(normed[...], v["query_weight"][:, cols])

        key_lin[...] = dot(normed[...], v["key_weight"][...])
        value[...] = dot(normed[...], v["value_weight"][...]).astype(BF)

        def turn(rows):
            return rows * v["cosine"][...] + pltpu.roll(rows, head // 2, 1) * v["sine"][...]

        key[...] = turn(norm(key_lin[...], v["key_gain"][...])).astype(BF)
        rows_at = lax.broadcasted_iota(jnp.int32, (tokens, tokens), 0)
        cols_at = lax.broadcasted_iota(jnp.int32, (tokens, tokens), 1)
        allowed = jnp.logical_and(v["doc_col"][...] == v["doc_row"][...], rows_at >= cols_at)
        bias[...] = jnp.where(allowed, 0.0, -1e30)

        cot_order_late = [[s for s in steps if s[0] >= 2.0] for steps in cot_order]

        @pl.loop(0, heads)
        def _(h):
            lanes = pl.ds(pl.multiple_of(h * head, head), head)
            query[:, lanes] = turn(norm(query_lin[:, lanes], v["query_gain"][...])).astype(BF)
            for first in range(0, tokens, block):
                rows = pl.ds(first, block)
                keys = pl.ds(0, first + block)
                scores = dot_nt(query[rows, lanes], key[keys, :]) * scale + bias[rows, keys]
                top = jnp.max(scores, axis=-1, keepdims=True)
                powers = jnp.exp(scores - top)
                total = jnp.sum(powers, axis=-1, keepdims=True)
                log_total[h, rows, :] = top + jnp.log(total)
                probs = (powers * (1.0 / total)).astype(BF)
                mixed[rows, lanes] = dot(probs, value[keys, :]).astype(BF)
            cot_plan.run_step(grid, cot_order_late, h, 10.0, FORWARD_US, heads, True)

        loads[-1].wait()

        @pl.loop(0, columns // tile)
        def _(t):
            cols = pl.ds(pl.multiple_of(t * tile, tile), tile)
            parts[:, cols] = dot(mixed[...], v["out_weight"][:, cols]).astype(BF)

        def put(at, total):
            summed[at, :] = total

        plan = Plan(side[1])
        for p in range(2):
            plan_scatter(plan, job, p, put)
        plan.run(side, plan.order(), *ALWAYS)
        cot_plan.run(grid, cot_order, 10.0 + heads * FORWARD_US, 1e9)

        @pl.loop(0, own_rows // 16)
        def _(i):
            rows = pl.ds(pl.multiple_of(i * 16, 16), 16)
            from_rows = pl.ds(pl.multiple_of(shard * own_rows + i * 16, 16), 16)
            total = v["rows"][from_rows, :].astype(F32) + summed[rows, :]
            residual[rows, :] = total
            normed_two[rows, :] = norm(total, v["norm_two_gain"][...]).astype(BF)

        at_each_line(side, job.finish)

        def end_cot(z):
            cot_job.finish(z)
            own_cot(z).wait()

        at_each_line(grid, end_cot)

    values = [arrays[name] for name in names]
    shape = jax.ShapeDtypeStruct
    return pl.pallas_call(
        kernel,
        out_shape=[
            shape((tokens, columns), BF),
            shape((tokens, inner), F32),
            shape((tokens, head), F32),
            shape((tokens, inner), BF),
            shape((tokens, head), BF),
            shape((tokens, head), BF),
            shape((tokens, inner), BF),
            shape((heads, tokens, 1), F32),
            shape((own_rows, columns), F32),
            shape((own_rows, columns), BF),
            shape((size * own_rows, columns), BF),
        ],
        in_specs=[hbm()] * (len(names) + 1),
        out_specs=[vmem()] * 10 + [hbm()],
        scratch_shapes=[pltpu.VMEM(a.shape, a.dtype) for a in values]
        + [
            pltpu.VMEM((tokens, tokens), F32),
            pltpu.VMEM((tokens, columns), BF),
            pltpu.VMEM((own_rows, columns), F32),
        ]
        + Scatter.buffers(side, own_rows, columns, BF)
        + [pltpu.SemaphoreType.DMA((len(names),)), pltpu.SemaphoreType.DMA((1,))]
        + Scatter.sems(side, 2)
        + Gather.sems(grid, 2),
        compiler_params=params(number),
        name="attention_forward",
    )(*values, cot_own)


def attention_backward(arrays, d_own, heads, number):
    grid, side = grid_of("expert"), grid_of("shard")
    _, lines, width, _ = grid
    size = lines * width
    shards = side[1] * side[2]
    names = list(arrays)
    tokens, columns = shards * d_own.shape[0], d_own.shape[1]
    inner = arrays["mixed"].shape[1]
    head = inner // heads
    count = inner // size
    pair = width * count
    tile = 256
    scale = head ** (-0.5)
    block = min(256, tokens)
    orders = [targets(lines, z) for z in range(lines)]
    split = [share_of(columns), columns - share_of(columns)]
    kinds = [(2, False), (1, True)]
    share = share_of(inner + 2 * head)

    def kernel(*refs):
        take = Taker(refs)
        hbm_refs, d_own_ref = take.take(len(names)), take.one()
        grad_refs = take.take(2)
        input_grad_ref, norm_gain_ref, gains_ref = take.take(3)
        sum_refs = take.take(2)
        v = dict(zip(names, take.take(len(names))))
        d_attn, d_mixed, bias, dk, dv, lines_ref, d_norm_ref = take.take(7)
        parts = take.take(2)
        jobs = [
            Reduce(grid, parts[i], sum_refs[i], take.take(Reduce.refs(kinds[i][1])), *kinds[i])
            for i in range(2)
        ]
        side_parts = take.one()
        side_buffers = take.take(3)
        load_sems, own_sems = take.take(2)
        gather = Gather(side, d_own_ref, d_attn, 2, take.take(4))
        side_job = Scatter(side, side_parts, side_buffers, 2, take.take(6))
        me, z, _ = position(grid)
        plan = Plan(lines)
        for job in jobs:
            job.plan(plan, [(i + 1) * PAIR_US for i in range(lines)], False)
        order = plan.order()

        def own(z):
            return pltpu.make_async_copy(d_own_ref, gather.own_slot(z), own_sems.at[0])

        at_each_line(side, lambda z: own(z).start())
        loads = [
            pltpu.make_async_copy(ref, v[name], load_sems.at[i])
            for i, (name, ref) in enumerate(zip(names, hbm_refs))
        ]
        for c in loads:
            c.start()
        greet([grid, side])

        def gather_start(z):
            for p in range(2):
                gather.start(z, p)
            for p in range(2):
                for origin in range(side[1]):
                    if origin != z:
                        gather.forward(z, origin, p)

        at_each_line(side, gather_start)
        for c in loads:
            c.wait()

        rows_at = lax.broadcasted_iota(jnp.int32, (tokens, tokens), 0)
        cols_at = lax.broadcasted_iota(jnp.int32, (tokens, tokens), 1)
        allowed = jnp.logical_and(v["doc_col"][...] == v["doc_row"][...], rows_at >= cols_at)
        bias[...] = jnp.where(allowed, 0.0, -1e30)
        dk[...] = jnp.zeros_like(dk)
        dv[...] = jnp.zeros_like(dv)
        gains_ref[...] = jnp.zeros_like(gains_ref)

        def gather_end(z):
            gather.finish(z)
            own(z).wait()

        at_each_line(side, gather_end)

        @pl.loop(0, lines)
        def _(i):
            k = jnp.int32(0)
            for at in range(lines):
                for step in range(lines):
                    k = jnp.where(jnp.logical_and(z == at, i == step), orders[at][step], k)
            lanes = pl.ds(pl.multiple_of(k * pair, pair), pair)

            rows = pl.ds(pl.multiple_of(k * pair, pair), pair)
            first = 0
            for n in range(2):

                value = dot_tn(v["mixed"][:, lanes], d_attn[:, first : first + split[n]])
                parts[n][rows, :] = value.astype(BF)
                first += split[n]
                for p in range(kinds[n][0]):
                    jobs[n].start_one(k, p)

        @pl.loop(0, inner // tile)
        def _(t):
            rows = pl.ds(pl.multiple_of(t * tile, tile), tile)
            d_mixed[:, rows] = dot_nt(d_attn[...], v["out_weight"][rows, :]).astype(BF)

        def unturn(grad):
            turned = pltpu.roll(grad * v["sine"][...], head // 2, 1)
            return grad * v["cosine"][...] + turned

        def unnorm(grad, linear, gain, row):
            inverse = lax.rsqrt(jnp.mean(linear * linear, axis=-1, keepdims=True) + EPS)
            gains_ref[row : row + 1, :] = gains_ref[row : row + 1, :] + jnp.sum(
                grad * linear * inverse, axis=0, keepdims=True
            )
            return rms_backward(linear, inverse, gain, grad)

        begin = lines * PAIR_US + 3.0

        @pl.loop(0, heads)
        def _(h):
            lanes = pl.ds(pl.multiple_of(h * head, head), head)
            grads = []
            for first in range(0, tokens, block):
                rows = pl.ds(first, block)
                keys = pl.ds(0, first + block)
                query = v["query"][rows, lanes]
                scores = dot_nt(query, v["key"][keys, :])
                probs = jnp.exp(scores * scale + bias[rows, keys] - v["log_total"][h, rows, :])
                back = d_mixed[rows, lanes]
                d_probs = dot_nt(back, v["value"][keys, :])
                inner_sum = jnp.sum(probs * d_probs, axis=-1, keepdims=True)
                d_scores = (probs * (d_probs - inner_sum)).astype(BF)
                dv[keys, :] = dv[keys, :] + dot_tn(probs.astype(BF), back)
                dk[keys, :] = dk[keys, :] + dot_tn(d_scores, query)
                grads.append(dot(d_scores, v["key"][keys, :]))
            grad = jnp.concatenate(grads, axis=0) * scale
            grad = unnorm(unturn(grad), v["query_lin"][:, lanes], v["query_gain"][...], 0)
            lines_ref[:, lanes] = grad.astype(BF)
            plan.run_step(grid, order, h, begin, HEAD_US, heads, True)

        grad = unnorm(unturn(dk[...] * scale), v["key_lin"][...], v["key_gain"][...], 1)
        lines_ref[:, inner : inner + head] = grad.astype(BF)
        lines_ref[:, inner + head : inner + 2 * head] = dv[...].astype(BF)

        @pl.loop(0, columns // tile)
        def _(t):
            rows = pl.ds(pl.multiple_of(t * tile, tile), tile)
            value = dot_nt(lines_ref[:, :inner], v["query_weight"][rows, :])
            value = value + dot_nt(lines_ref[:, inner : inner + head], v["key_weight"][rows, :])
            value = value + dot_nt(lines_ref[:, inner + head :], v["value_weight"][rows, :])
            side_parts[:, rows] = value.astype(BF)

        def put_norm(at, total):
            d_norm_ref[at, :] = total

        side_plan = Plan(side[1])
        for p in range(2):
            plan_scatter(side_plan, side_job, p, put_norm)
        side_order = side_plan.order()

        def side_begin(z):
            for _, act in side_order[z][:-2]:
                act()

        def side_end(z):
            for _, act in side_order[z][-2:]:
                act()

        at_each_line(side, side_begin)
        middle = begin + heads * HEAD_US
        tiles = columns // tile

        @pl.loop(0, tiles)
        def _(t):
            rows = pl.ds(pl.multiple_of(t * tile, tile), tile)
            value = dot_tn(v["normed"][:, rows], lines_ref[...])
            grad_refs[0][rows, :] = value[:, :share].astype(BF)
            grad_refs[1][rows, :] = value[:, share:].astype(BF)
            plan.run_step(grid, order, t, middle, TILE_US, tiles)

        at_each_line(side, side_end)
        plan.run(grid, order, middle + tiles * TILE_US, middle + tiles * TILE_US + 6.0)

        norm_gain_ref[...] = jnp.zeros_like(norm_gain_ref)

        @pl.loop(0, d_own.shape[0] // 16)
        def _(i):
            rows = pl.ds(pl.multiple_of(i * 16, 16), 16)
            value = v["input_own"][rows, :].astype(F32)
            grad = d_norm_ref[rows, :]
            inverse = lax.rsqrt(jnp.mean(value * value, axis=-1, keepdims=True) + EPS)
            norm_gain_ref[0:1, :] = norm_gain_ref[0:1, :] + jnp.sum(
                grad * value * inverse, axis=0, keepdims=True
            )
            back = rms_backward(value, inverse, v["norm_gain"][...], grad)
            input_grad_ref[rows, :] = (v["d_residual"][rows, :] + back).astype(BF)

        plan.run(grid, order, middle + tiles * TILE_US + 6.0, 1e9)

        def end(z):
            for job in jobs:
                job.finish(z)

        at_each_line(grid, end)
        at_each_line(side, side_job.finish)

    dma = pltpu.SemaphoreType.DMA
    values = [arrays[name] for name in names]
    out = pl.pallas_call(
        kernel,
        out_shape=[
            jax.ShapeDtypeStruct((columns, share), BF),
            jax.ShapeDtypeStruct((columns, inner + 2 * head - share), BF),
            jax.ShapeDtypeStruct(d_own.shape, BF),
            jax.ShapeDtypeStruct((8, columns), F32),
            jax.ShapeDtypeStruct((8, head), F32),
            jax.ShapeDtypeStruct((inner, split[0]), BF),
            jax.ShapeDtypeStruct((inner, split[1]), BF),
        ],
        in_specs=[hbm()] * (len(names) + 1),
        out_specs=[vmem()] * 5 + [hbm()] * 2,
        scratch_shapes=[pltpu.VMEM(a.shape, a.dtype) for a in values]
        + [
            pltpu.VMEM((tokens, columns), BF),
            pltpu.VMEM((tokens, inner), BF),
            pltpu.VMEM((tokens, tokens), F32),
            pltpu.VMEM((tokens, head), F32),
            pltpu.VMEM((tokens, head), F32),
            pltpu.VMEM((tokens, inner + 2 * head), BF),
            pltpu.VMEM(d_own.shape, F32),
            pltpu.VMEM((inner, split[0]), BF),
            pltpu.VMEM((inner, split[1]), BF),
        ]
        + Reduce.scratch(grid, inner, split[0], BF, *kinds[0])
        + Reduce.scratch(grid, inner, split[1], BF, *kinds[1])
        + [pltpu.VMEM((tokens, columns), BF)]
        + Scatter.buffers(side, d_own.shape[0], columns, BF)
        + [dma((len(names),)), dma((1,))]
        + Gather.sems(side, 2)
        + Scatter.sems(side, 2),
        compiler_params=params(number),
        name="attention_backward",
    )(*values, d_own)
    first, second, input_grad, norm_gain, gains, *out_sums = out
    out_sum = jnp.concatenate(out_sums, axis=1)
    return (first, second), input_grad, norm_gain[0], gains[0], gains[1], out_sum


def rope_tables(positions, head_size):
    half_size = head_size // 2
    frequency = THETA ** (-2.0 * jnp.arange(half_size, dtype=F32) / head_size)
    angles = positions.astype(F32)[:, None] * frequency[None, :]
    return (jnp.cos(angles), jnp.sin(angles))


def doc_positions(doc_ids):
    row_index = jnp.arange(doc_ids.shape[0], dtype=jnp.int32)
    doc_starts = jnp.concatenate([jnp.ones((1,), jnp.bool_), doc_ids[1:] != doc_ids[:-1]])
    first_row = lax.cummax(jnp.where(doc_starts, row_index, 0), axis=0)
    return row_index - first_row


def from_near(rows, count):
    return lax.ppermute(rows, "shard", [(s, s + 1 - 2 * (s % 2)) for s in range(count)])


def from_far(rows, count):
    return lax.ppermute(rows, "shard", [(s, (s + 2) % count) for s in range(count)])


def local(
    layer_input,
    doc_ids,
    routes,
    norm1_gain,
    query_weight,
    key_matrix,
    value_matrix,
    query_norm_gain,
    key_norm_gain,
    out_weight,
    norm2_gain,
    router_weight,
    gate_weight,
    up_weight,
    down_weight,
    cotangent,
):
    tokens_here, model_width = layer_input.shape
    head_size = query_norm_gain.shape[0]
    heads_here = query_weight.shape[1] // head_size
    experts_all = router_weight.shape[1]
    local_experts, _, hidden_here = gate_weight.shape
    expert_peers = lax.axis_size("expert")
    shard_count = lax.axis_size("shard")
    rows_here = tokens_here // shard_count
    shard_index = lax.axis_index("shard")
    expert_index = lax.axis_index("expert")
    hidden_all = shard_count * local_experts * hidden_here

    def own(rows):
        return lax.dynamic_slice_in_dim(rows, shard_index * rows_here, rows_here, axis=0)

    def gather_weight(weight):
        return lax.all_gather(weight, "shard", axis=0).reshape(hidden_all, model_width)

    fused = expert_peers * rows_here <= VMEM_ROWS
    cot_own = own(cotangent)
    routes_own = own(routes)
    experts = jnp.arange(experts_all, dtype=jnp.int32)
    chosen_own = jnp.any(routes_own[:, :, None] == experts[None, None, :], axis=1)
    gate_weight = jnp.swapaxes(gate_weight, 1, 2)
    up_weight = jnp.swapaxes(up_weight, 1, 2)
    if fused:
        gate_far = from_far(gate_weight, shard_count)
        gate_near = from_near(gate_weight, shard_count)
        first_far = from_far(up_weight[:1], shard_count)
        first_near = from_near(up_weight[:1], shard_count)
    else:
        down_all = gather_weight(down_weight)
        gate_all = gather_weight(gate_weight)
        up_all = gather_weight(up_weight)

    positions = doc_positions(doc_ids)
    cosine_table, sine_values = rope_tables(positions, head_size)
    inner = heads_here * head_size
    shared = dict(
        cosine=jnp.concatenate([cosine_table, cosine_table], axis=1),
        sine=jnp.concatenate([-sine_values, sine_values], axis=1),
        query_gain=query_norm_gain[None, :],
        key_gain=key_norm_gain[None, :],
        doc_col=doc_ids[:, None],
        doc_row=doc_ids[None, :],
        query_weight=query_weight,
        key_weight=key_matrix,
        value_weight=value_matrix,
        norm_gain=norm1_gain[None, :],
    )
    forward = dict(
        rows=layer_input, norm_two_gain=norm2_gain[None, :], **shared, out_weight=out_weight
    )
    normed_one, query_lin, key_lin, query, key, value, mixed, log_total, *rest = (
        attention_forward(forward, cot_own, heads_here, 1)
    )
    residual, normed_two, cot_all = rest
    if fused:
        gate_far, first_far, residual, normed_two = lax.optimization_barrier(
            (gate_far, first_far, residual, normed_two)
        )

    if fused:
        up_late, down_late, normed_two = lax.optimization_barrier(
            (up_weight[1:], down_weight, normed_two)
        )
        up_far, down_far = from_far(up_late, shard_count), from_far(down_late, shard_count)
        up_near, down_near = from_near(up_late, shard_count), from_near(down_late, shard_count)
    _, inverse_two = rms_forward(residual, norm2_gain)
    chosen_wide = jnp.pad(chosen_own.astype(BF), ((0, 0), (0, EXTRA - experts_all)))
    normed_all, chosen_all = gather_rows([normed_two, chosen_wide], [], 2, (2, 1))
    if fused:
        up_far, down_far, normed_all = lax.optimization_barrier((up_far, down_far, normed_all))
        rel = []
        for own_one, near, far in (
            (gate_weight, gate_near, gate_far),
            (up_weight[:1], first_near, first_far),
            (up_late, up_near, up_far),
            (down_late, down_near, down_far),
        ):
            rel.append([own_one, near, far, from_near(far, shard_count)])

    def gate_table(rows, chosen):
        logits = jnp.where(chosen, dot(rows, router_weight), -jnp.inf)
        top = jnp.max(logits, axis=-1, keepdims=True)
        powers = jnp.exp(logits - top)
        return powers / jnp.sum(powers, axis=-1, keepdims=True)

    if fused:
        router_wide = jnp.pad(router_weight, ((0, 0), (0, EXTRA - experts_all)))
        summed, out_part, gate_part, up_part, down_part = expert_rows(
            normed_all, cot_all, chosen_all, router_wide, *rel, 3
        )
        d_rows_own = summed[:, :model_width]
        d_gates_own = (
            summed[:, model_width : model_width + experts_all]
            + summed[:, model_width + experts_all : model_width + 2 * experts_all]
        )
    else:
        gates_here = lax.dynamic_slice_in_dim(
            gate_table(normed_all, chosen_all[:, :experts_all] > 0.5),
            expert_index * local_experts,
            local_experts,
            axis=1,
        )
        column_expert = (jnp.arange(hidden_all, dtype=jnp.int32) // hidden_here) % local_experts
        gate_columns = jnp.zeros((1, 1), F32)
        for j in range(local_experts):
            gate_columns = jnp.where(column_expert[None, :] == j, gates_here[:, j : j + 1], gate_columns)

        d_act_raw = dot_nt(cot_all, down_all)
        gate_pre = dot_nt(normed_all, gate_all)
        up_pre = dot_nt(normed_all, up_all)
        sig = jax.nn.sigmoid(gate_pre)
        silu = gate_pre * sig
        act = silu * up_pre
        act_gated = (act * gate_columns).astype(BF)
        d_act = d_act_raw * gate_columns
        d_gate_low = (d_act * up_pre * sig * (1.0 + gate_pre * (1.0 - sig))).astype(BF)
        d_up_low = (d_act * silu).astype(BF)
        act_back = act * d_act_raw
        d_gates_here = jnp.stack(
            [
                jnp.sum(jnp.where(column_expert[None, :] == j, act_back, 0.0), axis=1)
                for j in range(local_experts)
            ],
            axis=-1,
        )
        d_rows = dot(d_gate_low, gate_all) + dot(d_up_low, up_all)
        d_rows_own = scatter_rows(d_rows.astype(BF), "expert", 3, 2)
        out_part = dot(act_gated, down_all).astype(BF)

        def split(grad):
            return grad.astype(BF).reshape(shard_count, local_experts, hidden_here, model_width)

        gate_part = split(dot_tn(d_gate_low, normed_all))
        up_part = split(dot_tn(d_up_low, normed_all))
        down_part = split(dot_tn(act_gated, cot_all))

        d_gates_own = lax.all_to_all(
            d_gates_here.reshape(expert_peers, rows_here, local_experts),
            "expert",
            split_axis=0,
            concat_axis=0,
            tiled=True,
        )
        d_gates_own = jnp.swapaxes(d_gates_own, 0, 1).reshape(rows_here, experts_all)
    out_own = lax.psum_scatter(out_part, "expert", scatter_dimension=0, tiled=True)
    def scatter_grad(grad):
        return lax.psum_scatter(grad, "shard", scatter_dimension=0, tiled=False)

    gate_grad = jnp.swapaxes(scatter_grad(gate_part).astype(F32), 1, 2)
    up_grad = jnp.swapaxes(scatter_grad(up_part).astype(F32), 1, 2)

    gates_own = gate_table(normed_two, chosen_own)
    d_logits = gates_own * (
        d_gates_own - jnp.sum(gates_own * d_gates_own, axis=-1, keepdims=True)
    )
    d_logits_low = d_logits.astype(BF)
    router_grad = dot_tn(normed_two, d_logits_low)
    d_normed_two = d_rows_own + dot_nt(d_logits_low, router_weight)
    norm2_grad = jnp.sum(d_normed_two * residual * inverse_two, axis=0)
    d_residual = cot_own.astype(F32) + rms_backward(
        residual, inverse_two, norm2_gain, d_normed_two
    )
    backward = dict(
        mixed=mixed,
        query=query,
        key=key,
        value=value,
        query_lin=query_lin,
        key_lin=key_lin,
        log_total=log_total,
        out_weight=out_weight,
        normed=normed_one,
        input_own=own(layer_input),
        d_residual=d_residual,
        **shared,
    )
    line_grads, input_grad_own, norm1_grad, d_query_gain, d_key_gain, out_sum = (
        attention_backward(backward, d_residual.astype(BF), heads_here, 4)
    )
    share = share_of(inner + 2 * head_size)
    out_own, _ = lax.optimization_barrier((out_own, norm1_grad))
    layer_out_own = (residual + out_own).astype(BF)

    flat = jnp.concatenate(
        [router_grad.T.reshape(-1), norm2_grad, norm1_grad, d_query_gain, d_key_gain]
    )
    small_rows = 8 * expert_peers
    small_columns = -(-flat.shape[0] // (128 * small_rows)) * 128
    small = jnp.pad(flat, (0, small_rows * small_columns - flat.shape[0]))
    (line_first, line_second, small), (input_grad, layer_out), down_sum = sum_and_gather(
        *line_grads,
        small.reshape(small_rows, small_columns),
        (input_grad_own, layer_out_own),
        down_part.reshape(hidden_all, model_width),
        5,
    )
    down_grad = down_sum.reshape(local_experts, hidden_here, model_width)
    query_cols = inner - share
    query_sum = jnp.concatenate([line_first, line_second[:, :query_cols]], axis=1)
    key_sum = line_second[:, query_cols : query_cols + head_size]
    value_sum = line_second[:, query_cols + head_size :]
    small = small.reshape(-1)
    bounds = [experts_all * model_width, model_width, model_width, head_size, head_size]
    taken = []
    at = 0
    for bound in bounds:
        taken.append(small[at : at + bound])
        at += bound
    router_sum, norm2_sum, norm1_sum, query_gain_sum, key_gain_sum = taken
    router_sum = router_sum.reshape(experts_all, model_width).T
    return (
        layer_out,
        input_grad,
        norm1_sum,
        query_sum.astype(F32),
        key_sum.astype(F32),
        value_sum.astype(F32),
        query_gain_sum,
        key_gain_sum,
        out_sum.astype(F32),
        norm2_sum,
        router_sum,
        gate_grad,
        up_grad,
        down_grad,
    )


def solution(mesh):
    return jax.shard_map(
        local,
        mesh=mesh,
        in_specs=(
            P("expert", None),
            P("expert"),
            P("expert", None),
            P(),
            P(None, "shard"),
            P(None, "shard"),
            P(None, "shard"),
            P(),
            P(),
            P("shard", None),
            P(),
            P(),
            P("expert", None, "shard"),
            P("expert", None, "shard"),
            P("expert", "shard", None),
            P("expert", None),
        ),
        out_specs=(
            P("expert", None),
            P("expert", None),
            P(),
            P(None, "shard"),
            P(None, "shard"),
            P(None, "shard"),
            P(),
            P(),
            P("shard", None),
            P(),
            P(),
            P("expert", None, "shard"),
            P("expert", None, "shard"),
            P("expert", "shard", None),
        ),
        check_vma=False,
    )
```

```python
import jax
import jax.numpy as jnp
from jax import lax
from jax.experimental import pallas as pl
from jax.experimental.pallas import tpu as pltpu
from jax.sharding import PartitionSpec as P

EPS = 1e-06
THETA = 1000000.0
BF = jnp.bfloat16
F32 = jnp.float32
MESH = pl.DeviceIdType.MESH
VMEM_ROWS = 1024


def dot(a, b):
    return jnp.dot(a, b, preferred_element_type=F32)


def dot_nt(a, b):
    return lax.dot_general(a, b, (((1,), (1,)), ((), ())), preferred_element_type=F32)


def dot_tn(a, b):
    return lax.dot_general(a, b, (((0,), (0,)), ((), ())), preferred_element_type=F32)


LINK_BYTES_PER_US = 1e5


def grid_of(axis):
    size = lax.axis_size(axis)
    lines = 4 if axis == "expert" else 2
    return axis, lines, size // lines, size // lines


def line_of(grid):
    return grid[0], grid[1], 1, grid[3]


def cross_of(grid):
    return grid[0], 1, grid[2], grid[3]


def position(grid):
    axis, lines, width, stride = grid
    me = lax.axis_index(axis)
    return me, me // stride if lines > 1 else 0, me % width if width > 1 else 0


def at_each_line(grid, act):
    _, z, _ = position(grid)
    for at in range(grid[1]):

        @pl.when(z == at)
        def _():
            act(at)


def greet(grids):
    barrier = pltpu.get_barrier_semaphore()
    count = 0
    for grid in grids:
        axis, lines, width, stride = grid
        me, z, b = position(grid)

        def signal(peer):
            pl.semaphore_signal(barrier, inc=1, device_id={axis: peer}, device_id_type=MESH)

        @pl.when(z < lines - 1)
        def _():
            signal(me + stride)

        @pl.when(z > 0)
        def _():
            signal(me - stride)

        for o in range(1, width):
            signal(me - b + (b + o) % width)
        count = count + width - 1
        count = count + (z < lines - 1).astype(jnp.int32) + (z > 0).astype(jnp.int32)
    pl.semaphore_wait(barrier, count)


def slice_of(ref, start, rows):
    if not isinstance(start, int):
        start = pl.multiple_of(start, rows)
    return ref.at[pl.ds(start, rows)]


class Gather:
    def __init__(self, grid, source, out, pieces, sems):
        self.axis, self.lines, self.width, self.stride = grid
        self.source, self.out, self.pieces = source, out, pieces
        self.rows_all = source.shape[0]
        self.rows = self.rows_all // pieces
        self.send_r, self.send_l, self.send_x, self.recv = sems
        self.me, _, self.b = position(grid)
        self.bytes = self.rows * source.shape[1] * jnp.dtype(source.dtype).itemsize

    @staticmethod
    def sems(grid, pieces):
        _, lines, width, _ = grid
        dma = pltpu.SemaphoreType.DMA
        return [
            dma((lines, pieces)),
            dma((lines, pieces)),
            dma((max(1, width - 1), lines, pieces)),
            dma((lines * width, pieces)),
        ]

    def copy(self, slot, p, sem, peer, own=False):
        place = slice_of(self.out, slot * self.rows_all + p * self.rows, self.rows)
        source = slice_of(self.source, p * self.rows, self.rows) if own else place
        return pltpu.make_async_remote_copy(
            src_ref=source,
            dst_ref=place,
            send_sem=sem,
            recv_sem=self.recv.at[slot, p],
            device_id={self.axis: peer},
            device_id_type=MESH,
        )

    def sends(self, z, origin, p):
        slot = origin * self.width + self.b
        own = origin == z
        copies = []
        if origin <= z and z < self.lines - 1:
            sem = self.send_r.at[z - origin, p]
            copies.append(self.copy(slot, p, sem, self.me + self.stride, own))
        if origin >= z and z > 0:
            sem = self.send_l.at[origin - z, p]
            copies.append(self.copy(slot, p, sem, self.me - self.stride, own))
        for o in range(1, self.width):
            peer = self.me - self.b + (self.b + o) % self.width
            copies.append(self.copy(slot, p, self.send_x.at[o - 1, origin, p], peer, own))
        return copies

    def start(self, z, p):
        for c in self.sends(z, z, p):
            c.start()

    def arrived(self, slot, p):
        self.copy(slot, p, self.send_r.at[0, p], self.me).wait_recv()

    def forward(self, z, origin, p):
        self.arrived(origin * self.width + self.b, p)
        for c in self.sends(z, origin, p):
            c.start()

    def arrived_across(self, z, p):
        for o in range(1, self.width):
            self.arrived(z * self.width + (self.b + o) % self.width, p)

    def wait_sends(self, z):
        for p in range(self.pieces):
            for origin in range(self.lines):
                for c in self.sends(z, origin, p):
                    c.wait_send()

    def finish(self, z):
        for p in range(self.pieces):
            for line in range(self.lines):
                self.arrived_across(line, p)
        self.wait_sends(z)

    def own_slot(self, z):
        return slice_of(self.out, (z * self.width + self.b) * self.rows_all, self.rows_all)


class Scatter:
    def __init__(self, grid, parts, buffers, pieces, sems):
        self.axis, self.lines, self.width, self.stride = grid
        self.parts, self.pieces = parts, pieces
        self.cross, self.right, self.left = buffers
        self.rows_all = parts.shape[0] // (self.lines * self.width)
        self.rows = self.rows_all // pieces
        self.cross_send, self.cross_recv, self.r_send, self.r_recv, self.l_send, self.l_recv = sems
        self.me, _, self.b = position(grid)
        self.bytes = self.rows * parts.shape[1] * jnp.dtype(parts.dtype).itemsize

    @staticmethod
    def sems(grid, pieces):
        _, lines, width, _ = grid
        dma = pltpu.SemaphoreType.DMA
        across = (max(1, width - 1), lines, pieces)
        return [dma(across), dma(across)] + [dma((lines, pieces)) for _ in range(4)]

    @staticmethod
    def buffers(grid, rows_all, columns, kind):
        _, lines, width, _ = grid
        line = pltpu.VMEM((lines * rows_all if lines > 1 else 16, columns), kind)
        return [pltpu.VMEM((max(1, width - 1) * lines * rows_all, columns), kind), line, line]

    def start_of(self, slot, p):
        return slot * self.rows_all + p * self.rows

    def cross_copy(self, o, k, p):
        peer = (self.b + o) % self.width
        return pltpu.make_async_remote_copy(
            src_ref=slice_of(self.parts, self.start_of(k * self.width + peer, p), self.rows),
            dst_ref=slice_of(self.cross, self.start_of((o - 1) * self.lines + k, p), self.rows),
            send_sem=self.cross_send.at[o - 1, k, p],
            recv_sem=self.cross_recv.at[o - 1, k, p],
            device_id={self.axis: self.me - self.b + peer},
            device_id_type=MESH,
        )

    def line_copy(self, k, p, rightward):
        into = self.right if rightward else self.left
        at = self.start_of(k, p)
        return pltpu.make_async_remote_copy(
            src_ref=slice_of(self.cross, at, self.rows),
            dst_ref=slice_of(into, at, self.rows),
            send_sem=(self.r_send if rightward else self.l_send).at[k, p],
            recv_sem=(self.r_recv if rightward else self.l_recv).at[k, p],
            device_id={self.axis: self.me + self.stride if rightward else self.me - self.stride},
            device_id_type=MESH,
        )

    def start_one(self, k, p):
        for o in range(1, self.width):
            self.cross_copy(o, k, p).start()

    def add(self, k, p, sources, target):
        block = min(16, self.rows)
        own = self.start_of(k * self.width + self.b, p)

        @pl.loop(0, self.rows // block)
        def _(i):
            def rows_at(start):
                return pl.ds(pl.multiple_of(start + i * block, block), block)

            total = self.parts[rows_at(own), :].astype(F32)
            for o in range(self.width - 1):
                at = rows_at(self.start_of(o * self.lines + k, p))
                total = total + self.cross[at, :].astype(F32)
            for source in sources:
                total = total + source[rows_at(self.start_of(k, p)), :].astype(F32)
            target(rows_at(p * self.rows), total)

    def sources(self, z, k, p):
        found = []
        if k >= z and z > 0:
            self.line_copy(k, p, True).wait_recv()
            found.append(self.right)
        if k <= z and z < self.lines - 1:
            self.line_copy(k, p, False).wait_recv()
            found.append(self.left)
        return found

    def reduce_one(self, z, k, p):
        for o in range(1, self.width):
            self.cross_copy(o, k, p).wait_recv()

        def put(at, total):
            offset = pl.multiple_of(at.start + k * self.rows_all, at.size)
            self.cross[pl.ds(offset, at.size), :] = total.astype(self.cross.dtype)

        self.add(k, p, self.sources(z, k, p), put)
        self.line_copy(k, p, k > z).start()

    def total(self, z, p, target):
        for o in range(1, self.width):
            self.cross_copy(o, z, p).wait_recv()
        self.add(z, p, self.sources(z, z, p), target)

    def finish(self, z):
        for p in range(self.pieces):
            for k in range(self.lines):
                for o in range(1, self.width):
                    self.cross_copy(o, k, p).wait_send()
                if k != z:
                    self.line_copy(k, p, k > z).wait_send()


def targets(lines, z):
    others = sorted((k for k in range(lines) if k != z), key=lambda k: (-abs(k - z), -k))
    return others + [z]


class Plan:
    def __init__(self, lines):
        self.lines = lines
        self.steps = [[] for _ in range(lines)]
        self.jobs = 0

    def job(self):
        self.jobs += 1
        return self.jobs

    def add(self, z, waits, act, sends, begin=0.0):
        self.steps[z].append((begin, waits, act, sends))

    def order(self):
        arrived = [dict() for _ in range(self.lines)]
        free = {}
        clock = [0.0] * self.lines
        left = [list(enumerate(steps)) for steps in self.steps]
        result = [[] for _ in range(self.lines)]
        while any(left):
            best = None
            for z in range(self.lines):
                for i, (begin, waits, act, sends) in left[z]:
                    if all(key in arrived[z] for key in waits):
                        ready = max([begin] + [arrived[z][key] for key in waits])
                        if best is None or (max(ready, clock[z]), ready, z, i) < best[0]:
                            best = ((max(ready, clock[z]), ready, z, i), act, sends)
            (now, _, z, i), act, sends = best
            left[z] = [entry for entry in left[z] if entry[0] != i]
            result[z].append((now, act))
            clock[z] = now + 0.7
            for link, time, to, key in sends:
                start = max(now + 1.0, free.get((z, link), 0.0))
                free[z, link] = start + time
                arrived[to][key] = start + time + 1.0
        return result

    def run(self, grid, result, begin, end):
        def act(z):
            for now, step in result[z]:
                if begin <= now < end:
                    step()

        at_each_line(grid, act)


    def run_step(self, grid, result, index, begin, each, steps, early=False):
        _, z, _ = position(grid)
        for at in range(self.lines):
            for now, step in result[at]:
                due = int((now - begin) // each)
                if early:
                    due = max(0, due)
                if 0 <= due < steps:

                    @pl.when(jnp.logical_and(z == at, index == due))
                    def _():
                        step()


def plan_scatter(plan, scatter, p, put, then=None, begin=0.0, start=True):
    n = plan.job()
    lines, width = scatter.lines, scatter.width
    time = 2 * scatter.bytes / LINK_BYTES_PER_US
    for z in range(lines):
        ready = begin if isinstance(begin, (int, float)) else None
        for i, k in enumerate(targets(lines, z)):
            first = ready if ready is not None else begin[i]
            if width > 1:
                plan.add(
                    z,
                    [],
                    (lambda k=k: scatter.start_one(k, p)) if start else (lambda: None),
                    [("x", time * (width - 1), z, (n, "c", k))],
                    first,
                )
            waits = [(n, "c", k)] if width > 1 else []
            if k >= z and z > 0:
                waits.append((n, "r", k))
            if k <= z and z < lines - 1:
                waits.append((n, "l", k))
            if k > z:
                sends = [("r", time, z + 1, (n, "r", k))]
            elif k < z:
                sends = [("l", time, z - 1, (n, "l", k))]
            else:
                follow, sends = then(z) if then else ((lambda: None), [])

                def last(z=z, follow=follow):
                    scatter.total(z, p, put)
                    follow()

                plan.add(z, waits, last, sends, first)
                continue
            plan.add(z, waits, lambda z=z, k=k: scatter.reduce_one(z, k, p), sends, first)


def gather_sends(gather, n, time, z, origin):
    sends = []
    if origin <= z and z < gather.lines - 1:
        sends.append(("r", time, z + 1, (n, "g", origin)))
    if origin >= z and z > 0:
        sends.append(("l", time, z - 1, (n, "g", origin)))
    if gather.width > 1:
        sends.append(("x", time * (gather.width - 1), z, (n, "gx", origin)))
    return sends


def plan_gather(plan, gather, p, begin=None):
    n = plan.job()
    time = 2 * gather.bytes / LINK_BYTES_PER_US
    for z in range(gather.lines):
        for origin in range(gather.lines):
            if origin != z:
                plan.add(
                    z,
                    [(n, "g", origin)],
                    lambda z=z, origin=origin: gather.forward(z, origin, p),
                    gather_sends(gather, n, time, z, origin),
                )

    def then(z):
        return (lambda: gather.start(z, p)), gather_sends(gather, n, time, z, z)

    if begin is not None:
        for z in range(gather.lines):
            act, sends = then(z)
            plan.add(z, [], act, sends, begin)
    return then


class Reduce:
    def __init__(self, grid, parts, out, scratch, pieces, line_first):
        self.grid, self.parts, self.out = grid, parts, out
        self.line_first = line_first
        self.pieces = pieces
        take = Taker(scratch)
        self.sums = take.one()
        if line_first:
            self.pair_sums, self.pair_all = take.take(2)
            self.first = Scatter(line_of(grid), parts, take.take(3), 1, take.take(6))
            self.second = Scatter(cross_of(grid), self.pair_sums, take.take(3), 1, take.take(6))
            self.third = Gather(cross_of(grid), self.sums, self.pair_all, 1, take.take(4))
            self.fourth = Gather(line_of(grid), self.pair_all, out, 1, take.take(4))
        else:
            self.scatter = Scatter(grid, parts, take.take(3), pieces, take.take(6))
            self.gather = Gather(grid, self.sums, out, pieces, take.take(4))
        self.own_sem = take.one()

    @staticmethod
    def scratch(grid, rows, columns, kind, pieces, line_first):
        _, lines, width, _ = grid
        count = rows // (lines * width)
        shapes = [pltpu.VMEM((count, columns), kind)]
        if line_first:
            line, cross = line_of(grid), cross_of(grid)
            shapes += [pltpu.VMEM((width * count, columns), kind)] * 2
            shapes += Scatter.buffers(line, width * count, columns, kind) + Scatter.sems(line, 1)
            shapes += Scatter.buffers(cross, count, columns, kind) + Scatter.sems(cross, 1)
            shapes += Gather.sems(cross, 1) + Gather.sems(line, 1)
        else:
            shapes += Scatter.buffers(grid, count, columns, kind) + Scatter.sems(grid, pieces)
            shapes += Gather.sems(grid, pieces)
        return shapes + [pltpu.SemaphoreType.DMA]

    @staticmethod
    def refs(line_first):
        return 1 + (2 + 9 + 9 + 8 if line_first else 9 + 4) + 1

    def put(self, at, total):
        self.sums[at, :] = total.astype(self.sums.dtype)

    def put_pair(self, at, total):
        self.pair_sums[at, :] = total.astype(self.pair_sums.dtype)

    def own_copy(self, z):
        if self.line_first:
            return pltpu.make_async_copy(self.pair_all, self.fourth.own_slot(z), self.own_sem)
        return pltpu.make_async_copy(self.sums, self.gather.own_slot(z), self.own_sem)

    def start_one(self, k, p):
        if not self.line_first:
            self.scatter.start_one(k, p)

    def plan(self, plan, begin=0.0, start=True):
        if not self.line_first:
            for p in range(self.pieces):
                then = plan_gather(plan, self.gather, p)
                plan_scatter(plan, self.scatter, p, self.put, then, begin, start)
            return
        n = plan.job()
        time = 2 * self.second.bytes / LINK_BYTES_PER_US * (self.grid[2] - 1)
        along = plan_gather(plan, self.fourth, 0)

        def cross(z):
            return (lambda: self.second.start_one(0, 0)), [("x", time, z, (n, "c"))]

        plan_scatter(plan, self.first, 0, self.put_pair, cross, begin)
        for z in range(self.grid[1]):

            def across(z=z):
                self.second.total(0, 0, self.put)
                self.third.start(0, 0)
                at = pl.multiple_of(self.third.b * self.third.rows_all, self.third.rows_all)
                self.pair_all[pl.ds(at, self.third.rows_all), :] = self.sums[...]

            plan.add(z, [(n, "c")], across, [("x", time, z, (n, "x"))])
            follow, sends = along(z)

            def spread(follow=follow):
                self.third.arrived_across(0, 0)
                follow()

            plan.add(z, [(n, "x")], spread, sends)

    def finish(self, z):
        self.own_copy(z).start()
        if self.line_first:
            self.first.finish(z)
            self.second.finish(0)
            self.third.wait_sends(0)
            self.fourth.finish(z)
        else:
            self.scatter.finish(z)
            self.gather.finish(z)
        self.own_copy(z).wait()


def hbm():
    return pl.BlockSpec(memory_space=pl.ANY)


def vmem():
    return pl.BlockSpec(memory_space=pltpu.VMEM)


def params(number, mib=56):
    return pltpu.CompilerParams(
        collective_id=number, has_side_effects=True, vmem_limit_bytes=mib * 1024 * 1024
    )


class Taker:
    def __init__(self, refs):
        self.refs = list(refs)

    def take(self, count):
        taken = self.refs[:count]
        del self.refs[:count]
        return taken

    def one(self):
        return self.take(1)[0]


ALWAYS = (0.0, 1e9)


def gather_rows(arrays, side_arrays, number, pieces):
    grid, side = grid_of("expert"), grid_of("shard")
    values = list(arrays) + list(side_arrays)
    grids = [grid] * len(arrays) + [side] * len(side_arrays)
    n = len(values)

    def kernel(*refs):
        take = Taker(refs)
        ins, outs, own_sems = take.take(n), take.take(n), take.one()
        jobs = [Gather(grids[i], ins[i], outs[i], pieces[i], take.take(4)) for i in range(n)]

        def own(i, z):
            return pltpu.make_async_copy(ins[i], jobs[i].own_slot(z), own_sems.at[i])

        def each(i, act):
            at_each_line(grids[i], act)

        for i in range(n):
            each(i, lambda z, i=i: own(i, z).start())
        greet([grid] + ([side] if side_arrays else []))
        plan = Plan(grid[1])
        for i in range(len(arrays)):
            for p in range(pieces[i]):
                plan_gather(plan, jobs[i], p, 0.0)
        order = plan.order()
        plan.run(grid, order, 0.0, 1.0)
        late = 0.0 if not side_arrays else 1.0
        for i in range(len(arrays), n):
            for p in range(pieces[i]):
                each(i, lambda z, i=i, p=p: jobs[i].start(z, p))
        if side_arrays:
            edge = 2 * jobs[-1].bytes / LINK_BYTES_PER_US + 4.0
            begin = late
            for p in range(pieces[-1]):
                plan.run(grid, order, begin, edge * (p + 1))
                begin = edge * (p + 1)
                for i in range(len(arrays), n):

                    def forward(z, i=i, p=p):
                        for origin in range(grids[i][1]):
                            if origin != z:
                                jobs[i].forward(z, origin, p)

                    each(i, forward)
            plan.run(grid, order, begin, 1e9)
        else:
            plan.run(grid, order, 1.0, 1e9)
        for i in range(n):
            each(i, lambda z, i=i: jobs[i].finish(z))
            each(i, lambda z, i=i: own(i, z).wait())

    scratch = [pltpu.SemaphoreType.DMA((n,))]
    for g, p in zip(grids, pieces):
        scratch += Gather.sems(g, p)
    return pl.pallas_call(
        kernel,
        out_shape=[
            jax.ShapeDtypeStruct((g[1] * g[2] * a.shape[0], a.shape[1]), a.dtype)
            for a, g in zip(values, grids)
        ],
        in_specs=[hbm()] * n,
        out_specs=[hbm()] * n,
        scratch_shapes=scratch,
        compiler_params=params(number),
        name="gather_rows",
    )(*values)


def scatter_rows(parts, axis, number, pieces):
    grid = grid_of(axis)
    columns = parts.shape[1]
    count = parts.shape[0] // (grid[1] * grid[2])

    def kernel(parts_ref, out_ref, cross, right, left, *sems):
        greet([grid])
        job = Scatter(grid, parts_ref, (cross, right, left), pieces, sems)

        def put(at, total):
            out_ref[at, :] = total

        plan = Plan(grid[1])
        for p in range(pieces):
            plan_scatter(plan, job, p, put)
        plan.run(grid, plan.order(), *ALWAYS)
        at_each_line(grid, job.finish)

    return pl.pallas_call(
        kernel,
        out_shape=jax.ShapeDtypeStruct((count, columns), F32),
        in_specs=[vmem()],
        out_specs=vmem(),
        scratch_shapes=Scatter.buffers(grid, count, columns, parts.dtype)
        + Scatter.sems(grid, pieces),
        compiler_params=params(number),
        name="scatter_" + axis,
    )(parts)


def sum_and_gather(across_first, line_first, small, rows, spread, number):
    grid, side = grid_of("expert"), grid_of("shard")
    size = grid[1] * grid[2]
    shards = side[1] * side[2]
    values = [across_first, line_first, small]
    moved = [small] + list(rows)
    m = len(moved)
    kinds = [(2, False), (1, True), (1, False)]

    def kernel(*refs):
        take = Taker(refs)
        first_ref, second_ref, spread_ref = take.take(3)
        side_ins = take.take(m)
        outs, rows_outs, spread_out = take.take(3), take.take(m - 1), take.one()
        small_all, small_parts, own_sems = take.take(3)
        ins = [first_ref, second_ref, small_parts]
        jobs = [
            Reduce(grid, ins[i], outs[i], take.take(Reduce.refs(kinds[i][1])), *kinds[i])
            for i in range(3)
        ]
        spread_job = Scatter(side, spread_ref, take.take(3), 1, take.take(6))
        side_outs = [small_all] + rows_outs
        side_jobs = [Gather(side, side_ins[i], side_outs[i], 1, take.take(4)) for i in range(m)]

        def own(z, i):
            return pltpu.make_async_copy(side_ins[i], side_jobs[i].own_slot(z), own_sems.at[i])

        def begin_side(z):
            for i in range(m):
                own(z, i).start()

        at_each_line(side, begin_side)
        greet([grid, side])
        edges = [0.0, 6.0, 16.0, 28.0, 55.0]
        plan = Plan(grid[1])
        jobs[1].plan(plan)
        jobs[0].plan(plan)
        jobs[2].plan(plan, edges[3])
        order = plan.order()
        plan.run(grid, order, 0.0, edges[1])
        at_each_line(side, lambda z: side_jobs[0].start(z, 0))
        plan.run(grid, order, edges[1], edges[2])

        def forward(z, chosen):
            for origin in range(side[1]):
                if origin != z:
                    for job in chosen:
                        job.forward(z, origin, 0)

        def start(z):
            forward(z, side_jobs[:1])
            for job in side_jobs[1:]:
                job.start(z, 0)
            for k in targets(side[1], z):
                spread_job.start_one(k, 0)

        at_each_line(side, start)
        plan.run(grid, order, edges[2], edges[3])

        def end_small(z):
            side_jobs[0].finish(z)
            own(z, 0).wait()

        at_each_line(side, end_small)
        count = small.shape[0]
        total = small_all[pl.ds(0, count), :]
        for s in range(1, shards):
            total = total + small_all[pl.ds(s * count, count), :]
        small_parts[...] = total
        plan.run(grid, order, edges[3], edges[4])

        def spread_on(z):
            for k in targets(side[1], z)[:-1]:
                spread_job.reduce_one(z, k, 0)
            forward(z, side_jobs[1:])

        at_each_line(side, spread_on)
        plan.run(grid, order, edges[4], 1e9)

        def end(z):
            for job in jobs:
                job.finish(z)

        at_each_line(grid, end)

        def put_spread(at, total):
            spread_out[at, :] = total

        def end_rows(z):
            spread_job.total(z, 0, put_spread)
            spread_job.finish(z)
            for i in range(1, m):
                side_jobs[i].finish(z)
                own(z, i).wait()

        at_each_line(side, end_rows)

    scratch = [
        pltpu.VMEM((shards * small.shape[0], small.shape[1]), small.dtype),
        pltpu.VMEM(small.shape, small.dtype),
        pltpu.SemaphoreType.DMA((m,)),
    ]
    for a, kind in zip(values, kinds):
        scratch += Reduce.scratch(grid, a.shape[0], a.shape[1], a.dtype, *kind)
    spread_rows = spread.shape[0] // shards
    scratch += Scatter.buffers(side, spread_rows, spread.shape[1], BF) + Scatter.sems(side, 1)
    for _ in range(m):
        scratch += Gather.sems(side, 1)
    out = pl.pallas_call(
        kernel,
        out_shape=[jax.ShapeDtypeStruct(a.shape, a.dtype) for a in values]
        + [jax.ShapeDtypeStruct((shards * a.shape[0], a.shape[1]), a.dtype) for a in rows]
        + [jax.ShapeDtypeStruct((spread_rows, spread.shape[1]), F32)],
        in_specs=[vmem()] * 3 + [hbm()] * m,
        out_specs=[hbm()] * (2 + m) + [vmem()],
        scratch_shapes=scratch,
        compiler_params=params(number),
        name="sum_and_gather",
    )(across_first, line_first, spread, small, *rows)
    return out[:3], out[3:-1], out[-1]


CHUNK_US = 4.0
PAIR_US = 1.5
HEAD_US = 5.5
TILE_US = 1.5
EXTRA = 128


def share_of(columns):
    return 4 * columns // 5 // 256 * 256


def expert_rows(normed, cot, chosen, router, gate_rel, up_first, up_rel, down_rel, number):
    grid = grid_of("expert")
    _, lines, width, _ = grid
    size = lines * width
    experts, hidden, columns = gate_rel[0].shape
    shards = len(gate_rel)
    full = shards * hidden
    both = 2 * full
    total_rows = normed.shape[0]
    count = total_rows // size
    pair = width * count
    tile = 256
    half = 512
    wide = 2 * hidden
    extra = EXTRA
    orders = [targets(lines, z) for z in range(lines)]
    out_tiles = columns // tile
    grad_tiles = experts * 3 * full // wide
    out_us, grad_us = 1.3, 2.3

    def kernel(*refs):
        take = Taker(refs)
        normed_hbm, cot_hbm, chosen_hbm, router_ref = take.take(4)
        gate_hbm, up_first_hbm = take.take(shards), take.take(shards)
        up_hbm, down_hbm = take.take(shards), take.take(shards)
        sum_ref, out_hbm = take.take(2)
        grad_hbm = take.take(3)
        normed_v, cot_v, weights, down = take.take(4)
        grads_low, act_low, parts = take.take(3)
        buffers = take.take(3)
        out_stage, grad_stage, d_gates_ref = take.take(3)
        gates_ref, chosen_v = take.take(2)
        load_sems, weight_sems, out_sems, grad_sems = take.take(4)
        job = Scatter(grid, parts, buffers, 1, take.take(6))
        me, z, _ = position(grid)

        def put(at, total):
            sum_ref[at, :] = total

        plan = Plan(lines)
        plan_scatter(
            plan, job, 0, put, None, [(i + 1) * CHUNK_US for i in range(lines)], False
        )
        order = plan.order()
        shard = lax.axis_index("shard")
        near = shard + 1 - 2 * (shard % 2)
        places = [shard, near, (shard + 2) % shards, (near + 2) % shards]

        loads = [
            pltpu.make_async_copy(normed_hbm, normed_v, load_sems.at[0]),
            pltpu.make_async_copy(chosen_hbm, chosen_v, load_sems.at[2]),
            pltpu.make_async_copy(cot_hbm, cot_v, load_sems.at[1]),
        ]
        weight_loads = [[] for _ in range(experts)]
        for j in range(experts):
            for r in range(shards):
                for w, (source, target) in enumerate(
                    (
                        (gate_hbm[r].at[j], weights.at[pl.ds(j * both + r * hidden, hidden)]),
                        (
                            up_hbm[r].at[j - 1]
                            if j
                            else up_first_hbm[r].at[0],
                            weights.at[pl.ds(j * both + full + r * hidden, hidden)],
                        ),
                        (down_hbm[r].at[j], down.at[pl.ds(j * full + r * hidden, hidden)]),
                    )
                ):
                    weight_loads[j].append(
                        pltpu.make_async_copy(source, target, weight_sems.at[j, r, w])
                    )
        for c in loads + weight_loads[0]:
            c.start()
        for j in range(1, experts):
            for c in weight_loads[j]:
                c.start()
        greet([grid])
        for c in loads:
            c.wait()

        lane = lax.broadcasted_iota(jnp.int32, (half, EXTRA), 1)

        @pl.loop(0, total_rows // half)
        def _(m):
            rows = pl.ds(pl.multiple_of(m * half, half), half)
            named = chosen_v[rows, :].astype(F32) > 0.5
            logits = jnp.where(named, dot(normed_v[rows, :], router_ref[...]), -1e30)
            top = jnp.max(logits, axis=-1, keepdims=True)
            powers = jnp.where(named, jnp.exp(logits - top), 0.0)
            probs = powers / jnp.sum(powers, axis=-1, keepdims=True)
            for j in range(experts):
                gates_ref[rows, j : j + 1] = jnp.sum(
                    jnp.where(lane == me * experts + j, probs, 0.0), axis=-1, keepdims=True
                )

        for j in range(experts):
            for c in weight_loads[j]:
                c.wait()

            @pl.loop(0, total_rows // half)
            def _(m):
                rows = pl.ds(pl.multiple_of(m * half, half), half)

                @pl.loop(0, full // tile)
                def _(t):
                    at = t * tile

                    def lines_of(base):
                        return pl.ds(pl.multiple_of(base + at, tile), tile)

                    x = normed_v[rows, :]
                    gate_pre = dot_nt(x, weights[lines_of(j * both), :])
                    up_pre = dot_nt(x, weights[lines_of(j * both + full), :])
                    back = dot_nt(cot_v[rows, :], down[lines_of(j * full), :])
                    probs = gates_ref[rows, j : j + 1]
                    sig = 1.0 / (1.0 + jnp.exp(-gate_pre))
                    silu = gate_pre * sig
                    act = silu * up_pre
                    act_low[rows, lines_of(j * full)] = (act * probs).astype(BF)
                    d_act = back * probs
                    d_gate = d_act * up_pre * (sig * (1.0 + gate_pre * (1.0 - sig)))
                    grads_low[rows, lines_of(j * both)] = d_gate.astype(BF)
                    grads_low[rows, lines_of(j * both + full)] = (d_act * silu).astype(BF)
                    part = jnp.sum(act * back, axis=1, keepdims=True)

                    @pl.when(t == 0)
                    def _():
                        d_gates_ref[rows, j : j + 1] = part

                    @pl.when(t > 0)
                    def _():
                        d_gates_ref[rows, j : j + 1] = d_gates_ref[rows, j : j + 1] + part

        lane = lax.broadcasted_iota(jnp.int32, (count, extra), 1)

        @pl.loop(0, size)
        def _(e):
            rows = pl.ds(pl.multiple_of(e * count, count), count)
            block = jnp.zeros((count, extra), F32)
            for j in range(experts):
                value = d_gates_ref[rows, j : j + 1]
                high = value.astype(BF).astype(F32)
                mine = me * experts + j
                block = jnp.where(lane == mine, high, block)
                block = jnp.where(lane == mine + size * experts, value - high, block)
            parts[rows, columns:] = block.astype(BF)

        @pl.loop(0, lines)
        def _(i):
            k = jnp.int32(0)
            for at in range(lines):
                for step in range(lines):
                    k = jnp.where(jnp.logical_and(z == at, i == step), orders[at][step], k)
            rows = pl.ds(pl.multiple_of(k * pair, pair), pair)

            @pl.loop(0, columns // tile)
            def _(t):
                cols = pl.ds(pl.multiple_of(t * tile, tile), tile)
                value = dot(grads_low[rows, :], weights[:, cols])
                parts[rows, cols] = value.astype(BF)

            job.start_one(k, 0)

        begin = lines * CHUNK_US

        def out_copy(t, slot):
            cols = pl.ds(pl.multiple_of(t * tile, tile), tile)
            return pltpu.make_async_copy(
                out_stage.at[slot], out_hbm.at[:, cols], out_sems.at[slot]
            )

        plan.run(grid, order, -1.0, begin)

        @pl.loop(0, out_tiles)
        def _(t):
            slot = t % 2

            @pl.when(t >= 2)
            def _():
                out_copy(t - 2, slot).wait()

            cols = pl.ds(pl.multiple_of(t * tile, tile), tile)
            out_stage[slot, :, :] = dot(act_low[...], down[:, cols]).astype(BF)
            out_copy(t, slot).start()
            plan.run_step(grid, order, t, begin, out_us, out_tiles)

        begin = begin + out_tiles * out_us

        def grad_copies(kind, j, r, slot):
            copies = []
            for h in range(2):
                place = places[h]
                for step in range(1, shards // 2):
                    place = jnp.where(r == step, places[2 * step + h], place)
                copies.append(
                    pltpu.make_async_copy(
                        grad_stage.at[slot, pl.ds(h * hidden, hidden)],
                        grad_hbm[kind].at[place, j],
                        grad_sems.at[slot, h],
                    )
                )
            return copies

        per = full // wide
        for kind in range(3):

            @pl.loop(0, experts * per)
            def _(i):
                j, r = i // per, i % per
                slot = i % 2
                if kind == 2:
                    low, base, rows_v = act_low, j * full, cot_v
                else:
                    low, base, rows_v = grads_low, j * both + kind * full, normed_v
                lanes = pl.ds(pl.multiple_of(base + r * wide, wide), wide)

                @pl.when(i >= 2)
                def _():
                    for c in grad_copies(kind, (i - 2) // per, (i - 2) % per, slot):
                        c.wait()

                for q in range(2):
                    cols = pl.ds(q * columns // 2, columns // 2)
                    value = dot_tn(low[:, lanes], rows_v[:, cols])
                    grad_stage[slot, :, cols] = value.astype(BF)
                for c in grad_copies(kind, j, r, slot):
                    c.start()
                plan.run_step(grid, order, i, begin, grad_us, experts * per)

            for i in range(max(0, experts * per - 2), experts * per):
                for c in grad_copies(kind, i // per, i % per, i % 2):
                    c.wait()
            begin = begin + experts * per * grad_us

        plan.run(grid, order, begin, 1e9)

        for t in range(max(0, out_tiles - 2), out_tiles):
            out_copy(t, t % 2).wait()
        at_each_line(grid, job.finish)

    dma = pltpu.SemaphoreType.DMA
    weight_shape = jax.ShapeDtypeStruct((shards, experts, hidden, columns), BF)
    return pl.pallas_call(
        kernel,
        out_shape=[
            jax.ShapeDtypeStruct((count, columns + extra), F32),
            jax.ShapeDtypeStruct((total_rows, columns), BF),
            weight_shape,
            weight_shape,
            weight_shape,
        ],
        in_specs=[hbm()] * 3 + [vmem()] + [hbm()] * (4 * shards),
        out_specs=[vmem()] + [hbm()] * 4,
        scratch_shapes=[
            pltpu.VMEM((total_rows, columns), BF),
            pltpu.VMEM((total_rows, columns), BF),
            pltpu.VMEM((experts * both, columns), BF),
            pltpu.VMEM((experts * full, columns), BF),
            pltpu.VMEM((total_rows, experts * both), BF),
            pltpu.VMEM((total_rows, experts * full), BF),
            pltpu.VMEM((total_rows, columns + extra), BF),
        ]
        + Scatter.buffers(grid, count, columns + extra, BF)
        + [
            pltpu.VMEM((2, total_rows, tile), BF),
            pltpu.VMEM((2, wide, columns), BF),
            pltpu.VMEM((total_rows, experts), F32),
            pltpu.VMEM((total_rows, experts), F32),
            pltpu.VMEM((total_rows, EXTRA), BF),
            dma((3,)),
            dma((experts, shards, 3)),
            dma((2,)),
            dma((2, 2)),
        ]
        + Scatter.sems(grid, 1),
        compiler_params=params(number, 63),
        name="expert_rows",
    )(normed, cot, chosen, router, *gate_rel, *up_first, *up_rel, *down_rel)


def rms_forward(vector, gain):
    inverse = lax.rsqrt(jnp.mean(vector * vector, axis=-1, keepdims=True) + EPS)
    return vector * inverse * gain, inverse


def rms_backward(vector, inverse, gain, grad):
    scaled = grad * gain
    inner = jnp.mean(scaled * vector, axis=-1, keepdims=True)
    return inverse * scaled - vector * (inverse * inverse * inverse * inner)


def attention_forward(arrays, heads, number):
    side = grid_of("shard")
    shards = side[1] * side[2]
    names = list(arrays)
    tokens, columns = arrays["rows"].shape
    inner = arrays["query_weight"].shape[1]
    head = inner // heads
    own_rows = tokens // shards
    tile = 256
    scale = head ** (-0.5)
    block = min(256, tokens)

    def kernel(*refs):
        take = Taker(refs)
        hbm_refs = take.take(len(names))
        normed, query_lin, key_lin, query, key, value, mixed, log_total = take.take(8)
        residual, normed_two = take.take(2)
        v = dict(zip(names, take.take(len(names))))
        bias, parts, summed = take.take(3)
        buffers = take.take(3)
        load_sems = take.one()
        job = Scatter(side, parts, buffers, 2, take.take(6))
        shard = lax.axis_index("shard")
        loads = [
            pltpu.make_async_copy(ref, v[name], load_sems.at[i])
            for i, (name, ref) in enumerate(zip(names, hbm_refs))
        ]
        for c in loads:
            c.start()
        greet([side])
        for c in loads[:-1]:
            c.wait()

        def norm(value, gain):
            return value * lax.rsqrt(jnp.mean(value * value, axis=-1, keepdims=True) + EPS) * gain

        @pl.loop(0, tokens // 32)
        def _(i):
            rows = pl.ds(pl.multiple_of(i * 32, 32), 32)
            normed[rows, :] = norm(v["rows"][rows, :].astype(F32), v["norm_gain"][...]).astype(BF)

        @pl.loop(0, inner // tile)
        def _(t):
            cols = pl.ds(pl.multiple_of(t * tile, tile), tile)
            query_lin[:, cols] = dot(normed[...], v["query_weight"][:, cols])

        key_lin[...] = dot(normed[...], v["key_weight"][...])
        value[...] = dot(normed[...], v["value_weight"][...]).astype(BF)

        def turn(rows):
            return rows * v["cosine"][...] + pltpu.roll(rows, head // 2, 1) * v["sine"][...]

        key[...] = turn(norm(key_lin[...], v["key_gain"][...])).astype(BF)
        rows_at = lax.broadcasted_iota(jnp.int32, (tokens, tokens), 0)
        cols_at = lax.broadcasted_iota(jnp.int32, (tokens, tokens), 1)
        allowed = jnp.logical_and(v["doc_col"][...] == v["doc_row"][...], rows_at >= cols_at)
        bias[...] = jnp.where(allowed, 0.0, -1e30)

        @pl.loop(0, heads)
        def _(h):
            lanes = pl.ds(pl.multiple_of(h * head, head), head)
            query[:, lanes] = turn(norm(query_lin[:, lanes], v["query_gain"][...])).astype(BF)
            for first in range(0, tokens, block):
                rows = pl.ds(first, block)
                keys = pl.ds(0, first + block)
                scores = dot_nt(query[rows, lanes], key[keys, :]) * scale + bias[rows, keys]
                top = jnp.max(scores, axis=-1, keepdims=True)
                powers = jnp.exp(scores - top)
                total = jnp.sum(powers, axis=-1, keepdims=True)
                log_total[h, rows, :] = top + jnp.log(total)
                probs = (powers * (1.0 / total)).astype(BF)
                mixed[rows, lanes] = dot(probs, value[keys, :]).astype(BF)

        loads[-1].wait()

        @pl.loop(0, columns // tile)
        def _(t):
            cols = pl.ds(pl.multiple_of(t * tile, tile), tile)
            parts[:, cols] = dot(mixed[...], v["out_weight"][:, cols]).astype(BF)

        def put(at, total):
            summed[at, :] = total

        plan = Plan(side[1])
        for p in range(2):
            plan_scatter(plan, job, p, put)
        plan.run(side, plan.order(), *ALWAYS)

        @pl.loop(0, own_rows // 16)
        def _(i):
            rows = pl.ds(pl.multiple_of(i * 16, 16), 16)
            from_rows = pl.ds(pl.multiple_of(shard * own_rows + i * 16, 16), 16)
            total = v["rows"][from_rows, :].astype(F32) + summed[rows, :]
            residual[rows, :] = total
            normed_two[rows, :] = norm(total, v["norm_two_gain"][...]).astype(BF)

        at_each_line(side, job.finish)

    values = [arrays[name] for name in names]
    shape = jax.ShapeDtypeStruct
    return pl.pallas_call(
        kernel,
        out_shape=[
            shape((tokens, columns), BF),
            shape((tokens, inner), F32),
            shape((tokens, head), F32),
            shape((tokens, inner), BF),
            shape((tokens, head), BF),
            shape((tokens, head), BF),
            shape((tokens, inner), BF),
            shape((heads, tokens, 1), F32),
            shape((own_rows, columns), F32),
            shape((own_rows, columns), BF),
        ],
        in_specs=[hbm()] * len(names),
        out_specs=[vmem()] * 10,
        scratch_shapes=[pltpu.VMEM(a.shape, a.dtype) for a in values]
        + [
            pltpu.VMEM((tokens, tokens), F32),
            pltpu.VMEM((tokens, columns), BF),
            pltpu.VMEM((own_rows, columns), F32),
        ]
        + Scatter.buffers(side, own_rows, columns, BF)
        + [pltpu.SemaphoreType.DMA((len(names),))]
        + Scatter.sems(side, 2),
        compiler_params=params(number),
        name="attention_forward",
    )(*values)


def attention_backward(arrays, d_own, heads, number):
    grid, side = grid_of("expert"), grid_of("shard")
    _, lines, width, _ = grid
    size = lines * width
    shards = side[1] * side[2]
    names = list(arrays)
    tokens, columns = shards * d_own.shape[0], d_own.shape[1]
    inner = arrays["mixed"].shape[1]
    head = inner // heads
    count = inner // size
    pair = width * count
    tile = 256
    scale = head ** (-0.5)
    block = min(256, tokens)
    orders = [targets(lines, z) for z in range(lines)]
    split = [share_of(columns), columns - share_of(columns)]
    kinds = [(2, False), (1, True)]
    share = share_of(inner + 2 * head)

    def kernel(*refs):
        take = Taker(refs)
        hbm_refs, d_own_ref = take.take(len(names)), take.one()
        grad_refs = take.take(2)
        input_grad_ref, norm_gain_ref, gains_ref = take.take(3)
        sum_refs = take.take(2)
        v = dict(zip(names, take.take(len(names))))
        d_attn, d_mixed, bias, dk, dv, lines_ref, d_norm_ref = take.take(7)
        parts = take.take(2)
        jobs = [
            Reduce(grid, parts[i], sum_refs[i], take.take(Reduce.refs(kinds[i][1])), *kinds[i])
            for i in range(2)
        ]
        side_parts = take.one()
        side_buffers = take.take(3)
        load_sems, own_sems = take.take(2)
        gather = Gather(side, d_own_ref, d_attn, 2, take.take(4))
        side_job = Scatter(side, side_parts, side_buffers, 2, take.take(6))
        me, z, _ = position(grid)
        plan = Plan(lines)
        for job in jobs:
            job.plan(plan, [(i + 1) * PAIR_US for i in range(lines)], False)
        order = plan.order()

        def own(z):
            return pltpu.make_async_copy(d_own_ref, gather.own_slot(z), own_sems.at[0])

        at_each_line(side, lambda z: own(z).start())
        loads = [
            pltpu.make_async_copy(ref, v[name], load_sems.at[i])
            for i, (name, ref) in enumerate(zip(names, hbm_refs))
        ]
        for c in loads:
            c.start()
        greet([grid, side])

        def gather_start(z):
            for p in range(2):
                gather.start(z, p)
            for p in range(2):
                for origin in range(side[1]):
                    if origin != z:
                        gather.forward(z, origin, p)

        at_each_line(side, gather_start)
        for c in loads:
            c.wait()

        rows_at = lax.broadcasted_iota(jnp.int32, (tokens, tokens), 0)
        cols_at = lax.broadcasted_iota(jnp.int32, (tokens, tokens), 1)
        allowed = jnp.logical_and(v["doc_col"][...] == v["doc_row"][...], rows_at >= cols_at)
        bias[...] = jnp.where(allowed, 0.0, -1e30)
        dk[...] = jnp.zeros_like(dk)
        dv[...] = jnp.zeros_like(dv)
        gains_ref[...] = jnp.zeros_like(gains_ref)

        def gather_end(z):
            gather.finish(z)
            own(z).wait()

        at_each_line(side, gather_end)

        @pl.loop(0, lines)
        def _(i):
            k = jnp.int32(0)
            for at in range(lines):
                for step in range(lines):
                    k = jnp.where(jnp.logical_and(z == at, i == step), orders[at][step], k)
            lanes = pl.ds(pl.multiple_of(k * pair, pair), pair)

            rows = pl.ds(pl.multiple_of(k * pair, pair), pair)
            first = 0
            for n in range(2):

                value = dot_tn(v["mixed"][:, lanes], d_attn[:, first : first + split[n]])
                parts[n][rows, :] = value.astype(BF)
                first += split[n]
                for p in range(kinds[n][0]):
                    jobs[n].start_one(k, p)

        @pl.loop(0, inner // tile)
        def _(t):
            rows = pl.ds(pl.multiple_of(t * tile, tile), tile)
            d_mixed[:, rows] = dot_nt(d_attn[...], v["out_weight"][rows, :]).astype(BF)

        def unturn(grad):
            turned = pltpu.roll(grad * v["sine"][...], head // 2, 1)
            return grad * v["cosine"][...] + turned

        def unnorm(grad, linear, gain, row):
            inverse = lax.rsqrt(jnp.mean(linear * linear, axis=-1, keepdims=True) + EPS)
            gains_ref[row : row + 1, :] = gains_ref[row : row + 1, :] + jnp.sum(
                grad * linear * inverse, axis=0, keepdims=True
            )
            return rms_backward(linear, inverse, gain, grad)

        begin = lines * PAIR_US + 3.0

        @pl.loop(0, heads)
        def _(h):
            lanes = pl.ds(pl.multiple_of(h * head, head), head)
            grads = []
            for first in range(0, tokens, block):
                rows = pl.ds(first, block)
                keys = pl.ds(0, first + block)
                query = v["query"][rows, lanes]
                scores = dot_nt(query, v["key"][keys, :])
                probs = jnp.exp(scores * scale + bias[rows, keys] - v["log_total"][h, rows, :])
                back = d_mixed[rows, lanes]
                d_probs = dot_nt(back, v["value"][keys, :])
                inner_sum = jnp.sum(probs * d_probs, axis=-1, keepdims=True)
                d_scores = (probs * (d_probs - inner_sum)).astype(BF)
                dv[keys, :] = dv[keys, :] + dot_tn(probs.astype(BF), back)
                dk[keys, :] = dk[keys, :] + dot_tn(d_scores, query)
                grads.append(dot(d_scores, v["key"][keys, :]))
            grad = jnp.concatenate(grads, axis=0) * scale
            grad = unnorm(unturn(grad), v["query_lin"][:, lanes], v["query_gain"][...], 0)
            lines_ref[:, lanes] = grad.astype(BF)
            plan.run_step(grid, order, h, begin, HEAD_US, heads, True)

        grad = unnorm(unturn(dk[...] * scale), v["key_lin"][...], v["key_gain"][...], 1)
        lines_ref[:, inner : inner + head] = grad.astype(BF)
        lines_ref[:, inner + head : inner + 2 * head] = dv[...].astype(BF)

        @pl.loop(0, columns // tile)
        def _(t):
            rows = pl.ds(pl.multiple_of(t * tile, tile), tile)
            value = dot_nt(lines_ref[:, :inner], v["query_weight"][rows, :])
            value = value + dot_nt(lines_ref[:, inner : inner + head], v["key_weight"][rows, :])
            value = value + dot_nt(lines_ref[:, inner + head :], v["value_weight"][rows, :])
            side_parts[:, rows] = value.astype(BF)

        def put_norm(at, total):
            d_norm_ref[at, :] = total

        side_plan = Plan(side[1])
        for p in range(2):
            plan_scatter(side_plan, side_job, p, put_norm)
        side_order = side_plan.order()

        def side_begin(z):
            for _, act in side_order[z][:-2]:
                act()

        def side_end(z):
            for _, act in side_order[z][-2:]:
                act()

        at_each_line(side, side_begin)
        middle = begin + heads * HEAD_US
        tiles = columns // tile

        @pl.loop(0, tiles)
        def _(t):
            rows = pl.ds(pl.multiple_of(t * tile, tile), tile)
            value = dot_tn(v["normed"][:, rows], lines_ref[...])
            grad_refs[0][rows, :] = value[:, :share].astype(BF)
            grad_refs[1][rows, :] = value[:, share:].astype(BF)
            plan.run_step(grid, order, t, middle, TILE_US, tiles)

        at_each_line(side, side_end)
        plan.run(grid, order, middle + tiles * TILE_US, middle + tiles * TILE_US + 6.0)

        norm_gain_ref[...] = jnp.zeros_like(norm_gain_ref)

        @pl.loop(0, d_own.shape[0] // 16)
        def _(i):
            rows = pl.ds(pl.multiple_of(i * 16, 16), 16)
            value = v["input_own"][rows, :].astype(F32)
            grad = d_norm_ref[rows, :]
            inverse = lax.rsqrt(jnp.mean(value * value, axis=-1, keepdims=True) + EPS)
            norm_gain_ref[0:1, :] = norm_gain_ref[0:1, :] + jnp.sum(
                grad * value * inverse, axis=0, keepdims=True
            )
            back = rms_backward(value, inverse, v["norm_gain"][...], grad)
            input_grad_ref[rows, :] = (v["d_residual"][rows, :] + back).astype(BF)

        plan.run(grid, order, middle + tiles * TILE_US + 6.0, 1e9)

        def end(z):
            for job in jobs:
                job.finish(z)

        at_each_line(grid, end)
        at_each_line(side, side_job.finish)

    dma = pltpu.SemaphoreType.DMA
    values = [arrays[name] for name in names]
    out = pl.pallas_call(
        kernel,
        out_shape=[
            jax.ShapeDtypeStruct((columns, share), BF),
            jax.ShapeDtypeStruct((columns, inner + 2 * head - share), BF),
            jax.ShapeDtypeStruct(d_own.shape, BF),
            jax.ShapeDtypeStruct((8, columns), F32),
            jax.ShapeDtypeStruct((8, head), F32),
            jax.ShapeDtypeStruct((inner, split[0]), BF),
            jax.ShapeDtypeStruct((inner, split[1]), BF),
        ],
        in_specs=[hbm()] * (len(names) + 1),
        out_specs=[vmem()] * 5 + [hbm()] * 2,
        scratch_shapes=[pltpu.VMEM(a.shape, a.dtype) for a in values]
        + [
            pltpu.VMEM((tokens, columns), BF),
            pltpu.VMEM((tokens, inner), BF),
            pltpu.VMEM((tokens, tokens), F32),
            pltpu.VMEM((tokens, head), F32),
            pltpu.VMEM((tokens, head), F32),
            pltpu.VMEM((tokens, inner + 2 * head), BF),
            pltpu.VMEM(d_own.shape, F32),
            pltpu.VMEM((inner, split[0]), BF),
            pltpu.VMEM((inner, split[1]), BF),
        ]
        + Reduce.scratch(grid, inner, split[0], BF, *kinds[0])
        + Reduce.scratch(grid, inner, split[1], BF, *kinds[1])
        + [pltpu.VMEM((tokens, columns), BF)]
        + Scatter.buffers(side, d_own.shape[0], columns, BF)
        + [dma((len(names),)), dma((1,))]
        + Gather.sems(side, 2)
        + Scatter.sems(side, 2),
        compiler_params=params(number),
        name="attention_backward",
    )(*values, d_own)
    first, second, input_grad, norm_gain, gains, *out_sums = out
    out_sum = jnp.concatenate(out_sums, axis=1)
    return (first, second), input_grad, norm_gain[0], gains[0], gains[1], out_sum


def rope_tables(positions, head_size):
    half_size = head_size // 2
    frequency = THETA ** (-2.0 * jnp.arange(half_size, dtype=F32) / head_size)
    angles = positions.astype(F32)[:, None] * frequency[None, :]
    return (jnp.cos(angles), jnp.sin(angles))


def doc_positions(doc_ids):
    row_index = jnp.arange(doc_ids.shape[0], dtype=jnp.int32)
    doc_starts = jnp.concatenate([jnp.ones((1,), jnp.bool_), doc_ids[1:] != doc_ids[:-1]])
    first_row = lax.cummax(jnp.where(doc_starts, row_index, 0), axis=0)
    return row_index - first_row


def from_near(rows, count):
    return lax.ppermute(rows, "shard", [(s, s + 1 - 2 * (s % 2)) for s in range(count)])


def from_far(rows, count):
    return lax.ppermute(rows, "shard", [(s, (s + 2) % count) for s in range(count)])


def local(
    layer_input,
    doc_ids,
    routes,
    norm1_gain,
    query_weight,
    key_matrix,
    value_matrix,
    query_norm_gain,
    key_norm_gain,
    out_weight,
    norm2_gain,
    router_weight,
    gate_weight,
    up_weight,
    down_weight,
    cotangent,
):
    tokens_here, model_width = layer_input.shape
    head_size = query_norm_gain.shape[0]
    heads_here = query_weight.shape[1] // head_size
    experts_all = router_weight.shape[1]
    local_experts, _, hidden_here = gate_weight.shape
    expert_peers = lax.axis_size("expert")
    shard_count = lax.axis_size("shard")
    rows_here = tokens_here // shard_count
    shard_index = lax.axis_index("shard")
    expert_index = lax.axis_index("expert")
    hidden_all = shard_count * local_experts * hidden_here

    def own(rows):
        return lax.dynamic_slice_in_dim(rows, shard_index * rows_here, rows_here, axis=0)

    def gather_weight(weight):
        return lax.all_gather(weight, "shard", axis=0).reshape(hidden_all, model_width)

    fused = expert_peers * rows_here <= VMEM_ROWS
    cot_own = own(cotangent)
    cot_all = lax.all_gather(cot_own, "expert", axis=0, tiled=True)
    routes_own = own(routes)
    experts = jnp.arange(experts_all, dtype=jnp.int32)
    chosen_own = jnp.any(routes_own[:, :, None] == experts[None, None, :], axis=1)
    gate_weight = jnp.swapaxes(gate_weight, 1, 2)
    up_weight = jnp.swapaxes(up_weight, 1, 2)
    if fused:
        gate_far = from_far(gate_weight, shard_count)
        gate_near = from_near(gate_weight, shard_count)
        first_far = from_far(up_weight[:1], shard_count)
        first_near = from_near(up_weight[:1], shard_count)
    else:
        down_all = gather_weight(down_weight)
        gate_all = gather_weight(gate_weight)
        up_all = gather_weight(up_weight)

    positions = doc_positions(doc_ids)
    cosine_table, sine_values = rope_tables(positions, head_size)
    inner = heads_here * head_size
    shared = dict(
        cosine=jnp.concatenate([cosine_table, cosine_table], axis=1),
        sine=jnp.concatenate([-sine_values, sine_values], axis=1),
        query_gain=query_norm_gain[None, :],
        key_gain=key_norm_gain[None, :],
        doc_col=doc_ids[:, None],
        doc_row=doc_ids[None, :],
        query_weight=query_weight,
        key_weight=key_matrix,
        value_weight=value_matrix,
        norm_gain=norm1_gain[None, :],
    )
    forward = dict(
        rows=layer_input, norm_two_gain=norm2_gain[None, :], **shared, out_weight=out_weight
    )
    normed_one, query_lin, key_lin, query, key, value, mixed, log_total, *rest = (
        attention_forward(forward, heads_here, 1)
    )
    residual, normed_two = rest
    if fused:
        gate_far, first_far, residual, normed_two = lax.optimization_barrier(
            (gate_far, first_far, residual, normed_two)
        )

    if fused:
        up_late, down_late, normed_two = lax.optimization_barrier(
            (up_weight[1:], down_weight, normed_two)
        )
        up_far, down_far = from_far(up_late, shard_count), from_far(down_late, shard_count)
        up_near, down_near = from_near(up_late, shard_count), from_near(down_late, shard_count)
    _, inverse_two = rms_forward(residual, norm2_gain)
    chosen_wide = jnp.pad(chosen_own.astype(BF), ((0, 0), (0, EXTRA - experts_all)))
    normed_all, chosen_all = gather_rows([normed_two, chosen_wide], [], 2, (2, 1))
    if fused:
        up_far, down_far, normed_all = lax.optimization_barrier((up_far, down_far, normed_all))
        rel = []
        for own_one, near, far in (
            (gate_weight, gate_near, gate_far),
            (up_weight[:1], first_near, first_far),
            (up_late, up_near, up_far),
            (down_late, down_near, down_far),
        ):
            rel.append([own_one, near, far, from_near(far, shard_count)])

    def gate_table(rows, chosen):
        logits = jnp.where(chosen, dot(rows, router_weight), -jnp.inf)
        top = jnp.max(logits, axis=-1, keepdims=True)
        powers = jnp.exp(logits - top)
        return powers / jnp.sum(powers, axis=-1, keepdims=True)

    if fused:
        router_wide = jnp.pad(router_weight, ((0, 0), (0, EXTRA - experts_all)))
        summed, out_part, gate_part, up_part, down_part = expert_rows(
            normed_all, cot_all, chosen_all, router_wide, *rel, 3
        )
        d_rows_own = summed[:, :model_width]
        d_gates_own = (
            summed[:, model_width : model_width + experts_all]
            + summed[:, model_width + experts_all : model_width + 2 * experts_all]
        )
    else:
        gates_here = lax.dynamic_slice_in_dim(
            gate_table(normed_all, chosen_all[:, :experts_all] > 0.5),
            expert_index * local_experts,
            local_experts,
            axis=1,
        )
        column_expert = (jnp.arange(hidden_all, dtype=jnp.int32) // hidden_here) % local_experts
        gate_columns = jnp.zeros((1, 1), F32)
        for j in range(local_experts):
            gate_columns = jnp.where(column_expert[None, :] == j, gates_here[:, j : j + 1], gate_columns)

        d_act_raw = dot_nt(cot_all, down_all)
        gate_pre = dot_nt(normed_all, gate_all)
        up_pre = dot_nt(normed_all, up_all)
        sig = jax.nn.sigmoid(gate_pre)
        silu = gate_pre * sig
        act = silu * up_pre
        act_gated = (act * gate_columns).astype(BF)
        d_act = d_act_raw * gate_columns
        d_gate_low = (d_act * up_pre * sig * (1.0 + gate_pre * (1.0 - sig))).astype(BF)
        d_up_low = (d_act * silu).astype(BF)
        act_back = act * d_act_raw
        d_gates_here = jnp.stack(
            [
                jnp.sum(jnp.where(column_expert[None, :] == j, act_back, 0.0), axis=1)
                for j in range(local_experts)
            ],
            axis=-1,
        )
        d_rows = dot(d_gate_low, gate_all) + dot(d_up_low, up_all)
        d_rows_own = scatter_rows(d_rows.astype(BF), "expert", 3, 2)
        out_part = dot(act_gated, down_all).astype(BF)

        def split(grad):
            return grad.astype(BF).reshape(shard_count, local_experts, hidden_here, model_width)

        gate_part = split(dot_tn(d_gate_low, normed_all))
        up_part = split(dot_tn(d_up_low, normed_all))
        down_part = split(dot_tn(act_gated, cot_all))

        d_gates_own = lax.all_to_all(
            d_gates_here.reshape(expert_peers, rows_here, local_experts),
            "expert",
            split_axis=0,
            concat_axis=0,
            tiled=True,
        )
        d_gates_own = jnp.swapaxes(d_gates_own, 0, 1).reshape(rows_here, experts_all)
    out_own = lax.psum_scatter(out_part, "expert", scatter_dimension=0, tiled=True)
    def scatter_grad(grad):
        return lax.psum_scatter(grad, "shard", scatter_dimension=0, tiled=False)

    gate_grad = jnp.swapaxes(scatter_grad(gate_part).astype(F32), 1, 2)
    up_grad = jnp.swapaxes(scatter_grad(up_part).astype(F32), 1, 2)

    gates_own = gate_table(normed_two, chosen_own)
    d_logits = gates_own * (
        d_gates_own - jnp.sum(gates_own * d_gates_own, axis=-1, keepdims=True)
    )
    d_logits_low = d_logits.astype(BF)
    router_grad = dot_tn(normed_two, d_logits_low)
    d_normed_two = d_rows_own + dot_nt(d_logits_low, router_weight)
    norm2_grad = jnp.sum(d_normed_two * residual * inverse_two, axis=0)
    d_residual = cot_own.astype(F32) + rms_backward(
        residual, inverse_two, norm2_gain, d_normed_two
    )
    backward = dict(
        mixed=mixed,
        query=query,
        key=key,
        value=value,
        query_lin=query_lin,
        key_lin=key_lin,
        log_total=log_total,
        out_weight=out_weight,
        normed=normed_one,
        input_own=own(layer_input),
        d_residual=d_residual,
        **shared,
    )
    line_grads, input_grad_own, norm1_grad, d_query_gain, d_key_gain, out_sum = (
        attention_backward(backward, d_residual.astype(BF), heads_here, 4)
    )
    share = share_of(inner + 2 * head_size)
    out_own, _ = lax.optimization_barrier((out_own, norm1_grad))
    layer_out_own = (residual + out_own).astype(BF)

    flat = jnp.concatenate(
        [router_grad.T.reshape(-1), norm2_grad, norm1_grad, d_query_gain, d_key_gain]
    )
    small_rows = 8 * expert_peers
    small_columns = -(-flat.shape[0] // (128 * small_rows)) * 128
    small = jnp.pad(flat, (0, small_rows * small_columns - flat.shape[0]))
    (line_first, line_second, small), (input_grad, layer_out), down_sum = sum_and_gather(
        *line_grads,
        small.reshape(small_rows, small_columns),
        (input_grad_own, layer_out_own),
        down_part.reshape(hidden_all, model_width),
        5,
    )
    down_grad = down_sum.reshape(local_experts, hidden_here, model_width)
    query_cols = inner - share
    query_sum = jnp.concatenate([line_first, line_second[:, :query_cols]], axis=1)
    key_sum = line_second[:, query_cols : query_cols + head_size]
    value_sum = line_second[:, query_cols + head_size :]
    small = small.reshape(-1)
    bounds = [experts_all * model_width, model_width, model_width, head_size, head_size]
    taken = []
    at = 0
    for bound in bounds:
        taken.append(small[at : at + bound])
        at += bound
    router_sum, norm2_sum, norm1_sum, query_gain_sum, key_gain_sum = taken
    router_sum = router_sum.reshape(experts_all, model_width).T
    return (
        layer_out,
        input_grad,
        norm1_sum,
        query_sum.astype(F32),
        key_sum.astype(F32),
        value_sum.astype(F32),
        query_gain_sum,
        key_gain_sum,
        out_sum.astype(F32),
        norm2_sum,
        router_sum,
        gate_grad,
        up_grad,
        down_grad,
    )


def solution(mesh):
    return jax.shard_map(
        local,
        mesh=mesh,
        in_specs=(
            P("expert", None),
            P("expert"),
            P("expert", None),
            P(),
            P(None, "shard"),
            P(None, "shard"),
            P(None, "shard"),
            P(),
            P(),
            P("shard", None),
            P(),
            P(),
            P("expert", None, "shard"),
            P("expert", None, "shard"),
            P("expert", "shard", None),
            P("expert", None),
        ),
        out_specs=(
            P("expert", None),
            P("expert", None),
            P(),
            P(None, "shard"),
            P(None, "shard"),
            P(None, "shard"),
            P(),
            P(),
            P("shard", None),
            P(),
            P(),
            P("expert", None, "shard"),
            P("expert", None, "shard"),
            P("expert", "shard", None),
        ),
        check_vma=False,
    )
```
